32 devices in a mesh: section: 2 (over x), dp: 4 (over z), tensor: 4 (over y, core).
Axes of the slice: x: 2, y: 2, z: 4, core: 2. Of those that a mesh axis runs over, the one named last changes fastest.
Arguments:
- tokens: bfloat16 [2, 4, 1024, 1024], P(None, 'dp'), may hold values from -6 to 6
- cotangent: bfloat16 [2, 4, 1024, 1024], P(None, 'dp'), may hold values from -6 to 6
- lengths: int32 [2, 4], P(None, 'dp'), may hold values from 128 to 1024, as said below
- attn_gain: float32 [2, 1024], P('section'), may hold values from 0.25 to 1.75
- attn_bias: float32 [2, 1024], P('section'), may hold values from -1.75 to 1.75
- ffn_gain: float32 [2, 1024], P('section'), may hold values from 0.25 to 1.75
- ffn_bias: float32 [2, 1024], P('section'), may hold values from -1.75 to 1.75
- w_query: bfloat16 [2, 1024, 1024], P('section', None, 'tensor'), may hold values from -0.1875 to 0.1875
- w_key: bfloat16 [2, 1024, 1024], P('section', None, 'tensor'), may hold values from -0.1875 to 0.1875
- w_value: bfloat16 [2, 1024, 1024], P('section', None, 'tensor'), may hold values from -0.1875 to 0.1875
- w_out: bfloat16 [2, 1024, 1024], P('section', 'tensor'), may hold values from -1.5 to 1.5
- feat_scale: float32 [2, 16, 64], P('section', 'tensor'), may hold values from 0.25 to 4
- w_up: bfloat16 [2, 1024, 4096], P('section', None, 'tensor'), may hold values from -0.1875 to 0.1875
- w_down: bfloat16 [2, 4096, 1024], P('section', 'tensor'), may hold values from -0.09375 to 0.09375
- down_bias: float32 [2, 1024], P('section'), may hold values from -1.75 to 1.75
Outputs:
- ends: float32 [2, 2, 4, 1024, 1024], P('section', None, 'dp', 'tensor')
- grad_attn_gain: float32 [2, 1024], P('section', 'dp')
- grad_attn_bias: float32 [2, 1024], P('section', 'dp')
- grad_ffn_gain: float32 [2, 1024], P('section', 'dp')
- grad_ffn_bias: float32 [2, 1024], P('section', 'dp')
- grad_w_query: float32 [2, 1024, 1024], P('section', 'dp', 'tensor')
- grad_w_key: float32 [2, 1024, 1024], P('section', 'dp', 'tensor')
- grad_w_value: float32 [2, 1024, 1024], P('section', 'dp', 'tensor')
- grad_w_out: float32 [2, 1024, 1024], P('section', 'tensor', 'dp')
- grad_feat_scale: float32 [2, 16, 64], P('section', 'tensor', 'dp')
- grad_w_up: float32 [2, 1024, 4096], P('section', 'dp', 'tensor')
- grad_w_down: float32 [2, 4096, 1024], P('section', 'tensor', 'dp')
- grad_down_bias: float32 [2, 1024], P('section', 'dp')
The draws below stay inside these ranges and needn't reach their ends.
Inputs may be any that keep to these rules, and one draw needn't show every extreme that they name: `lengths`: in every draw some sequence fills all 1024 slots.
All inputs are finite; a program needn't handle non-finite values.
Results may differ from the reference program's by a relative error of at most 0.015.
Values may be sent and summed in bfloat16 or wider, within the bound.
No kernel may reach another device: no remote copies, remote signals or barrier semaphores. Data moves between devices by JAX's collectives and lax.ppermute only.
A program may use at most 320 MiB of HBM per device.

```python
import math
import jax
import jax.numpy as jnp
from jax import lax

D = 1024
H = 16
HD = 64
FF = 4096
ROT = 16
SPAN = 64
ROWS = 1024
MIN_LEN = 128
MB = 2
SEQS = 4


def draw_lengths(key, part):
    key = jax.random.fold_in(key, 7)
    first_key, second_key = jax.random.split(key)
    counts = jax.random.randint(first_key, (MB * SEQS,), MIN_LEN, ROWS + 1)
    chosen = jax.random.randint(second_key, (), 0, MB * SEQS)
    counts = jnp.where(jnp.arange(MB * SEQS) == chosen, ROWS, counts)
    return counts.reshape(MB, SEQS).astype(jnp.int32)


def raised(array, stream_key, source, target, shards_of, factor):
    owner, partner = [(jnp.arange(array.shape[axis_at]) // (array.shape[axis_at] // shards_of)).reshape([-1 if axis == axis_at else 1 for axis in range(array.ndim)]) for axis_at in (source, target)]
    chosen = jax.random.permutation(stream_key, shards_of)[partner]
    strong = (owner == chosen) | (owner == (partner + shards_of // 2) % shards_of)
    return jnp.where(strong, factor * array, array)


def level_of(own_key, dims, cuts, least, largest):
    def one(dim, blocks):
        draws = jax.random.uniform(jax.random.fold_in(jax.random.fold_in(own_key, 6), dim), (blocks,), jnp.float32, least / len(cuts), largest / len(cuts))
        return jnp.repeat(jnp.exp(draws), dims[dim] // blocks).reshape((-1,) + (1,) * (len(dims) - dim - 1))

    factor_of = one(*cuts[0])
    for cut in cuts[1:]:
        factor_of = factor_of * one(*cut)
    return factor_of


def gaussian(rng, extent, deviation, reach, cuts=(), kind=jnp.bfloat16):
    values = deviation * jax.random.normal(rng, extent, jnp.float32)
    if cuts:
        values = values * level_of(rng, extent, cuts, -0.22, 0.18)
    return jnp.clip(values, -reach, reach).astype(kind)


def noise_with(key, extent, scale, limit, pieces, heavy, kind=jnp.bfloat16):
    array = scale * jax.random.normal(key, extent, jnp.float32)
    if pieces:
        array = array * level_of(key, extent, pieces, -0.22, 0.18)
    return jnp.clip(raised(array, jax.random.fold_in(key, 3), *heavy), -limit, limit).astype(kind)


def setup_inputs(seed: int = 0) -> dict:
    keys = jax.random.split(jax.random.key(seed), 16)
    return {
        "tokens": noise_with(keys[0], (MB, SEQS, ROWS, D), 1.0, 6.0, ((1, 4),), (1, 3, 4, 2.0)),
        "cotangent": noise_with(keys[1], (MB, SEQS, ROWS, D), 1.0, 6.0, ((1, 4),), (1, 3, 4, 2.0)),
        "lengths": draw_lengths(jax.random.fold_in(keys[15], 71), 0),
        "attn_gain": jnp.clip(1.0 + 0.15 * jax.random.normal(keys[3], (2, D), jnp.float32), 0.25, 1.75),
        "attn_bias": gaussian(keys[4], (2, D), 0.3, 1.75, ((0, 2),), jnp.float32),
        "ffn_gain": jnp.clip(1.0 + 0.15 * jax.random.normal(keys[5], (2, D), jnp.float32), 0.25, 1.75),
        "ffn_bias": gaussian(keys[6], (2, D), 0.3, 1.75, ((0, 2),), jnp.float32),
        "w_query": gaussian(keys[7], (2, D, H * HD), D ** -0.5, 0.1875, ((0, 2), (2, 4))),
        "w_key": gaussian(keys[8], (2, D, H * HD), D ** -0.5, 0.1875, ((0, 2), (2, 4))),
        "w_value": gaussian(keys[9], (2, D, H * HD), D ** -0.5, 0.1875, ((0, 2), (2, 4))),
        "w_out": gaussian(keys[10], (2, H * HD, D), (H * HD // 64) ** -0.5, 1.5, ((0, 2), (1, 4))),
        "feat_scale": jnp.clip(jnp.exp(math.log(4.0) - 2.7725887 * jax.random.uniform(keys[11], (2, H, HD), jnp.float32) ** level_of(keys[11], (2, H, HD), ((0, 2), (1, 4)), -0.2, 0.2)), 0.25, 4.0),
        "w_up": gaussian(keys[12], (2, D, FF), D ** -0.5, 0.1875, ((0, 2), (2, 4))),
        "w_down": gaussian(keys[13], (2, FF, D), FF ** -0.5, 0.09375, ((0, 2), (1, 4))),
        "down_bias": gaussian(keys[14], (2, D), 0.3, 1.75, ((0, 2),), jnp.float32),
    }


EPSILON = 1e-05
HIGHEST = lax.Precision.HIGHEST

@jax.custom_vjp
def low(v):
    return lax.optimization_barrier(v.astype(jnp.bfloat16)).astype(jnp.float32)

@jax.custom_vjp
def low_back(v):
    return v

def low_keep(v):
    return (low(v), None)

def low_pass(kept, grad):
    return (grad,)

def back_keep(v):
    return (v, None)

def back_low(kept, grad):
    return (low(grad),)
low.defvjp(low_keep, low_pass)
low_back.defvjp(back_keep, back_low)

def layer_norm(hidden, gain, shift):
    center = hidden - lax.optimization_barrier(jnp.mean(hidden, axis=-1, keepdims=True))
    spread = lax.optimization_barrier(jnp.mean(center * center, axis=-1, keepdims=True))
    return center * lax.rsqrt(spread + EPSILON) * gain + shift

def rotary_tables(slot_rows, rotary_dims):
    position = jnp.arange(slot_rows).astype(jnp.float32)
    inverse = jnp.exp(jnp.arange(rotary_dims // 2).astype(jnp.float32) * (-2.0 * math.log(10000.0) / rotary_dims))
    angles = position[:, None] * inverse[None, :]
    return (jnp.cos(angles), jnp.sin(angles))

def dct_table(order):
    index = jnp.arange(order).astype(jnp.float32)
    table = jnp.cos(math.pi * (index[None, :] + 0.5) * index[:, None] / order) * math.sqrt(2.0 / order)
    return jnp.where(index[:, None] == 0.0, table * math.sqrt(0.5), table)

def rotate(values, cosines, sines):
    halfway = cosines.shape[1]
    lower_part = values[..., :halfway]
    upper_part = values[..., halfway:2 * halfway]
    cos_rows = cosines[:, None, :]
    sin_rows = sines[:, None, :]
    return jnp.concatenate([lower_part * cos_rows - upper_part * sin_rows, upper_part * cos_rows + lower_part * sin_rows, values[..., 2 * halfway:]], axis=-1)

def feat_map(queries, key_rows, scales, keep, cosines, sines, table):

    def lift(values):
        coeffs = jnp.einsum('brhd,fd->brhf', rotate(values, cosines, sines), table, precision=HIGHEST)
        return scales * jnp.exp(coeffs)
    return (lift(queries), lift(key_rows) * keep[:, :, None, None])

def linear_attend(query_feats, key_feats, value_rows, block):
    batch_count, slot_rows, head_count, feat_count = query_feats.shape
    value_width = value_rows.shape[3]
    blocks = slot_rows // block
    query_blocks = query_feats.reshape(batch_count, blocks, block, head_count, feat_count)
    key_blocks = key_feats.reshape(batch_count, blocks, block, head_count, feat_count)
    value_blocks = value_rows.reshape(batch_count, blocks, block, head_count, value_width)
    causal = (jnp.arange(block)[:, None] >= jnp.arange(block)[None, :]).astype(query_feats.dtype)
    scores = jnp.einsum('bnihf,bnjhf->bnhij', query_blocks, key_blocks, precision=HIGHEST) * causal
    inner = jnp.einsum('bnhij,bnjhd->bnihd', scores, value_blocks, precision=HIGHEST)
    inner_total = jnp.transpose(lax.optimization_barrier(jnp.sum(scores, axis=-1)), (0, 1, 3, 2))
    states = jnp.einsum('bnjhf,bnjhd->bnhfd', key_blocks, value_blocks, precision=HIGHEST)
    state_totals = lax.optimization_barrier(jnp.sum(key_blocks, axis=2))
    earlier = jnp.cumsum(states, axis=1) - states
    earlier_totals = jnp.cumsum(state_totals, axis=1) - state_totals
    outer = jnp.einsum('bnihf,bnhfd->bnihd', query_blocks, earlier, precision=HIGHEST)
    outer_total = jnp.einsum('bnihf,bnhf->bnih', query_blocks, earlier_totals, precision=HIGHEST)
    result = (inner + outer) / (inner_total + outer_total)[..., None]
    return result.reshape(batch_count, slot_rows, head_count, value_width)

def project(values, matrix):
    return jnp.einsum('brd,de->bre', values, matrix, precision=HIGHEST)

def one_layer(hidden, params, keep, cosines, sines, table):
    gain_one, shift_one, gain_two, shift_two, w_q, w_k, w_v, w_o, scales, w_in, w_back, bias_back = params
    batch_count, slot_rows, model_width = hidden.shape
    head_count, head_size = scales.shape
    shape_four = (batch_count, slot_rows, head_count, head_size)
    norm_one = low(layer_norm(hidden, gain_one, shift_one))
    queries = low_back(project(norm_one, w_q))
    key_rows = low_back(project(norm_one, w_k))
    value_rows = low(low_back(project(norm_one, w_v)))
    query_feats, key_feats = feat_map(queries.reshape(shape_four), key_rows.reshape(shape_four), scales, keep, cosines, sines, table)
    mixed = linear_attend(low(query_feats), low(key_feats), value_rows.reshape(shape_four), SPAN)
    mixed = low(low_back(mixed.reshape(batch_count, slot_rows, head_count * head_size)))
    attended = project(mixed, w_o)
    norm_two = low(layer_norm(hidden, gain_two, shift_two))
    up_rows = low_back(project(norm_two, w_in))
    act_rows = low(jax.nn.gelu(up_rows, approximate=False))
    forward_rows = project(act_rows, w_back)
    return hidden + low_back(attended + forward_rows) + bias_back

def reference(tokens, cotangent, lengths, attn_gain, attn_bias, ffn_gain, ffn_bias, w_query, w_key, w_value, w_out, feat_scale, w_up, w_down, down_bias):
    weights = (attn_gain, attn_bias, ffn_gain, ffn_bias, w_query, w_key, w_value, w_out, feat_scale, w_up, w_down, down_bias)
    weights = tuple((item.astype(jnp.float32) for item in weights))
    seq_total = MB * SEQS
    group = math.gcd(seq_total, max(1, 4096 // ROWS))
    inputs = tokens.astype(jnp.float32).reshape(seq_total // group, group, ROWS, D)
    grads_in = cotangent.astype(jnp.float32).reshape(seq_total // group, group, ROWS, D)
    lens = lengths.reshape(seq_total // group, group)
    cosines, sines = rotary_tables(ROWS, ROT)
    table = dct_table(HD)

    def both_layers(start, params, keep):
        first_out = one_layer(start, tuple((item[0] for item in params)), keep, cosines, sines, table)
        middle = low(low_back(first_out))
        return one_layer(middle, tuple((item[1] for item in params)), keep, cosines, sines, table)

    def step(carry, blocks):
        block_in, block_grad, block_lens = blocks
        keep = (jnp.arange(ROWS).astype(jnp.int32)[None, :] < block_lens[:, None]).astype(jnp.float32)
        result, pull = jax.vjp(lambda start, params: both_layers(start, params, keep), block_in, weights)
        grad_start, grad_params = pull(block_grad)
        carry = jax.tree.map(jnp.add, carry, grad_params)
        return (carry, (grad_start, result))
    init = tuple((jnp.zeros_like(item) for item in weights))
    grads, (grad_inputs, results) = lax.scan(step, init, (inputs, grads_in, lens))
    ends = jnp.stack([grad_inputs.reshape(MB, SEQS, ROWS, D), results.reshape(MB, SEQS, ROWS, D)])
    return (ends, grads[0], grads[1], grads[2], grads[3], grads[4], grads[5], grads[6], grads[7], grads[8], grads[9], grads[10], grads[11])
```

```python
import math

import jax
import jax.numpy as jnp
import numpy as np
from jax import lax
from jax.sharding import PartitionSpec as P

ROT = 16
SPAN = 64


EPSILON = 1e-05
HIGHEST = lax.Precision.HIGHEST


def from_behind(x, axis, by):
    size = lax.axis_size(axis)
    pairs = [(i, i + by) for i in range(size) if 0 <= i + by < size]
    return lax.ppermute(x, axis, pairs)


def layer_norm(hidden, gain, shift):
    center = hidden - jnp.mean(hidden, axis=-1, keepdims=True)
    spread = jnp.mean(center * center, axis=-1, keepdims=True)
    return center * lax.rsqrt(spread + EPSILON) * gain + shift


def flat_tables(slot_rows, rotary_dims, head_count, head_size):
    width = head_count * head_size
    halfway = rotary_dims // 2
    position = jnp.arange(slot_rows).astype(jnp.float32)
    column = jnp.arange(width) % head_size
    pair = jnp.where(column < halfway, column, column - halfway)
    inverse = jnp.exp(pair.astype(jnp.float32) * (-2.0 * math.log(10000.0) / rotary_dims))
    angles = position[:, None] * inverse[None, :]
    turned = column < 2 * halfway
    cos_full = jnp.where(turned[None, :], jnp.cos(angles), 1.0)
    sin_full = jnp.where(turned[None, :], jnp.sin(angles), 0.0)
    source = jnp.arange(width)[:, None]
    target = jnp.arange(width)[None, :]
    target_col = target % head_size
    minus_part = (target_col < halfway) & (source == target + halfway)
    plus_part = (target_col >= halfway) & (target_col < 2 * halfway) & (source == target - halfway)
    partner = jnp.where(minus_part, -1.0, 0.0) + jnp.where(plus_part, 1.0, 0.0)
    order = np.arange(head_size)
    table = np.cos(np.pi * (order[None, :] + 0.5) * order[:, None] / head_size) * np.sqrt(2.0 / head_size)
    table = np.where(order[:, None] == 0, table * np.sqrt(0.5), table)
    same_head = (source // head_size == target // head_size).astype(jnp.float32)
    dct_big = jnp.asarray(np.kron(np.eye(head_count), table.T), jnp.float32)
    head_mask = (jnp.arange(width)[None, :] // head_size == jnp.arange(head_count)[:, None]).astype(
        jnp.float32
    )
    return (cos_full, sin_full, partner, dct_big, head_mask, same_head)


def feat_map(queries, key_rows, scales, keep, tables):
    cos_full, sin_full, partner, dct_big, head_mask, same_head = tables

    def lift(values):
        swapped = jnp.einsum("srd,de->sre", values, partner, precision=HIGHEST)
        turned = values * cos_full + swapped * sin_full
        coeffs = jnp.einsum("srd,de->sre", turned, dct_big, precision=HIGHEST)
        return scales * jnp.exp(coeffs)

    return (lift(queries), lift(key_rows) * keep[:, :, None])


def linear_attend(query_feats, key_feats, value_rows, block, tables):
    cos_full, sin_full, partner, dct_big, head_mask, same_head = tables
    seq_count, slot_rows, width = query_feats.shape
    blocks = slot_rows // block
    query_blocks = query_feats.reshape(seq_count, blocks, block, width)
    key_blocks = key_feats.reshape(seq_count, blocks, block, width)
    value_blocks = value_rows.reshape(seq_count, blocks, block, width)
    causal = (jnp.arange(block)[:, None] >= jnp.arange(block)[None, :]).astype(jnp.float32)
    query_heads = query_blocks[:, :, None, :, :] * head_mask[None, None, :, None, :]
    scores = jnp.einsum("snhid,snjd->snhij", query_heads, key_blocks, precision=HIGHEST) * causal
    inner = jnp.einsum("snhij,snjd->snhid", scores, value_blocks, precision=HIGHEST)
    inner = jnp.sum(inner * head_mask[None, None, :, None, :], axis=2)
    inner_total = jnp.einsum("snhij,hd->snid", scores, head_mask, precision=HIGHEST)
    states = jnp.einsum("snjd,snje->snde", key_blocks, value_blocks, precision=HIGHEST) * same_head
    state_totals = jnp.sum(key_blocks, axis=2)
    earlier = jnp.cumsum(states, axis=1) - states
    earlier_totals = jnp.cumsum(state_totals, axis=1) - state_totals
    outer = jnp.einsum("snid,snde->snie", query_blocks, earlier, precision=HIGHEST)
    outer_total = jnp.einsum(
        "snid,de->snie", query_blocks * earlier_totals[:, :, None, :], same_head, precision=HIGHEST
    )
    result = (inner + outer) / (inner_total + outer_total)
    return result.reshape(seq_count, slot_rows, width)


def body(
    tokens,
    cotangent,
    lengths,
    attn_gain,
    attn_bias,
    ffn_gain,
    ffn_bias,
    w_query,
    w_key,
    w_value,
    w_out,
    feat_scale,
    w_up,
    w_down,
    down_bias,
):
    section_pos = lax.axis_index("section")
    is_first = section_pos == 0
    tensor_pos = lax.axis_index("tensor")
    tensor_count = lax.axis_size("tensor")
    micro_count, seq_count, slot_rows, model_width = tokens.shape
    part_rows = slot_rows // tensor_count
    gain_one = attn_gain[0]
    shift_one = attn_bias[0]
    gain_two = ffn_gain[0]
    shift_two = ffn_bias[0]
    mat_query = w_query[0]
    mat_key = w_key[0]
    mat_value = w_value[0]
    mat_out = w_out[0]
    head_count, head_size = (feat_scale.shape[1], feat_scale.shape[2])
    scales = feat_scale[0].reshape(-1)
    mat_up = w_up[0]
    mat_down = w_down[0]
    bias_back = down_bias[0]
    inner_width = head_count * head_size
    shape_flat = (seq_count, slot_rows, inner_width)
    tables = flat_tables(slot_rows, ROT, head_count, head_size)
    keep_all = (jnp.arange(slot_rows)[None, None, :] < lengths[:, :, None]).astype(jnp.float32)
    slot_count = micro_count + 1

    def own_rows(full_rows):
        return lax.dynamic_slice_in_dim(full_rows, tensor_pos * part_rows, part_rows, 1)

    def attend(query_feats, key_feats, value_rows):
        return linear_attend(query_feats, key_feats, value_rows, SPAN, tables)

    def backward(grad_out, saved, keep):
        (
            stored,
            norm_one,
            norm_two,
            queries,
            key_rows,
            query_low,
            key_low,
            value_rows,
            mixed_low,
            up_rows,
        ) = saved
        grad_low = lax.all_gather(grad_out.astype(jnp.bfloat16), "tensor", axis=1, tiled=True)
        grad_flat = grad_low.reshape(-1, model_width)
        grad_act = jnp.einsum("rd,fd->rf", grad_flat, mat_down, preferred_element_type=jnp.float32)
        act_full, gelu_back = jax.vjp(
            lambda inputs: jax.nn.gelu(inputs, approximate=False), up_rows
        )
        grad_up = gelu_back(grad_act)[0].astype(jnp.bfloat16)
        grad_mixed = jnp.einsum(
            "rd,ed->re", grad_flat, mat_out, preferred_element_type=jnp.float32
        ).astype(jnp.bfloat16)
        attend_out, attend_back = jax.vjp(
            attend,
            query_low.astype(jnp.float32),
            key_low.astype(jnp.float32),
            value_rows.reshape(shape_flat).astype(jnp.float32),
        )
        grad_qfeat, grad_kfeat, grad_values = attend_back(
            grad_mixed.reshape(shape_flat).astype(jnp.float32)
        )

        def features(query_in, key_in, scale_in):
            return feat_map(query_in, key_in, scale_in, keep, tables)

        feat_out, feat_back = jax.vjp(
            features, queries.reshape(shape_flat), key_rows.reshape(shape_flat), scales
        )
        grad_queries, grad_keys, grad_scales = feat_back((grad_qfeat, grad_kfeat))
        grad_scales = grad_scales.reshape(head_count, head_size)
        query_grads = grad_queries.reshape(-1, inner_width).astype(jnp.bfloat16)
        key_grads = grad_keys.reshape(-1, inner_width).astype(jnp.bfloat16)
        value_grads = grad_values.reshape(-1, inner_width).astype(jnp.bfloat16)
        grad_norm_one = jnp.einsum(
            "rf,df->rd", query_grads, mat_query, preferred_element_type=jnp.float32
        )
        grad_norm_one = grad_norm_one + jnp.einsum(
            "rf,df->rd", key_grads, mat_key, preferred_element_type=jnp.float32
        )
        grad_norm_one = grad_norm_one + jnp.einsum(
            "rf,df->rd", value_grads, mat_value, preferred_element_type=jnp.float32
        )
        grad_norm_two = jnp.einsum("rf,df->rd", grad_up, mat_up, preferred_element_type=jnp.float32)
        grad_norm_one = grad_norm_one.reshape(seq_count, slot_rows, model_width)
        grad_norm_two = grad_norm_two.reshape(seq_count, slot_rows, model_width)
        grad_norm_one, grad_norm_two = (
            lax.psum_scatter(
                grad_norm_one.astype(jnp.bfloat16), "tensor", scatter_dimension=1, tiled=True
            ).astype(jnp.float32),
            lax.psum_scatter(
                grad_norm_two.astype(jnp.bfloat16), "tensor", scatter_dimension=1, tiled=True
            ).astype(jnp.float32),
        )
        hidden_f = stored.astype(jnp.float32)
        norm_out, norm_back_one = jax.vjp(layer_norm, hidden_f, gain_one, shift_one)
        grad_hid_one, grad_gain_one, grad_shift_one = norm_back_one(grad_norm_one)
        norm_out, norm_back_two = jax.vjp(layer_norm, hidden_f, gain_two, shift_two)
        grad_hid_two, grad_gain_two, grad_shift_two = norm_back_two(grad_norm_two)
        grad_hid = grad_hid_one + grad_hid_two
        grad_hidden = grad_out + grad_hid
        small_grads = (
            grad_gain_one,
            grad_shift_one,
            grad_gain_two,
            grad_shift_two,
            jnp.sum(grad_out, axis=(0, 1)),
            grad_scales,
        )
        weight_data = (
            norm_one,
            norm_two,
            mixed_low,
            act_full.astype(jnp.bfloat16),
            grad_low,
            grad_up,
            query_grads,
            key_grads,
            value_grads,
        )
        return (grad_hidden, small_grads, weight_data)

    received = jnp.zeros((seq_count, part_rows, model_width), jnp.bfloat16)
    saved_list = []
    output_list = []
    for tick in range(slot_count):
        fresh = own_rows(tokens[min(tick, micro_count - 1)])
        hidden = jnp.where(is_first, fresh, received)
        which = jnp.clip(tick - section_pos, 0, micro_count - 1)
        keep = lax.dynamic_index_in_dim(keep_all, which, 0, keepdims=False)
        forward_hidden_f = hidden.astype(jnp.float32)
        forward_norm_one = layer_norm(forward_hidden_f, gain_one, shift_one).astype(jnp.bfloat16)
        forward_norm_two = layer_norm(forward_hidden_f, gain_two, shift_two).astype(jnp.bfloat16)
        forward_norm_one, forward_norm_two = (
            lax.all_gather(forward_norm_one, "tensor", axis=1, tiled=True),
            lax.all_gather(forward_norm_two, "tensor", axis=1, tiled=True),
        )
        forward_flat_one = forward_norm_one.reshape(-1, model_width)
        forward_flat_two = forward_norm_two.reshape(-1, model_width)
        forward_queries = jnp.dot(forward_flat_one, mat_query, preferred_element_type=jnp.float32)
        forward_key_rows = jnp.dot(forward_flat_one, mat_key, preferred_element_type=jnp.float32)
        forward_value_rows = jnp.dot(
            forward_flat_one, mat_value, preferred_element_type=jnp.float32
        ).astype(jnp.bfloat16)
        forward_query_feats, forward_key_feats = feat_map(
            forward_queries.reshape(shape_flat),
            forward_key_rows.reshape(shape_flat),
            scales,
            keep,
            tables,
        )
        forward_query_low = forward_query_feats.astype(jnp.bfloat16)
        forward_key_low = forward_key_feats.astype(jnp.bfloat16)
        mixed = attend(
            forward_query_low.astype(jnp.float32),
            forward_key_low.astype(jnp.float32),
            forward_value_rows.reshape(shape_flat).astype(jnp.float32),
        )
        forward_mixed_low = mixed.reshape(-1, inner_width).astype(jnp.bfloat16)
        forward_up_rows = jnp.dot(forward_flat_two, mat_up, preferred_element_type=jnp.float32)
        forward_act_rows = jax.nn.gelu(forward_up_rows, approximate=False).astype(jnp.bfloat16)
        branch = jnp.dot(forward_mixed_low, mat_out, preferred_element_type=jnp.float32) + jnp.dot(
            forward_act_rows, mat_down, preferred_element_type=jnp.float32
        )
        summed = lax.psum_scatter(
            branch.reshape(seq_count, slot_rows, model_width),
            "tensor",
            scatter_dimension=1,
            tiled=True,
        )
        result = forward_hidden_f + summed + bias_back
        result, saved = (
            result,
            (
                hidden,
                forward_norm_one,
                forward_norm_two,
                forward_queries,
                forward_key_rows,
                forward_query_low,
                forward_key_low,
                forward_value_rows,
                forward_mixed_low,
                forward_up_rows,
            ),
        )
        saved_list.append(saved)
        output_list.append(result)
        if tick < micro_count:
            received = from_behind(result.astype(jnp.bfloat16), "section", 1)
    saved_all = jax.tree.map(lambda *items: jnp.stack(items), *saved_list)
    back_received = jnp.zeros((seq_count, part_rows, model_width), jnp.bfloat16)
    small_total = None
    weight_list = []
    input_grads = []
    for tick in range(slot_count):
        which = tick - 1 + section_pos
        forward_tick = jnp.clip(tick - 1 + 2 * section_pos, 0, micro_count)
        saved = jax.tree.map(
            lambda stacked: lax.dynamic_index_in_dim(stacked, forward_tick, 0, keepdims=False),
            saved_all,
        )
        micro_pos = jnp.clip(which, 0, micro_count - 1)
        keep = lax.dynamic_index_in_dim(keep_all, micro_pos, 0, keepdims=False)
        given = own_rows(lax.dynamic_index_in_dim(cotangent, micro_pos, 0, keepdims=False)).astype(
            jnp.float32
        )
        grad_out = jnp.where(is_first, back_received.astype(jnp.float32), given)
        grad_hidden, small_grads, weight_data = backward(grad_out, saved, keep)
        valid = ((which >= 0) & (which < micro_count)).astype(jnp.float32)
        small_grads = tuple((valid * item for item in small_grads))
        small_total = (
            small_grads
            if small_total is None
            else tuple((left + right for left, right in zip(small_total, small_grads)))
        )
        weight_list.append(weight_data)
        input_grads.append(grad_hidden)
        if tick < micro_count:
            back_received = from_behind(grad_hidden.astype(jnp.bfloat16), "section", -1)
    ends = jnp.where(is_first, jnp.stack(input_grads[1:]), jnp.stack(output_list[1:]))[None]
    grad_gain_one, grad_shift_one, grad_gain_two, grad_shift_two, grad_bias_back = lax.psum(
        (small_total[0], small_total[1], small_total[2], small_total[3], small_total[4]), "tensor"
    )
    grad_scales = small_total[5]
    weight_all = jax.tree.map(lambda *items: jnp.stack(items), *weight_list)
    weight_sel = jax.tree.map(
        lambda stacked: lax.dynamic_slice_in_dim(stacked, 1 - section_pos, micro_count, 0),
        weight_all,
    )

    def weight_terms(
        norm_one,
        norm_two,
        mixed_low,
        act_rows,
        grad_low,
        grad_up,
        query_grads,
        key_grads,
        value_grads,
    ):
        flat_one = norm_one.reshape(-1, model_width)
        flat_two = norm_two.reshape(-1, model_width)
        flat_grad = grad_low.reshape(-1, model_width)
        flat_mixed = mixed_low.reshape(-1, inner_width)
        flat_act = act_rows.reshape(-1, act_rows.shape[-1])
        flat_up = grad_up.reshape(-1, grad_up.shape[-1])
        grad_wq = jnp.einsum(
            "rd,rf->df",
            flat_one,
            query_grads.reshape(-1, inner_width),
            preferred_element_type=jnp.float32,
        )
        grad_wk = jnp.einsum(
            "rd,rf->df",
            flat_one,
            key_grads.reshape(-1, inner_width),
            preferred_element_type=jnp.float32,
        )
        grad_wv = jnp.einsum(
            "rd,rf->df",
            flat_one,
            value_grads.reshape(-1, inner_width),
            preferred_element_type=jnp.float32,
        )
        grad_wo = jnp.einsum("rf,rd->fd", flat_mixed, flat_grad, preferred_element_type=jnp.float32)
        grad_wup = jnp.einsum("rd,rf->df", flat_two, flat_up, preferred_element_type=jnp.float32)
        grad_wdown = jnp.einsum(
            "rf,rd->fd", flat_act, flat_grad, preferred_element_type=jnp.float32
        )
        return (grad_wq, grad_wk, grad_wv, grad_wo, grad_wup, grad_wdown)

    grad_wq, grad_wk, grad_wv, grad_wo, grad_wup, grad_wdown = weight_terms(*weight_sel)
    shared = (
        lax.psum_scatter(
            grad_gain_one.astype(jnp.bfloat16), "dp", scatter_dimension=0, tiled=True
        ).astype(jnp.float32),
        lax.psum_scatter(
            grad_shift_one.astype(jnp.bfloat16), "dp", scatter_dimension=0, tiled=True
        ).astype(jnp.float32),
        lax.psum_scatter(
            grad_gain_two.astype(jnp.bfloat16), "dp", scatter_dimension=0, tiled=True
        ).astype(jnp.float32),
        lax.psum_scatter(
            grad_shift_two.astype(jnp.bfloat16), "dp", scatter_dimension=0, tiled=True
        ).astype(jnp.float32),
        lax.psum_scatter(
            grad_wq.astype(jnp.bfloat16), "dp", scatter_dimension=0, tiled=True
        ).astype(jnp.float32),
        lax.psum_scatter(
            grad_wk.astype(jnp.bfloat16), "dp", scatter_dimension=0, tiled=True
        ).astype(jnp.float32),
        lax.psum_scatter(
            grad_wv.astype(jnp.bfloat16), "dp", scatter_dimension=0, tiled=True
        ).astype(jnp.float32),
        lax.psum_scatter(
            grad_wo.astype(jnp.bfloat16), "dp", scatter_dimension=1, tiled=True
        ).astype(jnp.float32),
        lax.psum_scatter(
            grad_scales.astype(jnp.bfloat16), "dp", scatter_dimension=1, tiled=True
        ).astype(jnp.float32),
        lax.psum_scatter(
            grad_wup.astype(jnp.bfloat16), "dp", scatter_dimension=0, tiled=True
        ).astype(jnp.float32),
        lax.psum_scatter(
            grad_wdown.astype(jnp.bfloat16), "dp", scatter_dimension=1, tiled=True
        ).astype(jnp.float32),
        lax.psum_scatter(
            grad_bias_back.astype(jnp.bfloat16), "dp", scatter_dimension=0, tiled=True
        ).astype(jnp.float32),
    )
    return (
        ends,
        shared[0][None],
        shared[1][None],
        shared[2][None],
        shared[3][None],
        shared[4][None],
        shared[5][None],
        shared[6][None],
        shared[7][None],
        shared[8][None],
        shared[9][None],
        shared[10][None],
        shared[11][None],
    )


def solution(mesh):
    return jax.shard_map(
        body,
        mesh=mesh,
        in_specs=(
            P(None, "dp", None, None),
            P(None, "dp", None, None),
            P(None, "dp"),
            P("section", None),
            P("section", None),
            P("section", None),
            P("section", None),
            P("section", None, "tensor"),
            P("section", None, "tensor"),
            P("section", None, "tensor"),
            P("section", "tensor", None),
            P("section", "tensor", None),
            P("section", None, "tensor"),
            P("section", "tensor", None),
            P("section", None),
        ),
        out_specs=(
            P("section", None, "dp", "tensor", None),
            P("section", "dp"),
            P("section", "dp"),
            P("section", "dp"),
            P("section", "dp"),
            P("section", "dp", "tensor"),
            P("section", "dp", "tensor"),
            P("section", "dp", "tensor"),
            P("section", "tensor", "dp"),
            P("section", "tensor", "dp"),
            P("section", "dp", "tensor"),
            P("section", "tensor", "dp"),
            P("section", "dp"),
        ),
        check_vma=False,
    )
```

```python
import functools
import math

import jax
import jax.numpy as jnp
import numpy as np
from jax import lax
from jax.experimental import pallas as pl
from jax.experimental.pallas import tpu as pltpu
from jax.sharding import PartitionSpec as P

ROT = 16
EPSILON = 1e-05
BLOCK = 256
CHUNK = 128
BF = jnp.bfloat16
F32 = jnp.float32
VMEM_BYTES = 60 * 1024 * 1024
ANY = pl.BlockSpec(memory_space=pl.ANY)
SMEM = pl.BlockSpec(memory_space=pltpu.SMEM)
VMEM = pl.BlockSpec(memory_space=pltpu.VMEM)


def host_tables(slot_rows, head_count, head_size):
    width = head_count * head_size
    halfway = ROT // 2
    column = np.arange(width) % head_size
    pair = np.where(column < halfway, column, column - halfway)
    inverse = np.exp(pair * (-2.0 * math.log(10000.0) / ROT))
    angles = np.arange(slot_rows)[:, None] * inverse[None, :]
    turned = (column < 2 * halfway)[None, :]
    cos_full = np.where(turned, np.cos(angles), 1.0)
    sin_full = np.where(turned, np.sin(angles), 0.0)
    order = np.arange(head_size)
    table = np.cos(np.pi * (order[None, :] + 0.5) * order[:, None] / head_size) * np.sqrt(2.0 / head_size)
    table = np.where(order[:, None] == 0, table * np.sqrt(0.5), table)
    partner = np.zeros((head_size, head_size))
    for i in range(halfway):
        partner[i + halfway, i] = -1.0
        partner[i, i + halfway] = 1.0
    eye = np.eye(head_count)
    dct = np.concatenate([np.kron(eye, table.T), np.kron(eye, partner @ table.T)], axis=0)
    high = dct.astype(np.float32).astype(BF)
    low = (dct - high.astype(np.float64)).astype(np.float32).astype(BF)
    lane_head = np.arange(width) // head_size
    heads = (np.arange(head_count)[:, None] == lane_head[None, :]).astype(np.float32)
    stacked = np.repeat(heads, CHUNK, axis=0)
    same = (lane_head[:, None] == lane_head[None, :]).astype(np.float32)
    return {
        "cos": cos_full.astype(np.float32),
        "sin": sin_full.astype(np.float32),
        "dct": np.stack([high, low]),
        "heads": stacked.astype(BF),
        "same": same.astype(np.float32),
    }


def dot(a, b):
    return jnp.dot(a, b, preferred_element_type=F32)


def dot_nt(a, b):
    return lax.dot_general(a, b, (((1,), (1,)), ((), ())), preferred_element_type=F32)


def dot_tn(a, b):
    return lax.dot_general(a, b, (((0,), (0,)), ((), ())), preferred_element_type=F32)


def split(x):
    high = x.astype(BF)
    return high, (x - high.astype(F32)).astype(BF)


def stack_heads(x, heads, head_count):
    return jnp.concatenate([x] * head_count, axis=0) * heads


def lanes_of_heads(x, head_count):
    rows = x.shape[0] // head_count
    return jnp.concatenate([x[h * rows:(h + 1) * rows] for h in range(head_count)], axis=1)


def gelu_parts(u):
    z = jnp.abs(u) * (1.0 / math.sqrt(2.0))
    t = 1.0 / (1.0 + 0.3275911 * z)
    e = jnp.exp(-0.5 * u * u)
    poly = t * (0.5 * 0.254829592 + t * (0.5 * -0.284496736 + t * (0.5 * 1.421413741 + t * (0.5 * -1.453152027 + t * (0.5 * 1.061405429)))))
    tail = poly * e
    cdf = jnp.where(u >= 0, 1.0 - tail, tail)
    return u * cdf, cdf + u * e * (1.0 / math.sqrt(2.0 * math.pi))


class Copies:
    def __init__(self, sems):
        self.sems = sems
        self.used = 0
        self.open = []

    def start(self, src, dst):
        copy = pltpu.make_async_copy(src, dst, self.sems.at[self.used])
        self.used += 1
        copy.start()
        return copy

    def out(self, src, dst):
        self.open.append(self.start(src, dst))

    def finish(self):
        for copy in self.open:
            copy.wait()


def forward_kernel(cfg, info, *refs):
    (wq, wk, wv, wo, wup, wdown, norms, scales, cos, sin, dct, heads, same) = refs[cfg["pieces"]:cfg["pieces"] + 13]
    h_in = refs[:cfg["pieces"]]
    refs = refs[cfg["pieces"] + 13 + cfg["alias"]:]
    (s_n1, s_n2, s_am, s_gp, s_qf, s_kf, s_v, s_mf, s_inv, s_st, s_kt, s_h, part) = refs[:13]
    (v_h, v_wqkv, v_wo, v_wup, v_wdown, v_norms, v_scales, v_cos, v_sin, v_dct, v_heads, v_same,
     o_n1, o_n2, o_am, o_gp, o_qf, o_kf, o_v, o_mf, o_inv, o_st, o_kt, o_part, state, total, sems, o_sems) = refs[13:]
    m = cfg["m"]
    rows = v_h.shape[0]
    e = v_wqkv.shape[1] // 3
    f = v_wup.shape[1]
    hc = cfg["heads"]
    blocks = rows // BLOCK
    count = BLOCK // CHUNK
    me = info[1]

    def outs(b):
        rb = pl.ds(pl.multiple_of(b * BLOCK, BLOCK), BLOCK)
        at = b ^ me
        pairs = [(o.at[rb], s.at[rb]) for o, s in (
            (o_n1, s_n1), (o_n2, s_n2), (o_am, s_am), (o_gp, s_gp), (o_qf, s_qf), (o_kf, s_kf), (o_v, s_v), (o_mf, s_mf), (o_inv, s_inv))]
        pairs.append((o_st.at[pl.ds(b * count, count)], s_st.at[pl.ds(b * count, count)]))
        pairs.append((o_kt.at[pl.ds(b * count, count)], s_kt.at[pl.ds(b * count, count)]))
        pairs.append((o_part.at[b], part.at[at & 1, at >> 1]))
        return [pltpu.make_async_copy(src, dst, o_sems.at[i, b]) for i, (src, dst) in enumerate(pairs)]

    @pl.when(info[0] == cfg["section"])
    def _():
        io = Copies(sems)
        if cfg["pieces"] == 1:
            h_copies = [io.start(h_in[0].at[m, 0], v_h)]
        else:
            h_copies = [io.start(h_in[k], v_h.at[pl.ds((me ^ k) * BLOCK, BLOCK)]) for k in range(cfg["pieces"])]
        h_copies += [io.start(norms, v_norms), io.start(scales, v_scales)]
        loads = [io.start(w.at[0], v_wqkv.at[:, pl.ds(i * e, e)]) for i, w in enumerate((wq, wk, wv))]
        loads += [io.start(cos, v_cos), io.start(sin, v_sin), io.start(dct, v_dct), io.start(heads, v_heads), io.start(same, v_same)]
        loads += [io.start(wup.at[0], v_wup)]
        loads += [io.start(wo.at[0], v_wo), io.start(wdown.at[0], v_wdown)]
        state[...] = jnp.zeros_like(state)
        total[...] = jnp.zeros_like(total)
        for copy in h_copies:
            copy.wait()

        def normed(b):
            rb = pl.ds(pl.multiple_of(b * BLOCK, BLOCK), BLOCK)
            hidden = v_h[rb].astype(F32)
            center = hidden - jnp.mean(hidden, axis=-1, keepdims=True)
            spread = jnp.mean(center * center, axis=-1, keepdims=True)
            xhat = center * lax.rsqrt(spread + EPSILON)
            o_n1[rb] = (xhat * v_norms[0:1, :] + v_norms[1:2, :]).astype(BF)
            o_n2[rb] = (xhat * v_norms[2:3, :] + v_norms[3:4, :]).astype(BF)

        @pl.loop(0, blocks)
        def _(b):
            normed(b)

        for copy in loads:
            copy.wait()
        if cfg["pieces"] > 1:
            io.out(v_h, s_h)

        @pl.loop(0, blocks)
        def _(b):
            rb = pl.ds(pl.multiple_of(b * BLOCK, BLOCK), BLOCK)
            qkv = dot(o_n1[rb], v_wqkv[...])
            cos_b = v_cos[rb]
            sin_b = v_sin[rb]

            def lift(x):
                pair = jnp.concatenate([x * cos_b, x * sin_b], axis=1)
                high, low = split(pair)
                coeffs = dot(high, v_dct[0]) + dot(low, v_dct[0]) + dot(high, v_dct[1])
                return v_scales[0:1, :] * jnp.exp(coeffs)

            q_feat = lift(qkv[:, :e])
            slot = lax.broadcasted_iota(jnp.int32, (BLOCK, e), 0) + b * BLOCK
            k_feat = jnp.where(slot < info[2 + m], lift(qkv[:, e:2 * e]), 0.0)
            value = qkv[:, 2 * e:].astype(BF)
            o_qf[rb] = q_feat
            o_kf[rb] = k_feat
            o_v[rb] = value
            q_b = q_feat.astype(BF)
            k_b = k_feat.astype(BF)
            row = lax.broadcasted_iota(jnp.int32, (CHUNK, hc * CHUNK), 0)
            col = lax.broadcasted_iota(jnp.int32, (CHUNK, hc * CHUNK), 1) % CHUNK
            causal = row >= col
            for c in range(count):
                rc = slice(c * CHUNK, (c + 1) * CHUNK)
                at = b * count + c
                q_c, k_c, v_c = q_b[rc], k_b[rc], value[rc]
                o_st[at] = state[...]
                o_kt[at] = total[...]
                weighted = (q_c.astype(F32) * total[0:1, :]).astype(BF)
                scores = jnp.where(causal, dot_nt(q_c, stack_heads(k_c, v_heads[...], hc)), 0.0).astype(BF)
                both = dot(scores, jnp.concatenate([stack_heads(v_c, v_heads[...], hc), v_heads[...]], axis=1))
                inverse = 1.0 / (both[:, e:] + dot(weighted, v_same[...].astype(BF)))
                mixed = (both[:, :e] + dot(q_c, state[...].astype(BF))) * inverse
                rg = pl.ds(pl.multiple_of(b * BLOCK + c * CHUNK, CHUNK), CHUNK)
                o_inv[rg] = inverse
                o_mf[rg] = mixed
                o_am[rg, f:] = mixed.astype(BF)
                state[...] += dot_tn(k_c, v_c) * v_same[...]
                total[...] += jnp.sum(k_c.astype(F32), axis=0, keepdims=True)
            up = dot(o_n2[rb], v_wup[...])
            act, slope = gelu_parts(up)
            o_am[rb, :f] = act.astype(BF)
            o_gp[rb] = slope.astype(BF)
            branch = dot(o_am[rb, f:], v_wo[...]) + dot(o_am[rb, :f], v_wdown[...])
            o_part[b] = branch.astype(BF)
            for copy in outs(b):
                copy.start()

        io.finish()

        @pl.loop(0, blocks)
        def _(b):
            for copy in outs(b):
                copy.wait()


def backward_kernel(cfg, info, *refs):
    np_ = cfg["pieces"]
    g_in = refs[:np_]
    (h_in, wq, wk, wv, wo, wup, wdown, norms, scales, cos, sin, dct, heads, same,
     s_am, s_gp, s_qf, s_kf, s_v, s_mf, s_inv, s_st, s_kt) = refs[np_:np_ + 23]
    refs = refs[np_ + 23 + cfg["alias"]:]
    (s_gb, s_gup, s_gqkv, part, sums) = refs[:5]
    (v_g, v_h, v_wqkv, v_wo, v_wup, v_wdown, v_norms, v_scales, v_cos, v_sin, v_dct, v_heads, v_same,
     i_gp, i_qf, i_kf, i_v, i_mf, i_inv, i_st, i_kt,
     o_gup, o_gqkv, o_part, o_sums, acc, acc_s, state, total, sems, o_sems) = refs[5:]
    m = cfg["m"]
    rows = v_h.shape[0]
    e = v_wqkv.shape[1] // 3
    hc = cfg["heads"]
    hd = e // hc
    d = v_h.shape[1]
    blocks = rows // BLOCK
    count = BLOCK // CHUNK
    me = info[1]

    def outs(b):
        rb = pl.ds(pl.multiple_of(b * BLOCK, BLOCK), BLOCK)
        at = b ^ me
        pairs = [(o_gup.at[rb], s_gup.at[rb]), (o_gqkv.at[rb], s_gqkv.at[rb]), (o_part.at[b], part.at[at & 1, at >> 1])]
        return [pltpu.make_async_copy(src, dst, o_sems.at[i, b]) for i, (src, dst) in enumerate(pairs)]

    @pl.when(info[0] == cfg["section"])
    def _():
        io = Copies(sems)
        if np_ == 1:
            loads = [io.start(g_in[0].at[m, 0], v_g)]
        else:
            loads = [io.start(g_in[k], v_g.at[pl.ds((me ^ k) * BLOCK, BLOCK)]) for k in range(np_)]
        h_src = h_in.at[m, 0] if cfg["h_rank"] == 4 else h_in
        loads += [io.start(wo.at[0], v_wo), io.start(wdown.at[0], v_wdown)]
        loads += [io.start(s_gp, i_gp)]
        loads += [io.start(s_mf, i_mf), io.start(s_inv, i_inv), io.start(heads, v_heads), io.start(same, v_same),
                 io.start(s_qf, i_qf), io.start(s_kf, i_kf), io.start(s_v, i_v), io.start(s_st, i_st), io.start(s_kt, i_kt)]
        loads += [io.start(cos, v_cos), io.start(sin, v_sin), io.start(dct, v_dct)]
        loads += [io.start(w.at[0], v_wqkv.at[:, pl.ds(i * e, e)]) for i, w in enumerate((wq, wk, wv))]
        loads += [io.start(wup.at[0], v_wup)]
        loads += [io.start(h_src, v_h), io.start(norms, v_norms), io.start(scales, v_scales)]
        state[...] = jnp.zeros_like(state)
        total[...] = jnp.zeros_like(total)
        acc[...] = jnp.zeros_like(acc)
        acc_s[...] = jnp.zeros_like(acc_s)
        for copy in loads:
            copy.wait()
        io.out(v_g, s_gb)

        def fold(x):
            return jnp.sum(x.reshape(x.shape[0] // 8, 8, x.shape[1]), axis=0)

        @pl.loop(0, blocks)
        def _(step):
            b = blocks - 1 - step
            rb = pl.ds(pl.multiple_of(b * BLOCK, BLOCK), BLOCK)
            g_b = v_g[rb]
            g_act = dot_nt(g_b, v_wdown[...])
            g_up = (g_act * i_gp[rb].astype(F32)).astype(BF)
            o_gup[rb] = g_up
            g_mixed = dot_nt(g_b, v_wo[...]).astype(BF).astype(F32)
            inverse = i_inv[rb]
            g_num = (g_mixed * inverse).astype(BF)
            high, low = split(g_num.astype(F32) * i_mf[rb])
            same_b = v_same[...].astype(BF)
            g_den = -(dot(high, same_b) + dot(low, same_b))
            gd_high, gd_low = split(g_den)
            q_feat = i_qf[rb]
            k_feat = i_kf[rb]
            value = i_v[rb]
            q_b = q_feat.astype(BF)
            k_b = k_feat.astype(BF)
            row = lax.broadcasted_iota(jnp.int32, (CHUNK, hc * CHUNK), 0)
            col = lax.broadcasted_iota(jnp.int32, (CHUNK, hc * CHUNK), 1) % CHUNK
            causal = row >= col
            row_t = lax.broadcasted_iota(jnp.int32, (hc * CHUNK, CHUNK), 0) % CHUNK
            col_t = lax.broadcasted_iota(jnp.int32, (hc * CHUNK, CHUNK), 1)
            causal_t = col_t >= row_t
            hm = v_heads[...]
            sel = hm * jnp.asarray(1.0 / hd, BF)
            gq_parts, gk_parts, gv_parts = [None] * count, [None] * count, [None] * count
            for c in reversed(range(count)):
                rc = slice(c * CHUNK, (c + 1) * CHUNK)
                at = b * count + c
                q_c, k_c, v_c, n_c, dh, dl = q_b[rc], k_b[rc], value[rc], g_num[rc], gd_high[rc], gd_low[rc]
                k_x = stack_heads(k_c, hm, hc)
                v_x = jnp.concatenate([stack_heads(v_c, hm, hc), sel, sel], axis=1)
                g_x = jnp.concatenate([n_c, dh, dl], axis=1)
                grid = jnp.where(causal, dot_nt(g_x, v_x), 0.0).astype(BF)
                grid_t = jnp.where(causal_t, dot_nt(v_x, g_x), 0.0).astype(BF)
                scores_t = jnp.where(causal_t, dot_nt(k_x, q_c), 0.0).astype(BF)
                before = jnp.concatenate(split(i_st[at]), axis=1)
                gq_parts[c] = dot(grid, k_x) + dot_nt(jnp.concatenate([n_c, n_c], axis=1), before) + g_den[rc] * i_kt[at][0:1, :]
                after = jnp.concatenate(split(state[...]), axis=1)
                gk_parts[c] = dot(lanes_of_heads(grid_t, hc), stack_heads(q_c, hm, hc)) + dot_nt(jnp.concatenate([v_c, v_c], axis=1), after) + total[0:1, :]
                gv_parts[c] = dot(lanes_of_heads(scores_t, hc), stack_heads(n_c, hm, hc)) + dot(k_c, after[:, :e])
                state[...] += dot_tn(q_c, n_c) * v_same[...]
                total[...] += jnp.sum(q_c.astype(F32) * g_den[rc], axis=0, keepdims=True)
            gc_q = jnp.concatenate(gq_parts, axis=0) * q_feat
            gc_k = jnp.concatenate(gk_parts, axis=0) * k_feat
            g_value = jnp.concatenate(gv_parts, axis=0)
            acc_s[...] += fold(gc_q + gc_k)
            cos_b = v_cos[rb]
            sin_b = v_sin[rb]

            def lower(gc):
                high, low = split(gc)
                both = dot_nt(high, v_dct[0]) + dot_nt(low, v_dct[0]) + dot_nt(high, v_dct[1])
                return cos_b * both[:, :e] + sin_b * both[:, e:]

            gqkv = jnp.concatenate([lower(gc_q), lower(gc_k), g_value], axis=1).astype(BF)
            o_gqkv[rb] = gqkv
            g_one = dot_nt(gqkv, v_wqkv[...])
            g_two = dot_nt(o_gup[rb], v_wup[...])
            hidden = v_h[rb].astype(F32)
            center = hidden - jnp.mean(hidden, axis=-1, keepdims=True)
            spread = jnp.mean(center * center, axis=-1, keepdims=True)
            rstd = lax.rsqrt(spread + EPSILON)
            xhat = center * rstd
            acc[0] += fold(g_one * xhat)
            acc[1] += fold(g_one)
            acc[2] += fold(g_two * xhat)
            acc[3] += fold(g_two)
            acc[4] += fold(v_g[rb].astype(F32))
            inner = g_one * v_norms[0:1, :] + g_two * v_norms[2:3, :]
            mean_t = jnp.mean(inner, axis=-1, keepdims=True)
            mean_x = jnp.mean(inner * xhat, axis=-1, keepdims=True)
            g_h = rstd * (inner - mean_t - xhat * mean_x)
            o_part[b] = g_h.astype(BF)
            for copy in outs(b):
                copy.start()

        for i in range(5):
            o_sums[i:i + 1, :] = jnp.sum(acc[i], axis=0, keepdims=True)
        o_sums[5:8, :] = jnp.zeros((3, d), F32)
        o_sums[5:6, :e] = jnp.sum(acc_s[...], axis=0, keepdims=True) / v_scales[0:1, :]
        io.out(o_sums, sums)
        io.finish()

        @pl.loop(0, blocks)
        def _(b):
            for copy in outs(b):
                copy.wait()


def like(shape, dtype):
    return jax.ShapeDtypeStruct(shape, dtype)


def forward_call(sizes, m, section, info, h_pieces, weights, tabs, store):
    rows, d, e, f, hc = sizes
    pieces = len(h_pieces)
    chunks = rows // CHUNK
    blocks = rows // BLOCK
    shapes = [
        like((rows, d), BF), like((rows, d), BF), like((rows, f + e), BF), like((rows, f), BF),
        like((rows, e), F32), like((rows, e), F32), like((rows, e), BF), like((rows, e), F32),
        like((rows, e), F32), like((chunks, e, e), F32), like((chunks, 8, e), F32), like((rows, d), BF),
    ]
    out_shapes = shapes + [like((2, 2, BLOCK, d), BF)]
    alias = len(store)
    operands = [info, *h_pieces, *weights, *tabs, *store]
    scratch = [
        pltpu.VMEM((rows, d), BF), pltpu.VMEM((d, 3 * e), BF), pltpu.VMEM((e, d), BF), pltpu.VMEM((d, f), BF), pltpu.VMEM((f, d), BF),
        pltpu.VMEM((8, d), F32), pltpu.VMEM((8, e), F32), pltpu.VMEM((rows, e), F32), pltpu.VMEM((rows, e), F32),
        pltpu.VMEM((2, 2 * e, e), BF), pltpu.VMEM((hc * CHUNK, e), BF), pltpu.VMEM((e, e), F32),
        pltpu.VMEM((rows, d), BF), pltpu.VMEM((rows, d), BF), pltpu.VMEM((rows, f + e), BF), pltpu.VMEM((rows, f), BF),
        pltpu.VMEM((rows, e), F32), pltpu.VMEM((rows, e), F32), pltpu.VMEM((rows, e), BF), pltpu.VMEM((rows, e), F32),
        pltpu.VMEM((rows, e), F32), pltpu.VMEM((chunks, e, e), F32), pltpu.VMEM((chunks, 8, e), F32), pltpu.VMEM((blocks, BLOCK, d), BF),
        pltpu.VMEM((e, e), F32), pltpu.VMEM((8, e), F32), pltpu.SemaphoreType.DMA((32,)), pltpu.SemaphoreType.DMA((12, blocks)),
    ]
    cfg = {"m": m, "section": section, "pieces": pieces, "heads": hc, "alias": alias}
    first = len(operands) - alias
    results = pl.pallas_call(
        functools.partial(forward_kernel, cfg),
        out_shape=out_shapes,
        in_specs=[SMEM] + [ANY] * (len(operands) - 1),
        out_specs=[ANY] * len(out_shapes),
        scratch_shapes=scratch,
        input_output_aliases={first + i: i for i in range(alias)},
        compiler_params=pltpu.CompilerParams(vmem_limit_bytes=VMEM_BYTES),
        cost_estimate=pl.CostEstimate(flops=2 * rows * d * (4 * e + 2 * f), bytes_accessed=25 * 2 ** 20, transcendentals=rows * (f + 2 * e)),
        name="forward",
    )(*operands)
    return list(results[:12]), results[12]


def backward_call(sizes, m, section, info, g_pieces, h_in, weights, tabs, store, back):
    rows, d, e, f, hc = sizes
    s_n1, s_n2, s_am, s_gp, s_qf, s_kf, s_v, s_mf, s_inv, s_st, s_kt, s_h = store
    pieces = len(g_pieces)
    chunks = rows // CHUNK
    blocks = rows // BLOCK
    shapes = [like((rows, d), BF), like((rows, f), BF), like((rows, 3 * e), BF)]
    out_shapes = shapes + [like((2, 2, BLOCK, d), BF), like((8, d), F32)]
    alias = len(back)
    operands = [info, *g_pieces, h_in, *weights, *tabs, s_am, s_gp, s_qf, s_kf, s_v, s_mf, s_inv, s_st, s_kt, *back]
    scratch = [
        pltpu.VMEM((rows, d), BF), pltpu.VMEM((rows, d), BF),
        pltpu.VMEM((d, 3 * e), BF), pltpu.VMEM((e, d), BF), pltpu.VMEM((d, f), BF), pltpu.VMEM((f, d), BF),
        pltpu.VMEM((8, d), F32), pltpu.VMEM((8, e), F32), pltpu.VMEM((rows, e), F32), pltpu.VMEM((rows, e), F32),
        pltpu.VMEM((2, 2 * e, e), BF), pltpu.VMEM((hc * CHUNK, e), BF), pltpu.VMEM((e, e), F32),
        pltpu.VMEM((rows, f), BF), pltpu.VMEM((rows, e), F32), pltpu.VMEM((rows, e), F32), pltpu.VMEM((rows, e), BF),
        pltpu.VMEM((rows, e), F32), pltpu.VMEM((rows, e), F32), pltpu.VMEM((chunks, e, e), F32), pltpu.VMEM((chunks, 8, e), F32),
        pltpu.VMEM((rows, f), BF), pltpu.VMEM((rows, 3 * e), BF), pltpu.VMEM((blocks, BLOCK, d), BF), pltpu.VMEM((8, d), F32),
        pltpu.VMEM((5, 8, d), F32), pltpu.VMEM((8, e), F32), pltpu.VMEM((e, e), F32), pltpu.VMEM((8, e), F32), pltpu.SemaphoreType.DMA((40,)), pltpu.SemaphoreType.DMA((3, blocks)),
    ]
    cfg = {"m": m, "section": section, "pieces": pieces, "heads": hc, "alias": alias, "h_rank": h_in.ndim}
    first = len(operands) - alias
    to = [0, 1, 2, 4]
    results = pl.pallas_call(
        functools.partial(backward_kernel, cfg),
        out_shape=out_shapes,
        in_specs=[SMEM] + [ANY] * (len(operands) - 1),
        out_specs=[ANY] * len(out_shapes),
        scratch_shapes=scratch,
        input_output_aliases={first + i: to[i] for i in range(alias)},
        compiler_params=pltpu.CompilerParams(vmem_limit_bytes=VMEM_BYTES),
        cost_estimate=pl.CostEstimate(flops=2 * rows * d * (4 * e + 2 * f), bytes_accessed=30 * 2 ** 20, transcendentals=0),
        name="backward",
    )(*operands)
    return [results[0], results[1], results[2], results[4]], results[3]


def body(tokens, cotangent, lengths, attn_gain, attn_bias, ffn_gain, ffn_bias, w_query, w_key, w_value, w_out, feat_scale, w_up, w_down, down_bias):
    section = lax.axis_index("section")
    tensor = lax.axis_index("tensor")
    teams = lax.axis_size("tensor")
    micro, _, rows, d = tokens.shape
    hc, hd = feat_scale.shape[1:]
    e = hc * hd
    f = w_up.shape[2]
    sizes = (rows, d, e, f, hc)
    share = rows // teams
    is_first = section == 0
    info = jnp.concatenate([jnp.stack([section, tensor]).astype(jnp.int32), lengths[:, 0]])
    norms = jnp.concatenate([attn_gain, attn_bias, ffn_gain, ffn_bias, jnp.zeros((4, d), F32)], axis=0)
    scales = jnp.broadcast_to(feat_scale.reshape(1, e), (8, e))
    made = host_tables(rows, hc, hd)
    tabs = [norms, scales] + [jnp.asarray(made[k]) for k in ("cos", "sin", "dct", "heads", "same")]
    weights = [w_query, w_key, w_value, w_out, w_up, w_down]
    both = ("section", "tensor")

    def swap(x, sec, bit):
        return lax.ppermute(x, both, [(sec * teams + i, sec * teams + (i ^ bit)) for i in range(teams)])

    def hand(x, source):
        return lax.ppermute(x, "section", [(source, 1 - source)])

    def reduce_rows(part, sec):
        near = part[0].astype(F32) + swap(part[1], sec, 1).astype(F32)
        return near[0] + swap(near[1].astype(BF), sec, 2).astype(F32)

    def gather_rows(own, sec):
        far = swap(own, sec, 2)
        return [own, swap(own, sec, 1), far, swap(far, sec, 1)]

    def own_rows(x, m):
        return lax.dynamic_slice(x[m, 0], (tensor * share, 0), (share, d)).astype(F32)

    stores, hidden = [], []
    for m in range(micro):
        store, part = forward_call(sizes, m, 0, info, [tokens], weights, tabs, [])
        stores.append(store)
        out = own_rows(tokens, m) + reduce_rows(part, 0) + down_bias[0]
        hidden.append(gather_rows(hand(out.astype(BF), 0), 1))
    tops, backs, grads = [], [], []
    for m in range(micro):
        stores[m], part = forward_call(sizes, m, 1, info, hidden[m], weights, tabs, stores[m])
        tops.append(hidden[m][0].astype(F32) + reduce_rows(part, 1) + down_bias[0])
        back, part = backward_call(sizes, m, 1, info, [cotangent], stores[m][11], weights, tabs, stores[m], [])
        backs.append(back)
        grad = own_rows(cotangent, m) + reduce_rows(part, 1)
        grads.append(gather_rows(hand(grad.astype(BF), 1), 0))
    bottoms = []
    for m in range(micro):
        backs[m], part = backward_call(sizes, m, 0, info, grads[m], tokens, weights, tabs, stores[m], backs[m])
        bottoms.append(grads[m][0].astype(F32) + reduce_rows(part, 0))
    ends = jnp.stack([jnp.where(is_first, bottoms[m], tops[m]) for m in range(micro)])[None, :, None]

    def weight_grad(lefts, rights):
        total = sum(dot_tn(left, right) for left, right in zip(lefts, rights))
        return lax.psum_scatter(total.astype(BF), "dp", scatter_dimension=0, tiled=True).astype(F32)

    gb = [back[0] for back in backs]
    down = weight_grad(gb, [store[2] for store in stores]).T
    up = weight_grad([store[1] for store in stores], [back[1] for back in backs])
    qkv = weight_grad([store[0] for store in stores], [back[2] for back in backs])
    small = sum(back[3] for back in backs)
    rows_small = lax.psum(lax.psum(small[:5], "tensor"), "dp")
    scale_small = lax.psum(small[5, :e], "dp").reshape(hc, hd)
    group = lax.axis_size("dp")
    place = lax.axis_index("dp")
    cut = lax.dynamic_slice(rows_small, (0, place * (d // group)), (5, d // group))
    scale_cut = lax.dynamic_slice(scale_small, (0, place * (hd // group)), (hc, hd // group))
    return (
        ends, cut[0:1], cut[1:2], cut[2:3], cut[3:4],
        qkv[None, :, :e], qkv[None, :, e:2 * e], qkv[None, :, 2 * e:], down[None, f:], scale_cut[None], up[None], down[None, :f],
        cut[4:5] / teams,
    )


def solution(mesh):
    return jax.shard_map(
        body,
        mesh=mesh,
        in_specs=(
            P(None, "dp", None, None), P(None, "dp", None, None), P(None, "dp"),
            P("section", None), P("section", None), P("section", None), P("section", None),
            P("section", None, "tensor"), P("section", None, "tensor"), P("section", None, "tensor"),
            P("section", "tensor", None), P("section", "tensor", None), P("section", None, "tensor"),
            P("section", "tensor", None), P("section", None),
        ),
        out_specs=(
            P("section", None, "dp", "tensor", None),
            P("section", "dp"), P("section", "dp"), P("section", "dp"), P("section", "dp"),
            P("section", "dp", "tensor"), P("section", "dp", "tensor"), P("section", "dp", "tensor"),
            P("section", "tensor", "dp"), P("section", "tensor", "dp"), P("section", "dp", "tensor"),
            P("section", "tensor", "dp"), P("section", "dp"),
        ),
        check_vma=False,
    )
```

```python
import functools
import math

import jax
import jax.numpy as jnp
import numpy as np
from jax import lax
from jax.experimental import pallas as pl
from jax.experimental.pallas import tpu as pltpu
from jax.sharding import PartitionSpec as P

ROT = 16
EPSILON = 1e-05
BLOCK = 256
CHUNK = 128
BF = jnp.bfloat16
F32 = jnp.float32
VMEM_BYTES = 60 * 1024 * 1024
ANY = pl.BlockSpec(memory_space=pl.ANY)
SMEM = pl.BlockSpec(memory_space=pltpu.SMEM)
VMEM = pl.BlockSpec(memory_space=pltpu.VMEM)


def host_tables(slot_rows, head_count, head_size):
    width = head_count * head_size
    halfway = ROT // 2
    column = np.arange(width) % head_size
    pair = np.where(column < halfway, column, column - halfway)
    inverse = np.exp(pair * (-2.0 * math.log(10000.0) / ROT))
    angles = np.arange(slot_rows)[:, None] * inverse[None, :]
    turned = (column < 2 * halfway)[None, :]
    cos_full = np.where(turned, np.cos(angles), 1.0)
    sin_full = np.where(turned, np.sin(angles), 0.0)
    order = np.arange(head_size)
    table = np.cos(np.pi * (order[None, :] + 0.5) * order[:, None] / head_size) * np.sqrt(2.0 / head_size)
    table = np.where(order[:, None] == 0, table * np.sqrt(0.5), table)
    partner = np.zeros((head_size, head_size))
    for i in range(halfway):
        partner[i + halfway, i] = -1.0
        partner[i, i + halfway] = 1.0
    eye = np.eye(head_count)
    dct = np.concatenate([np.kron(eye, table.T), np.kron(eye, partner @ table.T)], axis=0)
    high = dct.astype(np.float32).astype(BF)
    low = (dct - high.astype(np.float64)).astype(np.float32).astype(BF)
    lane_head = np.arange(width) // head_size
    heads = (np.arange(head_count)[:, None] == lane_head[None, :]).astype(np.float32)
    stacked = np.repeat(heads, CHUNK, axis=0)
    same = (lane_head[:, None] == lane_head[None, :]).astype(np.float32)
    return {
        "cos": cos_full.astype(np.float32),
        "sin": sin_full.astype(np.float32),
        "dct": np.stack([high, low]),
        "heads": stacked.astype(BF),
        "same": same.astype(np.float32),
    }


def dot(a, b):
    return jnp.dot(a, b, preferred_element_type=F32)


def dot_nt(a, b):
    return lax.dot_general(a, b, (((1,), (1,)), ((), ())), preferred_element_type=F32)


def dot_tn(a, b):
    return lax.dot_general(a, b, (((0,), (0,)), ((), ())), preferred_element_type=F32)


def split(x):
    high = x.astype(BF)
    return high, (x - high.astype(F32)).astype(BF)


def stack_heads(x, heads, head_count):
    return jnp.concatenate([x] * head_count, axis=0) * heads


def lanes_of_heads(x, head_count):
    rows = x.shape[0] // head_count
    return jnp.concatenate([x[h * rows:(h + 1) * rows] for h in range(head_count)], axis=1)


def gelu_parts(u):
    cdf = 0.5 + 0.5 * lax.erf(u * (1.0 / math.sqrt(2.0)))
    return u * cdf, cdf + u * (jnp.exp(-0.5 * u * u) * (1.0 / math.sqrt(2.0 * math.pi)))


class Copies:
    def __init__(self, sems):
        self.sems = sems
        self.used = 0
        self.open = []

    def start(self, src, dst):
        copy = pltpu.make_async_copy(src, dst, self.sems.at[self.used])
        self.used += 1
        copy.start()
        return copy

    def out(self, src, dst):
        self.open.append(self.start(src, dst))

    def finish(self):
        for copy in self.open:
            copy.wait()


def forward_kernel(cfg, info, *refs):
    (wq, wk, wv, wo, wup, wdown, norms, scales, cos, sin, dct, heads, same) = refs[cfg["pieces"]:cfg["pieces"] + 13]
    h_in = refs[:cfg["pieces"]]
    refs = refs[cfg["pieces"] + 13 + cfg["alias"]:]
    (s_n1, s_n2, s_am, s_gp, s_qf, s_kf, s_v, s_mf, s_inv, s_st, s_kt, s_h, part) = refs[:13]
    (v_h, v_wqkv, v_wo, v_wup, v_wdown, v_norms, v_scales, v_cos, v_sin, v_dct, v_heads, v_same,
     o_n1, o_n2, o_am, o_gp, o_qf, o_kf, o_v, o_mf, o_inv, o_st, o_kt, o_part, state, total, sems, o_sems) = refs[13:]
    m = cfg["m"]
    rows = v_h.shape[0]
    e = v_wqkv.shape[1] // 3
    f = v_wup.shape[1]
    hc = cfg["heads"]
    blocks = rows // BLOCK
    count = BLOCK // CHUNK
    me = info[1]

    def outs(b):
        rb = pl.ds(pl.multiple_of(b * BLOCK, BLOCK), BLOCK)
        at = b ^ me
        pairs = [(o.at[rb], s.at[rb]) for o, s in (
            (o_n1, s_n1), (o_n2, s_n2), (o_am, s_am), (o_gp, s_gp), (o_qf, s_qf), (o_kf, s_kf), (o_v, s_v), (o_mf, s_mf), (o_inv, s_inv))]
        pairs.append((o_st.at[pl.ds(b * count, count)], s_st.at[pl.ds(b * count, count)]))
        pairs.append((o_kt.at[pl.ds(b * count, count)], s_kt.at[pl.ds(b * count, count)]))
        pairs.append((o_part.at[b], part.at[at & 1, at >> 1]))
        return [pltpu.make_async_copy(src, dst, o_sems.at[i, b]) for i, (src, dst) in enumerate(pairs)]

    @pl.when(info[0] == cfg["section"])
    def _():
        io = Copies(sems)
        if cfg["pieces"] == 1:
            h_copies = [io.start(h_in[0].at[m, 0], v_h)]
        else:
            h_copies = [io.start(h_in[k], v_h.at[pl.ds((me ^ k) * BLOCK, BLOCK)]) for k in range(cfg["pieces"])]
        h_copies += [io.start(norms, v_norms), io.start(scales, v_scales)]
        loads = [io.start(w.at[0], v_wqkv.at[:, pl.ds(i * e, e)]) for i, w in enumerate((wq, wk, wv))]
        loads += [io.start(cos, v_cos), io.start(sin, v_sin), io.start(dct, v_dct), io.start(heads, v_heads), io.start(same, v_same)]
        loads += [io.start(wup.at[0], v_wup)]
        loads += [io.start(wo.at[0], v_wo), io.start(wdown.at[0], v_wdown)]
        state[...] = jnp.zeros_like(state)
        total[...] = jnp.zeros_like(total)
        for copy in h_copies:
            copy.wait()

        def normed(b):
            rb = pl.ds(pl.multiple_of(b * BLOCK, BLOCK), BLOCK)
            hidden = v_h[rb].astype(F32)
            center = hidden - jnp.mean(hidden, axis=-1, keepdims=True)
            spread = jnp.mean(center * center, axis=-1, keepdims=True)
            xhat = center * lax.rsqrt(spread + EPSILON)
            o_n1[rb] = (xhat * v_norms[0:1, :] + v_norms[1:2, :]).astype(BF)
            o_n2[rb] = (xhat * v_norms[2:3, :] + v_norms[3:4, :]).astype(BF)

        @pl.loop(0, blocks)
        def _(b):
            normed(b)

        for copy in loads:
            copy.wait()
        if cfg["pieces"] > 1:
            io.out(v_h, s_h)

        @pl.loop(0, blocks)
        def _(b):
            rb = pl.ds(pl.multiple_of(b * BLOCK, BLOCK), BLOCK)
            qkv = dot(o_n1[rb], v_wqkv[...])
            cos_b = v_cos[rb]
            sin_b = v_sin[rb]

            def lift(x):
                pair = jnp.concatenate([x * cos_b, x * sin_b], axis=1)
                high, low = split(pair)
                coeffs = dot(high, v_dct[0]) + dot(low, v_dct[0]) + dot(high, v_dct[1])
                return v_scales[0:1, :] * jnp.exp(coeffs)

            q_feat = lift(qkv[:, :e])
            slot = lax.broadcasted_iota(jnp.int32, (BLOCK, e), 0) + b * BLOCK
            k_feat = jnp.where(slot < info[2 + m], lift(qkv[:, e:2 * e]), 0.0)
            value = qkv[:, 2 * e:].astype(BF)
            o_qf[rb] = q_feat
            o_kf[rb] = k_feat
            o_v[rb] = value
            q_b = q_feat.astype(BF)
            k_b = k_feat.astype(BF)
            row = lax.broadcasted_iota(jnp.int32, (CHUNK, hc * CHUNK), 0)
            col = lax.broadcasted_iota(jnp.int32, (CHUNK, hc * CHUNK), 1) % CHUNK
            causal = row >= col
            for c in range(count):
                rc = slice(c * CHUNK, (c + 1) * CHUNK)
                at = b * count + c
                q_c, k_c, v_c = q_b[rc], k_b[rc], value[rc]
                o_st[at] = state[...]
                o_kt[at] = total[...]
                weighted = (q_c.astype(F32) * total[0:1, :]).astype(BF)
                scores = jnp.where(causal, dot_nt(q_c, stack_heads(k_c, v_heads[...], hc)), 0.0).astype(BF)
                both = dot(scores, jnp.concatenate([stack_heads(v_c, v_heads[...], hc), v_heads[...]], axis=1))
                inverse = 1.0 / (both[:, e:] + dot(weighted, v_same[...].astype(BF)))
                mixed = (both[:, :e] + dot(q_c, state[...].astype(BF))) * inverse
                rg = pl.ds(pl.multiple_of(b * BLOCK + c * CHUNK, CHUNK), CHUNK)
                o_inv[rg] = inverse
                o_mf[rg] = mixed
                o_am[rg, f:] = mixed.astype(BF)
                state[...] += dot_tn(k_c, v_c) * v_same[...]
                total[...] += jnp.sum(k_c.astype(F32), axis=0, keepdims=True)
            up = dot(o_n2[rb], v_wup[...])
            act, slope = gelu_parts(up)
            o_am[rb, :f] = act.astype(BF)
            o_gp[rb] = slope.astype(BF)
            branch = dot(o_am[rb, f:], v_wo[...]) + dot(o_am[rb, :f], v_wdown[...])
            o_part[b] = branch.astype(BF)
            for copy in outs(b):
                copy.start()

        io.finish()

        @pl.loop(0, blocks)
        def _(b):
            for copy in outs(b):
                copy.wait()


def backward_kernel(cfg, info, *refs):
    np_ = cfg["pieces"]
    g_in = refs[:np_]
    (h_in, wq, wk, wv, wo, wup, wdown, norms, scales, cos, sin, dct, heads, same,
     s_am, s_gp, s_qf, s_kf, s_v, s_mf, s_inv, s_st, s_kt) = refs[np_:np_ + 23]
    refs = refs[np_ + 23 + cfg["alias"]:]
    (s_gup, s_gqkv, part, sums) = refs[:4]
    (v_g, v_h, v_wqkv, v_wo, v_wup, v_wdown, v_norms, v_scales, v_cos, v_sin, v_dct, v_heads, v_same,
     i_gp, i_qf, i_kf, i_v, i_mf, i_inv, i_st, i_kt,
     o_gup, o_gqkv, o_part, o_sums, acc, acc_s, state, total, sems, o_sems) = refs[4:]
    m = cfg["m"]
    rows = v_h.shape[0]
    e = v_wqkv.shape[1] // 3
    hc = cfg["heads"]
    hd = e // hc
    d = v_h.shape[1]
    blocks = rows // BLOCK
    count = BLOCK // CHUNK
    me = info[1]

    def outs(b):
        rb = pl.ds(pl.multiple_of(b * BLOCK, BLOCK), BLOCK)
        at = b ^ me
        pairs = [(o_gup.at[rb], s_gup.at[rb]), (o_gqkv.at[rb], s_gqkv.at[rb]), (o_part.at[b], part.at[at & 1, at >> 1])]
        return [pltpu.make_async_copy(src, dst, o_sems.at[i, b]) for i, (src, dst) in enumerate(pairs)]

    @pl.when(info[0] == cfg["section"])
    def _():
        io = Copies(sems)
        loads = [io.start(g_in[0].at[m, 0] if cfg["g_rank"] == 4 else g_in[0], v_g)]
        h_src = h_in.at[m, 0] if cfg["h_rank"] == 4 else h_in
        loads += [io.start(wo.at[0], v_wo), io.start(wdown.at[0], v_wdown)]
        loads += [io.start(s_gp, i_gp)]
        loads += [io.start(s_mf, i_mf), io.start(s_inv, i_inv), io.start(heads, v_heads), io.start(same, v_same),
                 io.start(s_qf, i_qf), io.start(s_kf, i_kf), io.start(s_v, i_v), io.start(s_st, i_st), io.start(s_kt, i_kt)]
        loads += [io.start(cos, v_cos), io.start(sin, v_sin), io.start(dct, v_dct)]
        loads += [io.start(w.at[0], v_wqkv.at[:, pl.ds(i * e, e)]) for i, w in enumerate((wq, wk, wv))]
        loads += [io.start(wup.at[0], v_wup)]
        loads += [io.start(h_src, v_h), io.start(norms, v_norms), io.start(scales, v_scales)]
        state[...] = jnp.zeros_like(state)
        total[...] = jnp.zeros_like(total)
        acc[...] = jnp.zeros_like(acc)
        acc_s[...] = jnp.zeros_like(acc_s)
        for copy in loads:
            copy.wait()

        def fold(x):
            return jnp.sum(x.reshape(x.shape[0] // 8, 8, x.shape[1]), axis=0)

        @pl.loop(0, blocks)
        def _(step):
            b = blocks - 1 - step
            rb = pl.ds(pl.multiple_of(b * BLOCK, BLOCK), BLOCK)
            g_b = v_g[rb]
            g_act = dot_nt(g_b, v_wdown[...])
            g_up = (g_act * i_gp[rb].astype(F32)).astype(BF)
            o_gup[rb] = g_up
            g_mixed = dot_nt(g_b, v_wo[...]).astype(BF).astype(F32)
            inverse = i_inv[rb]
            g_num = (g_mixed * inverse).astype(BF)
            high, low = split(g_num.astype(F32) * i_mf[rb])
            same_b = v_same[...].astype(BF)
            g_den = -(dot(high, same_b) + dot(low, same_b))
            gd_high, gd_low = split(g_den)
            q_feat = i_qf[rb]
            k_feat = i_kf[rb]
            value = i_v[rb]
            q_b = q_feat.astype(BF)
            k_b = k_feat.astype(BF)
            row = lax.broadcasted_iota(jnp.int32, (CHUNK, hc * CHUNK), 0)
            col = lax.broadcasted_iota(jnp.int32, (CHUNK, hc * CHUNK), 1) % CHUNK
            causal = row >= col
            row_t = lax.broadcasted_iota(jnp.int32, (hc * CHUNK, CHUNK), 0) % CHUNK
            col_t = lax.broadcasted_iota(jnp.int32, (hc * CHUNK, CHUNK), 1)
            causal_t = col_t >= row_t
            hm = v_heads[...]
            sel = hm * jnp.asarray(1.0 / hd, BF)
            gq_parts, gk_parts, gv_parts = [None] * count, [None] * count, [None] * count
            for c in reversed(range(count)):
                rc = slice(c * CHUNK, (c + 1) * CHUNK)
                at = b * count + c
                q_c, k_c, v_c, n_c, dh, dl = q_b[rc], k_b[rc], value[rc], g_num[rc], gd_high[rc], gd_low[rc]
                k_x = stack_heads(k_c, hm, hc)
                v_x = jnp.concatenate([stack_heads(v_c, hm, hc), sel, sel], axis=1)
                g_x = jnp.concatenate([n_c, dh, dl], axis=1)
                grid = jnp.where(causal, dot_nt(g_x, v_x), 0.0).astype(BF)
                grid_t = jnp.where(causal_t, dot_nt(v_x, g_x), 0.0).astype(BF)
                scores_t = jnp.where(causal_t, dot_nt(k_x, q_c), 0.0).astype(BF)
                before = jnp.concatenate(split(i_st[at]), axis=1)
                gq_parts[c] = dot(grid, k_x) + dot_nt(jnp.concatenate([n_c, n_c], axis=1), before) + g_den[rc] * i_kt[at][0:1, :]
                after = jnp.concatenate(split(state[...]), axis=1)
                gk_parts[c] = dot(lanes_of_heads(grid_t, hc), stack_heads(q_c, hm, hc)) + dot_nt(jnp.concatenate([v_c, v_c], axis=1), after) + total[0:1, :]
                gv_parts[c] = dot(lanes_of_heads(scores_t, hc), stack_heads(n_c, hm, hc)) + dot(k_c, after[:, :e])
                state[...] += dot_tn(q_c, n_c) * v_same[...]
                total[...] += jnp.sum(q_c.astype(F32) * g_den[rc], axis=0, keepdims=True)
            gc_q = jnp.concatenate(gq_parts, axis=0) * q_feat
            gc_k = jnp.concatenate(gk_parts, axis=0) * k_feat
            g_value = jnp.concatenate(gv_parts, axis=0)
            acc_s[...] += fold(gc_q + gc_k)
            cos_b = v_cos[rb]
            sin_b = v_sin[rb]

            def lower(gc):
                high, low = split(gc)
                both = dot_nt(high, v_dct[0]) + dot_nt(low, v_dct[0]) + dot_nt(high, v_dct[1])
                return cos_b * both[:, :e] + sin_b * both[:, e:]

            gqkv = jnp.concatenate([lower(gc_q), lower(gc_k), g_value], axis=1).astype(BF)
            o_gqkv[rb] = gqkv
            g_one = dot_nt(gqkv, v_wqkv[...])
            g_two = dot_nt(o_gup[rb], v_wup[...])
            hidden = v_h[rb].astype(F32)
            center = hidden - jnp.mean(hidden, axis=-1, keepdims=True)
            spread = jnp.mean(center * center, axis=-1, keepdims=True)
            rstd = lax.rsqrt(spread + EPSILON)
            xhat = center * rstd
            acc[0] += fold(g_one * xhat)
            acc[1] += fold(g_one)
            acc[2] += fold(g_two * xhat)
            acc[3] += fold(g_two)
            acc[4] += fold(v_g[rb].astype(F32))
            inner = g_one * v_norms[0:1, :] + g_two * v_norms[2:3, :]
            mean_t = jnp.mean(inner, axis=-1, keepdims=True)
            mean_x = jnp.mean(inner * xhat, axis=-1, keepdims=True)
            g_h = rstd * (inner - mean_t - xhat * mean_x)
            o_part[b] = g_h.astype(BF)
            for copy in outs(b):
                copy.start()

        for i in range(5):
            o_sums[i:i + 1, :] = jnp.sum(acc[i], axis=0, keepdims=True)
        o_sums[5:8, :] = jnp.zeros((3, d), F32)
        o_sums[5:6, :e] = jnp.sum(acc_s[...], axis=0, keepdims=True) / v_scales[0:1, :]
        io.out(o_sums, sums)
        io.finish()

        @pl.loop(0, blocks)
        def _(b):
            for copy in outs(b):
                copy.wait()


def like(shape, dtype):
    return jax.ShapeDtypeStruct(shape, dtype)


def forward_call(sizes, m, section, info, h_pieces, weights, tabs, store):
    rows, d, e, f, hc = sizes
    pieces = len(h_pieces)
    chunks = rows // CHUNK
    blocks = rows // BLOCK
    shapes = [
        like((rows, d), BF), like((rows, d), BF), like((rows, f + e), BF), like((rows, f), BF),
        like((rows, e), F32), like((rows, e), F32), like((rows, e), BF), like((rows, e), F32),
        like((rows, e), F32), like((chunks, e, e), F32), like((chunks, 8, e), F32), like((rows, d), BF),
    ]
    out_shapes = shapes + [like((2, 2, BLOCK, d), BF)]
    alias = len(store)
    operands = [info, *h_pieces, *weights, *tabs, *store]
    scratch = [
        pltpu.VMEM((rows, d), BF), pltpu.VMEM((d, 3 * e), BF), pltpu.VMEM((e, d), BF), pltpu.VMEM((d, f), BF), pltpu.VMEM((f, d), BF),
        pltpu.VMEM((8, d), F32), pltpu.VMEM((8, e), F32), pltpu.VMEM((rows, e), F32), pltpu.VMEM((rows, e), F32),
        pltpu.VMEM((2, 2 * e, e), BF), pltpu.VMEM((hc * CHUNK, e), BF), pltpu.VMEM((e, e), F32),
        pltpu.VMEM((rows, d), BF), pltpu.VMEM((rows, d), BF), pltpu.VMEM((rows, f + e), BF), pltpu.VMEM((rows, f), BF),
        pltpu.VMEM((rows, e), F32), pltpu.VMEM((rows, e), F32), pltpu.VMEM((rows, e), BF), pltpu.VMEM((rows, e), F32),
        pltpu.VMEM((rows, e), F32), pltpu.VMEM((chunks, e, e), F32), pltpu.VMEM((chunks, 8, e), F32), pltpu.VMEM((blocks, BLOCK, d), BF),
        pltpu.VMEM((e, e), F32), pltpu.VMEM((8, e), F32), pltpu.SemaphoreType.DMA((32,)), pltpu.SemaphoreType.DMA((12, blocks)),
    ]
    cfg = {"m": m, "section": section, "pieces": pieces, "heads": hc, "alias": alias}
    first = len(operands) - alias
    results = pl.pallas_call(
        functools.partial(forward_kernel, cfg),
        out_shape=out_shapes,
        in_specs=[SMEM] + [ANY] * (len(operands) - 1),
        out_specs=[ANY] * len(out_shapes),
        scratch_shapes=scratch,
        input_output_aliases={first + i: i for i in range(alias)},
        compiler_params=pltpu.CompilerParams(vmem_limit_bytes=VMEM_BYTES),
        cost_estimate=pl.CostEstimate(flops=2 * rows * d * (4 * e + 2 * f), bytes_accessed=25 * 2 ** 20, transcendentals=rows * (f + 2 * e)),
        name="forward",
    )(*operands)
    return list(results[:12]), results[12]


def backward_call(sizes, m, section, info, g_in, h_in, weights, tabs, store, back):
    rows, d, e, f, hc = sizes
    s_n1, s_n2, s_am, s_gp, s_qf, s_kf, s_v, s_mf, s_inv, s_st, s_kt, s_h = store
    chunks = rows // CHUNK
    blocks = rows // BLOCK
    shapes = [like((rows, f), BF), like((rows, 3 * e), BF)]
    out_shapes = shapes + [like((2, 2, BLOCK, d), BF), like((8, d), F32)]
    alias = len(back)
    operands = [info, g_in, h_in, *weights, *tabs, s_am, s_gp, s_qf, s_kf, s_v, s_mf, s_inv, s_st, s_kt, *back]
    scratch = [
        pltpu.VMEM((rows, d), BF), pltpu.VMEM((rows, d), BF),
        pltpu.VMEM((d, 3 * e), BF), pltpu.VMEM((e, d), BF), pltpu.VMEM((d, f), BF), pltpu.VMEM((f, d), BF),
        pltpu.VMEM((8, d), F32), pltpu.VMEM((8, e), F32), pltpu.VMEM((rows, e), F32), pltpu.VMEM((rows, e), F32),
        pltpu.VMEM((2, 2 * e, e), BF), pltpu.VMEM((hc * CHUNK, e), BF), pltpu.VMEM((e, e), F32),
        pltpu.VMEM((rows, f), BF), pltpu.VMEM((rows, e), F32), pltpu.VMEM((rows, e), F32), pltpu.VMEM((rows, e), BF),
        pltpu.VMEM((rows, e), F32), pltpu.VMEM((rows, e), F32), pltpu.VMEM((chunks, e, e), F32), pltpu.VMEM((chunks, 8, e), F32),
        pltpu.VMEM((rows, f), BF), pltpu.VMEM((rows, 3 * e), BF), pltpu.VMEM((blocks, BLOCK, d), BF), pltpu.VMEM((8, d), F32),
        pltpu.VMEM((5, 8, d), F32), pltpu.VMEM((8, e), F32), pltpu.VMEM((e, e), F32), pltpu.VMEM((8, e), F32), pltpu.SemaphoreType.DMA((40,)), pltpu.SemaphoreType.DMA((3, blocks)),
    ]
    cfg = {"m": m, "section": section, "pieces": 1, "heads": hc, "alias": alias, "h_rank": h_in.ndim, "g_rank": g_in.ndim}
    first = len(operands) - alias
    to = [0, 1, 3]
    results = pl.pallas_call(
        functools.partial(backward_kernel, cfg),
        out_shape=out_shapes,
        in_specs=[SMEM] + [ANY] * (len(operands) - 1),
        out_specs=[ANY] * len(out_shapes),
        scratch_shapes=scratch,
        input_output_aliases={first + i: to[i] for i in range(alias)},
        compiler_params=pltpu.CompilerParams(vmem_limit_bytes=VMEM_BYTES),
        cost_estimate=pl.CostEstimate(flops=2 * rows * d * (4 * e + 2 * f), bytes_accessed=30 * 2 ** 20, transcendentals=0),
        name="backward",
    )(*operands)
    return [results[0], results[1], results[3]], results[2]


def arrange_kernel(m, info, p_0, p_1, p_2, p_3, cotangent, out, held, sems):
    me = info[1]
    block = p_0.shape[0]

    def run(copies):
        for copy in copies:
            copy.start()
        for copy in copies:
            copy.wait()

    @pl.when(info[0] == 0)
    def _():
        run([pltpu.make_async_copy(p, held.at[pl.ds((me ^ k) * block, block)], sems.at[k]) for k, p in enumerate((p_0, p_1, p_2, p_3))])

    @pl.when(info[0] != 0)
    def _():
        run([pltpu.make_async_copy(cotangent.at[m, 0], held, sems.at[0])])

    run([pltpu.make_async_copy(held, out, sems.at[0])])


def arrange_call(rows, d, m, info, pieces, cotangent):
    return pl.pallas_call(
        functools.partial(arrange_kernel, m),
        out_shape=like((rows, d), BF),
        in_specs=[SMEM] + [ANY] * 5,
        out_specs=ANY,
        scratch_shapes=[pltpu.VMEM((rows, d), BF), pltpu.SemaphoreType.DMA((4,))],
        cost_estimate=pl.CostEstimate(flops=0, bytes_accessed=4 * rows * d, transcendentals=0),
        name="arrange",
    )(info, *pieces, cotangent)


def body(tokens, cotangent, lengths, attn_gain, attn_bias, ffn_gain, ffn_bias, w_query, w_key, w_value, w_out, feat_scale, w_up, w_down, down_bias):
    section = lax.axis_index("section")
    tensor = lax.axis_index("tensor")
    teams = lax.axis_size("tensor")
    micro, _, rows, d = tokens.shape
    hc, hd = feat_scale.shape[1:]
    e = hc * hd
    f = w_up.shape[2]
    sizes = (rows, d, e, f, hc)
    share = rows // teams
    is_first = section == 0
    info = jnp.concatenate([jnp.stack([section, tensor]).astype(jnp.int32), lengths[:, 0]])
    norms = jnp.concatenate([attn_gain, attn_bias, ffn_gain, ffn_bias, jnp.zeros((4, d), F32)], axis=0)
    scales = jnp.broadcast_to(feat_scale.reshape(1, e), (8, e))
    made = host_tables(rows, hc, hd)
    tabs = [norms, scales] + [jnp.asarray(made[k]) for k in ("cos", "sin", "dct", "heads", "same")]
    weights = [w_query, w_key, w_value, w_out, w_up, w_down]
    both = ("section", "tensor")

    def swap(x, sec, bit):
        return lax.ppermute(x, both, [(sec * teams + i, sec * teams + (i ^ bit)) for i in range(teams)])

    def hand(x, source):
        return lax.ppermute(x, "section", [(source, 1 - source)])

    def gather_rows(own, sec):
        far = swap(own, sec, 2)
        return [own, swap(own, sec, 1), far, swap(far, sec, 1)]

    def own_rows(x, m):
        return lax.dynamic_slice(x[m, 0], (tensor * share, 0), (share, d)).astype(F32)

    def weight_grad_sum(lefts, rights):
        return sum(dot_tn(left, right) for left, right in zip(lefts, rights)).astype(BF)

    def scatter(total):
        return lax.psum_scatter(total, "dp", scatter_dimension=0, tiled=True)

    def tie(x, *after):
        return lax.optimization_barrier((x, *after))[0]

    def near_sum(part, sec):
        return part[0].astype(F32) + swap(part[1], sec, 1).astype(F32)

    def far_sum(near, sec):
        return near[0] + swap(near[1].astype(BF), sec, 2).astype(F32)

    def tie_all(*values):
        return lax.optimization_barrier(values)

    def residual(start, near, far):
        return start + near[0] + far.astype(F32)

    def forward(m, sec, after, pieces, store):
        return forward_call(sizes, m, sec, tie(info, after), pieces, weights, tabs, store)

    def backward(m, sec, after, g_in, h_in, back):
        back, part = backward_call(sizes, m, sec, tie(info, after), g_in, h_in, weights, tabs, stores[m], back)
        return back, part

    def far_part(near, sec):
        sent = near[1].astype(BF)
        return sent, swap(sent, sec, 2)

    stores, backs = [None, None], [None, None]
    stores[0], part = forward(0, 0, lengths, [tokens], [])
    near = near_sum(part, 0)
    sent, far = far_part(near, 0)
    out = (residual(own_rows(tokens, 0), near, far) + down_bias[0]).astype(BF)
    took = hand(out, 0)
    stores[1], part = forward(1, 0, out, [tokens], [])
    took, part = tie_all(took, part)
    pieces = gather_rows(took, 1)
    near = near_sum(part, 0)
    sent, far = far_part(near, 0)
    out = (residual(own_rows(tokens, 1), near, far) + down_bias[0]).astype(BF)
    took = hand(out, 0)
    first_rows = pieces[0]
    stores[0], top_zero = forward(0, 1, out, pieces, stores[0])
    took, top_zero = tie_all(took, top_zero)
    second_rows = took
    far_rows, near_rows = swap(took, 1, 2), swap(took, 1, 1)
    backs[0], part = backward(0, 1, took, cotangent, stores[0][11], [])
    far_rows, near_rows, part = tie_all(far_rows, near_rows, part)
    pieces = [second_rows, near_rows, far_rows, swap(far_rows, 1, 1)]
    near = near_sum(part, 1)
    sent, far = far_part(near, 1)
    stores[1], top_one = forward(1, 1, sent, pieces, stores[1])
    far, top_one = tie_all(far, top_one)
    grad = residual(own_rows(cotangent, 0), near, far).astype(BF)
    took = hand(grad, 1)
    backs[1], part = backward(1, 1, grad, cotangent, stores[1][11], [])
    took, part = tie_all(took, part)
    near = near_sum(part, 1)
    sent, far = far_part(near, 1)
    grad = residual(own_rows(cotangent, 1), near, far).astype(BF)
    took_next = hand(grad, 1)
    got_zero = gather_rows(tie(took, grad), 0)
    gb_zero = arrange_call(rows, d, 0, info, got_zero, cotangent)
    backs[0], low_zero = backward(0, 0, gb_zero, gb_zero, tokens, backs[0])
    took_next, low_zero = tie_all(took_next, low_zero)
    got_one = gather_rows(took_next, 0)
    gb_one = arrange_call(rows, d, 1, info, got_one, cotangent)
    gb = [gb_zero, gb_one]
    down_sum = weight_grad_sum(gb, [store[2] for store in stores])
    down = scatter(down_sum)
    backs[1], low_one = backward(1, 0, down_sum, gb_one, tokens, backs[1])
    bottoms = [(low_zero, got_zero[0]), (low_one, got_one[0])]
    parts = [(top_zero, first_rows), (top_one, second_rows)]
    qkv_sum = weight_grad_sum([store[0] for store in stores], [back[1] for back in backs])
    up_sum = weight_grad_sum([store[1] for store in stores], [back[0] for back in backs])
    rest_sum = jnp.concatenate([up_sum, qkv_sum], axis=1)
    rest = scatter(rest_sum)
    bottoms = [far_sum(near_sum(tie(part, rest_sum), 0), 0) + got.astype(F32) for part, got in bottoms]
    tops = [far_sum(near_sum(tie(part, rest_sum), 1), 1) + got.astype(F32) + down_bias[0] for part, got in parts]
    ends = jnp.stack([jnp.where(is_first, bottoms[m], tops[m]) for m in range(micro)])[None, :, None]
    down = down.astype(F32).T
    up, qkv = rest[:, :f].astype(F32), rest[:, f:].astype(F32)
    small = tie(sum(back[2] for back in backs), rest_sum)
    rows_small = lax.psum(lax.psum(small[:5], "tensor"), "dp")
    scale_small = lax.psum(small[5, :e], "dp").reshape(hc, hd)
    group = lax.axis_size("dp")
    place = lax.axis_index("dp")
    cut = lax.dynamic_slice(rows_small, (0, place * (d // group)), (5, d // group))
    scale_cut = lax.dynamic_slice(scale_small, (0, place * (hd // group)), (hc, hd // group))
    return (
        ends, cut[0:1], cut[1:2], cut[2:3], cut[3:4],
        qkv[None, :, :e], qkv[None, :, e:2 * e], qkv[None, :, 2 * e:], down[None, f:], scale_cut[None], up[None], down[None, :f],
        cut[4:5] / teams,
    )


def solution(mesh):
    return jax.shard_map(
        body,
        mesh=mesh,
        in_specs=(
            P(None, "dp", None, None), P(None, "dp", None, None), P(None, "dp"),
            P("section", None), P("section", None), P("section", None), P("section", None),
            P("section", None, "tensor"), P("section", None, "tensor"), P("section", None, "tensor"),
            P("section", "tensor", None), P("section", "tensor", None), P("section", None, "tensor"),
            P("section", "tensor", None), P("section", None),
        ),
        out_specs=(
            P("section", None, "dp", "tensor", None),
            P("section", "dp"), P("section", "dp"), P("section", "dp"), P("section", "dp"),
            P("section", "dp", "tensor"), P("section", "dp", "tensor"), P("section", "dp", "tensor"),
            P("section", "tensor", "dp"), P("section", "tensor", "dp"), P("section", "dp", "tensor"),
            P("section", "tensor", "dp"), P("section", "dp"),
        ),
        check_vma=False,
    )
```

```python
import functools
import math

import jax
import jax.numpy as jnp
import numpy as np
from jax import lax
from jax.experimental import pallas as pl
from jax.experimental.pallas import tpu as pltpu
from jax.sharding import PartitionSpec as P

ROT = 16
EPSILON = 1e-05
BLOCK = 512
CHUNK = 128
WIDE = 512
BF = jnp.bfloat16
F32 = jnp.float32
VMEM_BYTES = 60 * 1024 * 1024
ANY = pl.BlockSpec(memory_space=pl.ANY)


def host_tables(slot_rows, head_count, head_size):
    width = head_count * head_size
    halfway = ROT // 2
    column = np.arange(2 * head_size) % head_size
    pair = np.where(column < halfway, column, column - halfway)
    inverse = np.exp(pair * (-2.0 * math.log(10000.0) / ROT))
    angles = np.arange(slot_rows)[:, None] * inverse[None, :]
    turned = (column < 2 * halfway)[None, :]
    sign = np.where(column < halfway, -1.0, 1.0)[None, :]
    cos_full = np.where(turned, np.cos(angles), 1.0)
    sin_full = np.where(turned, sign * np.sin(angles), 0.0)
    order = np.arange(head_size)
    table = np.cos(np.pi * (order[None, :] + 0.5) * order[:, None] / head_size) * np.sqrt(2.0 / head_size)
    table = np.where(order[:, None] == 0, table * np.sqrt(0.5), table)
    dct = np.kron(np.eye(head_count), table.T)
    high = dct.astype(np.float32).astype(BF)
    low = (dct - high.astype(np.float64)).astype(np.float32).astype(BF)
    lane_head = np.arange(width) // head_size
    heads = (np.arange(head_count)[:, None] == lane_head[None, :]).astype(np.float32)
    same = (lane_head[:, None] == lane_head[None, :]).astype(np.float32)
    return {
        "turn": np.stack([cos_full, sin_full]).astype(np.float32),
        "dct": np.stack([high, low]),
        "heads": np.repeat(heads, CHUNK, axis=0).astype(BF),
        "same": same.astype(np.float32),
    }


def dot(a, b):
    return jnp.dot(a, b, preferred_element_type=F32)


def dot_nt(a, b):
    return lax.dot_general(a, b, (((1,), (1,)), ((), ())), preferred_element_type=F32)


def dot_tn(a, b):
    return lax.dot_general(a, b, (((0,), (0,)), ((), ())), preferred_element_type=F32)


def split(x):
    high = x.astype(BF)
    return high, (x - high.astype(F32)).astype(BF)


def stack_heads(x, heads, head_count):
    return jnp.concatenate([x] * head_count, axis=0) * heads


def lanes_of_heads(x, head_count):
    rows = x.shape[0] // head_count
    return jnp.concatenate([x[h * rows:(h + 1) * rows] for h in range(head_count)], axis=1)


def gelu_parts(u):
    cdf = 0.5 + 0.5 * lax.erf(u * (1.0 / math.sqrt(2.0)))
    return u * cdf, cdf + u * (jnp.exp(-0.5 * u * u) * (1.0 / math.sqrt(2.0 * math.pi)))


def partner(x, head_size):
    half = ROT // 2
    lane = lax.broadcasted_iota(jnp.int32, x.shape, 1) & (head_size - 1)
    return jnp.where(lane < half, pltpu.roll(x, x.shape[1] - half, 1), pltpu.roll(x, half, 1))


def standardize(hidden):
    center = hidden - jnp.mean(hidden, axis=-1, keepdims=True)
    spread = jnp.mean(center * center, axis=-1, keepdims=True)
    rstd = lax.rsqrt(spread + EPSILON)
    return center * rstd, rstd


def rows_at(b, size, base=0):
    return pl.ds(pl.multiple_of(b * size + base, size), size)


def flat_scales(ref, head_count):
    return jnp.concatenate([ref[h:h + 1, :] for h in range(head_count)], axis=1)


class Routed:
    def __init__(self, src, keep, send, at, sem):
        self.near = pltpu.make_async_copy(src, keep.at[at >> 1], sem)
        self.far = pltpu.make_async_copy(src, send.at[at >> 1], sem)
        self.at = at

    def start(self):
        @pl.when((self.at & 1) == 0)
        def _():
            self.near.start()

        @pl.when((self.at & 1) != 0)
        def _():
            self.far.start()

    def wait(self):
        self.near.wait()


class Copies:
    def __init__(self, sems):
        self.sems = sems
        self.used = 0

    def start(self, *pairs):
        made = []
        for src, dst in pairs:
            copy = pltpu.make_async_copy(src, dst, self.sems.at[self.used])
            self.used += 1
            copy.start()
            made.append(copy)
        return made


def wait(copies):
    for copy in copies:
        copy.wait()


def looped_out(pairs, sems, first, b):
    return [pltpu.make_async_copy(src, dst, sems.at[first + i, b]) for i, (src, dst) in enumerate(pairs)]


def forward_kernel(cfg, order, *refs):
    pieces, base, share, origin, e, f, hc = (cfg[k] for k in ("pieces", "base", "share", "origin", "e", "f", "hc"))
    hd = e // hc
    carried = cfg["carried"]
    refs = list(refs)

    def take(n):
        out = refs[:n]
        del refs[:n]
        return out

    h_in = take(pieces)
    wq, wk, wv, wo, wup, wdown, *norms, scales, turn, dct, heads, same, lengths = take(16)
    cotangent = None if cfg["branch"] else take(1)[0]
    c_in = take(2 if carried else 0)
    take(cfg["alias"])
    s_n1, s_n2, s_am, s_gp, s_qf, s_kf, s_v, s_mf, s_inv, s_st, s_kt, s_h, own, c_st, c_kt = take(15)
    keep, send = take(2) if cfg["branch"] else (None, None)
    s_mix = None if cfg["branch"] else take(1)[0]
    (v_h, v_wqkv, v_wo, v_wup, v_wdown, v_norms, v_scales, v_turn, v_dct, v_heads, v_same,
     o_n1, o_n2, o_am, o_gp, o_qf, o_kf, o_v, o_mf, o_inv, o_st, o_kt, o_part, state, total, v_len, v_g, o_mix, sems, o_sems) = refs
    rows = v_h.shape[0]
    blocks = rows // BLOCK
    wides = rows // WIDE
    count = BLOCK // CHUNK
    me = lax.axis_index("tensor")

    def outs_a(b):
        rb, ro = rows_at(b, BLOCK), rows_at(b, BLOCK, base)
        return looped_out([(o_n1.at[rb], s_n1.at[ro]), (o_n2.at[rb], s_n2.at[ro])], o_sems, 0, b)

    def outs_b(b):
        rb, ro = rows_at(b, BLOCK), rows_at(b, BLOCK, base)
        cb, co = pl.ds(b * count, count), pl.ds(b * count + base // CHUNK, count)
        return looped_out([(o.at[rb], s.at[ro]) for o, s in ((o_qf, s_qf), (o_kf, s_kf), (o_v, s_v), (o_mf, s_mf), (o_inv, s_inv))]
                          + [(o_st.at[cb], s_st.at[co]), (o_kt.at[cb], s_kt.at[co])], o_sems, 2, b)

    def outs_c(b):
        rb, ro = rows_at(b, WIDE), rows_at(b, WIDE, base)
        copies = looped_out([(o_am.at[rb], s_am.at[ro]), (o_gp.at[rb], s_gp.at[ro])] + ([] if cfg["branch"] else [(o_mix.at[rb], s_mix.at[ro])]), o_sems, 9, b)
        for i in range(WIDE // share if cfg["branch"] else 0):
            at = (b * (WIDE // share) + i + origin) ^ me
            copies.append(Routed(o_part.at[rows_at(b * (WIDE // share) + i, share)], keep, send, at, o_sems.at[11 + i, b]))
        return copies

    @pl.when(lax.axis_index("section") == cfg["section"])
    def _():
        io = Copies(sems)
        if pieces == 1:
            in_h = io.start((h_in[0].at[cfg["m"], 0, pl.ds(base, rows)] if len(h_in[0].shape) == 4 else h_in[0], v_h))
        else:
            halves = pieces // 4
            in_h = io.start(*[(h_in[h * 4 + k], v_h.at[rows_at((me ^ k) * halves + h, rows // pieces)]) for h in range(halves) for k in range(4)])
        in_h += io.start(*[(norm, v_norms.at[i]) for i, norm in enumerate(norms)], (scales.at[0], v_scales))
        in_b = io.start(*[(w.at[0], v_wqkv.at[:, pl.ds(i * e, e)]) for i, w in enumerate((wq, wk, wv))], (turn.at[:, pl.ds(base, rows)], v_turn),
                        (dct, v_dct), (heads, v_heads), (same, v_same), (lengths, v_len))
        if carried:
            in_b += io.start((c_in[0], state), (c_in[1], total))
        else:
            state[...] = jnp.zeros_like(state)
            total[...] = jnp.zeros_like(total)
        in_c = io.start((wup.at[0], v_wup), (wo.at[0], v_wo), (wdown.at[0], v_wdown),
                        *([] if cfg["branch"] else [(cotangent.at[cfg["m"], 0], v_g)]))
        wait(in_h)
        out_h = io.start(*([(v_h, s_h.at[pl.ds(base, rows)])] if cfg["section"] else []), (v_h.at[rows_at(me, rows // 4)], own))

        @pl.loop(0, blocks)
        def _(b):
            rb = rows_at(b, BLOCK)
            xhat, _ = standardize(v_h[rb].astype(F32))
            o_n1[rb] = (xhat * v_norms[0] + v_norms[1]).astype(BF)
            o_n2[rb] = (xhat * v_norms[2] + v_norms[3]).astype(BF)
            for copy in outs_a(b):
                copy.start()

        wait(in_b)

        @pl.loop(0, blocks)
        def _(b):
            rb = rows_at(b, BLOCK)
            qkv = dot(o_n1[rb], v_wqkv[...])
            cos_b = jnp.concatenate([jnp.concatenate([v_turn[0, rb]] * (hc // 2), axis=1)] * 2, axis=0)
            sin_b = jnp.concatenate([jnp.concatenate([v_turn[1, rb]] * (hc // 2), axis=1)] * 2, axis=0)
            pair = jnp.concatenate([qkv[:, :e], qkv[:, e:2 * e]], axis=0)
            high, low = split(pair * cos_b + partner(pair, hd) * sin_b)
            feats = flat_scales(v_scales, hc) * jnp.exp(dot(high, v_dct[0]) + dot(low, v_dct[0]) + dot(high, v_dct[1]))
            q_feat = feats[:BLOCK]
            slot = lax.broadcasted_iota(jnp.int32, (BLOCK, e), 0) + (b * BLOCK + base)
            k_feat = jnp.where(slot < v_len[cfg["m"]:cfg["m"] + 1, :], feats[BLOCK:], 0.0)
            value = qkv[:, 2 * e:].astype(BF)
            o_qf[rb] = q_feat
            o_kf[rb] = k_feat
            o_v[rb] = value
            q_b = q_feat.astype(BF)
            k_b = k_feat.astype(BF)
            row = lax.broadcasted_iota(jnp.int32, (CHUNK, hc * CHUNK), 0)
            col = lax.broadcasted_iota(jnp.int32, (CHUNK, hc * CHUNK), 1) & (CHUNK - 1)
            causal = row >= col
            for c in range(count):
                rc = slice(c * CHUNK, (c + 1) * CHUNK)
                at = b * count + c
                q_c, k_c, v_c = q_b[rc], k_b[rc], value[rc]
                o_st[at] = state[...]
                o_kt[at] = total[...]
                weighted = (q_c.astype(F32) * total[0:1, :]).astype(BF)
                scores = jnp.where(causal, dot_nt(q_c, stack_heads(k_c, v_heads[...], hc)), 0.0).astype(BF)
                both = dot(scores, jnp.concatenate([stack_heads(v_c, v_heads[...], hc), v_heads[...]], axis=1))
                inverse = 1.0 / (both[:, e:] + dot(weighted, v_same[...].astype(BF)))
                mixed = (both[:, :e] + dot(q_c, state[...].astype(BF))) * inverse
                rg = rows_at(at, CHUNK)
                o_inv[rg] = inverse
                o_mf[rg] = mixed
                o_am[rg, f:] = mixed.astype(BF)
                state[...] += dot_tn(k_c, v_c) * v_same[...]
                total[...] += jnp.sum(k_c.astype(F32), axis=0, keepdims=True)
            for copy in outs_b(b):
                copy.start()

        out_s = io.start((state, c_st), (total, c_kt))
        wait(in_c)

        @pl.loop(0, wides)
        def _(b):
            rb = rows_at(b, WIDE)
            act, slope = gelu_parts(dot(o_n2[rb], v_wup[...]))
            o_am[rb, :f] = act.astype(BF)
            if not cfg["branch"]:
                slope = slope * dot_nt(v_g[rb], v_wdown[...])
                o_mix[rb] = dot_nt(v_g[rb], v_wo[...]).astype(BF)
            o_gp[rb] = slope.astype(BF)
            if cfg["branch"]:
                o_part[rb] = (dot(o_am[rb, f:], v_wo[...]) + dot(o_am[rb, :f], v_wdown[...])).astype(BF)
            for copy in outs_c(b):
                copy.start()

        wait(out_h + out_s)

        @pl.loop(0, blocks)
        def _(b):
            wait(outs_a(b) + outs_b(b))

        @pl.loop(0, wides)
        def _(b):
            wait(outs_c(b))


def backward_kernel(cfg, order, *refs):
    base, share, e, f, hc = (cfg[k] for k in ("base", "share", "e", "f", "hc"))
    hd = e // hc
    carried = cfg["carried"]
    refs = list(refs)

    def take(n):
        out = refs[:n]
        del refs[:n]
        return out

    g_in = take(cfg["grads"])
    h_in, wq, wk, wv, wo, wup, wdown, *norms, scales, turn, dct, heads, same, _ = take(17)
    s_qf, s_kf, s_v, s_mf, s_inv, s_st, s_kt = take(7)
    opened = cfg["opened"]
    (in_gup, in_mix) = take(2) if opened else (None, None)
    c_in = take(2 if carried else 0)
    s_gp = take(cfg["alias"])[0] if not opened else None
    s_gup = take(1)[0] if not opened else None
    s_gqkv, keep, send, own, sums, c_st, c_kt = take(7)
    (v_g, v_h, v_wqkv, v_wo, v_wup, v_wdown, v_norms, v_scales, v_turn, v_dct, v_heads, v_same,
     i_gp, i_qf, i_kf, i_v, i_mf, i_inv, i_st, i_kt,
     o_gup, o_gqkv, o_part, o_sums, mixes, acc, acc_s, state, total, sems, o_sems) = refs
    rows, d = v_h.shape
    blocks = rows // BLOCK
    wides = rows // WIDE
    chunks = rows // CHUNK
    count = BLOCK // CHUNK
    me = lax.axis_index("tensor")

    def place(x):
        return x.at[cfg["m"], 0, pl.ds(base, rows)] if len(x.shape) == 4 else x.at[pl.ds(base, rows)]

    def outs_a(b):
        rb, ro = rows_at(b, WIDE), rows_at(b, WIDE, base)
        return [] if opened else looped_out([(o_gup.at[rb], s_gup.at[ro])], o_sems, 0, b)

    def outs_b(b):
        rb, ro = rows_at(b, BLOCK), rows_at(b, BLOCK, base)
        return looped_out([(o_gqkv.at[rb], s_gqkv.at[ro])], o_sems, 1, b)

    def outs_c(b):
        copies = []
        for i in range(BLOCK // share):
            at = (b * (BLOCK // share) + i) ^ me
            copies.append(Routed(o_part.at[rows_at(b * (BLOCK // share) + i, share)], keep, send, at, o_sems.at[2 + i, b]))
        return copies

    @pl.when(lax.axis_index("section") == cfg["section"])
    def _():
        io = Copies(sems)
        some = pl.ds(base, rows)
        some_chunks = pl.ds(base // CHUNK, chunks)
        in_g = [(place(g_in[0]), v_g)] if len(g_in) == 1 else [(g, v_g.at[pl.ds(i * g.shape[0], g.shape[0])]) for i, g in enumerate(g_in)]
        in_a = io.start(*in_g, *([(in_gup.at[some], o_gup), (in_mix.at[some], mixes)] if opened else
                                [(wdown.at[0], v_wdown), (wo.at[0], v_wo), (s_gp.at[some], i_gp)]))
        in_b = io.start((s_mf.at[some], i_mf), (s_inv.at[some], i_inv), (s_qf.at[some], i_qf), (s_kf.at[some], i_kf), (s_v.at[some], i_v),
                        (s_st.at[some_chunks], i_st), (s_kt.at[some_chunks], i_kt), (heads, v_heads), (same, v_same),
                        (turn.at[:, some], v_turn), (dct, v_dct))
        if carried:
            in_b += io.start((c_in[0], state), (c_in[1], total))
        else:
            state[...] = jnp.zeros_like(state)
            total[...] = jnp.zeros_like(total)
        in_c = io.start(*[(w.at[0], v_wqkv.at[:, pl.ds(i * e, e)]) for i, w in enumerate((wq, wk, wv))], (wup.at[0], v_wup), (place(h_in), v_h),
                        *[(norm, v_norms.at[i]) for i, norm in enumerate(norms)], (scales.at[0], v_scales))
        acc[...] = jnp.zeros_like(acc)
        acc_s[...] = jnp.zeros_like(acc_s)
        wait(in_a)
        out_s = io.start((v_g.at[rows_at(me, rows // 4)], own))

        def fold(x):
            return jnp.sum(x.reshape(x.shape[0] // 8, 8, x.shape[1]), axis=0)

        @pl.loop(0, 0 if opened else wides)
        def _(b):
            rb = rows_at(b, WIDE)
            g_b = v_g[rb]
            o_gup[rb] = (dot_nt(g_b, v_wdown[...]) * i_gp[rb].astype(F32)).astype(BF)
            mixes[rb] = dot_nt(g_b, v_wo[...]).astype(BF)
            for copy in outs_a(b):
                copy.start()

        wait(in_b)

        @pl.loop(0, blocks)
        def _(step):
            b = blocks - 1 - step
            rb = rows_at(b, BLOCK)
            g_num = (mixes[rb].astype(F32) * i_inv[rb]).astype(BF)
            high, low = split(g_num.astype(F32) * i_mf[rb])
            same_b = v_same[...].astype(BF)
            g_den = -(dot(high, same_b) + dot(low, same_b))
            gd_high, gd_low = split(g_den)
            q_feat = i_qf[rb]
            k_feat = i_kf[rb]
            value = i_v[rb]
            q_b = q_feat.astype(BF)
            k_b = k_feat.astype(BF)
            row = lax.broadcasted_iota(jnp.int32, (CHUNK, hc * CHUNK), 0)
            col = lax.broadcasted_iota(jnp.int32, (CHUNK, hc * CHUNK), 1) & (CHUNK - 1)
            causal = row >= col
            row_t = lax.broadcasted_iota(jnp.int32, (hc * CHUNK, CHUNK), 0) & (CHUNK - 1)
            col_t = lax.broadcasted_iota(jnp.int32, (hc * CHUNK, CHUNK), 1)
            causal_t = col_t >= row_t
            hm = v_heads[...]
            sel = hm * jnp.asarray(1.0 / hd, BF)
            gq_parts, gk_parts, gv_parts = [None] * count, [None] * count, [None] * count
            for c in reversed(range(count)):
                rc = slice(c * CHUNK, (c + 1) * CHUNK)
                at = b * count + c
                q_c, k_c, v_c, n_c, dh, dl = q_b[rc], k_b[rc], value[rc], g_num[rc], gd_high[rc], gd_low[rc]
                k_x = stack_heads(k_c, hm, hc)
                spread = jnp.concatenate([jnp.broadcast_to(g_den[rc, h * hd:h * hd + 1], (CHUNK, CHUNK)) for h in range(hc)], axis=1)
                grid = jnp.where(causal, dot_nt(n_c, stack_heads(v_c, hm, hc)) + spread, 0.0).astype(BF)
                grid_s = jnp.concatenate([grid[:, h * CHUNK:(h + 1) * CHUNK] for h in range(hc)], axis=0)
                scores_t = jnp.where(causal_t, dot_nt(k_x, q_c), 0.0).astype(BF)
                before = jnp.concatenate(split(i_st[at]), axis=1)
                gq_parts[c] = dot(grid, k_x) + dot_nt(jnp.concatenate([n_c, n_c], axis=1), before) + g_den[rc] * i_kt[at][0:1, :]
                after = jnp.concatenate(split(state[...]), axis=1)
                gk_parts[c] = dot_tn(grid_s, stack_heads(q_c, hm, hc)) + dot_nt(jnp.concatenate([v_c, v_c], axis=1), after) + total[0:1, :]
                gv_parts[c] = dot(lanes_of_heads(scores_t, hc), stack_heads(n_c, hm, hc)) + dot(k_c, after[:, :e])
                state[...] += dot_tn(q_c, n_c) * v_same[...]
                total[...] += jnp.sum(q_c.astype(F32) * g_den[rc], axis=0, keepdims=True)
            gc_q = jnp.concatenate(gq_parts, axis=0) * q_feat
            gc_k = jnp.concatenate(gk_parts, axis=0) * k_feat
            g_value = jnp.concatenate(gv_parts, axis=0)
            acc_s[...] += fold(gc_q + gc_k)
            cos_b = jnp.concatenate([jnp.concatenate([v_turn[0, rb]] * (hc // 2), axis=1)] * 2, axis=0)
            sin_b = jnp.concatenate([jnp.concatenate([v_turn[1, rb]] * (hc // 2), axis=1)] * 2, axis=0)
            turned = dot_nt(jnp.concatenate([gc_q, gc_k], axis=0).astype(BF), v_dct[0])
            g_qk = turned * cos_b - partner(turned, hd) * sin_b
            o_gqkv[rb] = jnp.concatenate([g_qk[:BLOCK], g_qk[BLOCK:], g_value], axis=1).astype(BF)
            for copy in outs_b(b):
                copy.start()

        out_s += io.start((state, c_st), (total, c_kt))
        wait(in_c)

        @pl.loop(0, blocks)
        def _(b):
            rb = rows_at(b, BLOCK)
            g_one = dot_nt(o_gqkv[rb], v_wqkv[...])
            g_two = dot_nt(o_gup[rb], v_wup[...])
            xhat, rstd = standardize(v_h[rb].astype(F32))
            acc[0] += fold(g_one * xhat)
            acc[1] += fold(g_one)
            acc[2] += fold(g_two * xhat)
            acc[3] += fold(g_two)
            acc[4] += fold(v_g[rb].astype(F32))
            inner = g_one * v_norms[0] + g_two * v_norms[2]
            mean_t = jnp.mean(inner, axis=-1, keepdims=True)
            mean_x = jnp.mean(inner * xhat, axis=-1, keepdims=True)
            o_part[rb] = (rstd * (inner - mean_t - xhat * mean_x)).astype(BF)
            for copy in outs_c(b):
                copy.start()

        for i in range(5):
            o_sums[i:i + 1, :] = jnp.sum(acc[i], axis=0, keepdims=True)
        o_sums[5:8, :] = jnp.zeros((3, d), F32)
        o_sums[5:6, :e] = jnp.sum(acc_s[...], axis=0, keepdims=True) / flat_scales(v_scales, hc)
        out_s += io.start((o_sums, sums))
        wait(out_s)

        @pl.loop(0, 0 if opened else wides)
        def _(b):
            wait(outs_a(b))

        @pl.loop(0, blocks)
        def _(b):
            wait(outs_b(b) + outs_c(b))


def like(shape, dtype):
    return jax.ShapeDtypeStruct(shape, dtype)


def forward_call(sizes, m, section, order, pieces, weights, tabs, store, span=None, carry=(), parts=(), ends=False, cotangent=None):
    rows, d, e, f, hc = sizes
    base, end = span or (0, rows)
    some = end - base
    share = rows // 4 if ends or some == rows else some // 4
    chunks = rows // CHUNK
    own = some // CHUNK
    shapes = [
        like((rows, d), BF), like((rows, d), BF), like((rows, f + e), BF), like((rows, f), BF),
        like((rows, e), F32), like((rows, e), F32), like((rows, e), BF), like((rows, e), F32),
        like((rows, e), F32), like((chunks, e, e), F32), like((chunks, 8, e), F32), like((rows, d), BF),
        like((some // 4, d), BF), like((e, e), F32), like((8, e), F32),
    ] + ([like((2, share, d), BF)] * 2 if section == 0 else [like((rows, e), BF)])
    through = list(store) + list(parts)
    operands = [order, *pieces, *weights, *tabs, *([] if section == 0 else [cotangent]), *carry, *through]
    scratch = [pltpu.VMEM(shape, dtype) for shape, dtype in (
        ((some, d), BF), ((d, 3 * e), BF), ((e, d), BF), ((d, f), BF), ((f, d), BF),
        ((4, 1, d), F32), ((hc, e // hc), F32), ((2, some, 2 * (e // hc)), F32), ((2, e, e), BF), ((hc * CHUNK, e), BF), ((e, e), F32),
        ((some, d), BF), ((some, d), BF), ((some, f + e), BF), ((some, f), BF),
        ((some, e), F32), ((some, e), F32), ((some, e), BF), ((some, e), F32),
        ((some, e), F32), ((own, e, e), F32), ((own, 8, e), F32), ((some, d), BF),
        ((e, e), F32), ((8, e), F32))]
    scratch += [pltpu.VMEM(tabs[-1].shape, jnp.int32), pltpu.VMEM((some, d), BF), pltpu.VMEM((some, e), BF), pltpu.SemaphoreType.DMA((32,)), pltpu.SemaphoreType.DMA((16, some // BLOCK))]
    cfg = {"m": m, "section": section, "pieces": len(pieces), "base": base, "share": share, "origin": base // share if ends else 0,
           "e": e, "f": f, "hc": hc, "carried": bool(carry), "alias": len(through), "branch": section == 0}
    first = len(operands) - len(through)
    results = pl.pallas_call(
        functools.partial(forward_kernel, cfg),
        out_shape=shapes,
        in_specs=[ANY] * len(operands),
        out_specs=[ANY] * len(shapes),
        scratch_shapes=scratch,
        input_output_aliases={first + i: i for i in range(len(through))},
        compiler_params=pltpu.CompilerParams(vmem_limit_bytes=VMEM_BYTES),
        cost_estimate=pl.CostEstimate(flops=2 * some * d * (4 * e + 2 * f), bytes_accessed=25 * 2 ** 20, transcendentals=some * (f + 2 * e)),
        name="forward",
    )(*operands)
    return list(results[:12]), results[12], list(results[15:])


def backward_call(sizes, m, section, order, g_in, h_in, weights, tabs, store, back, span=None, carry=(), opened=()):
    rows, d, e, f, hc = sizes
    base, end = span or (0, rows)
    some = end - base
    share = some // 4
    own = some // CHUNK
    shapes = [like((rows, f), BF)] * (not opened) + [like((rows, 3 * e), BF), like((2, share, d), BF), like((2, share, d), BF), like((some // 4, d), BF), like((8, d), F32), like((e, e), F32), like((8, e), F32)]
    operands = [order, *g_in, h_in, *weights, *tabs, *store[4:11], *opened, *carry, *back]
    scratch = [pltpu.VMEM(shape, dtype) for shape, dtype in (
        ((some, d), BF), ((some, d), BF), ((d, 3 * e), BF), ((e, d), BF), ((d, f), BF), ((f, d), BF),
        ((4, 1, d), F32), ((hc, e // hc), F32), ((2, some, 2 * (e // hc)), F32), ((2, e, e), BF), ((hc * CHUNK, e), BF), ((e, e), F32),
        ((some, f), BF), ((some, e), F32), ((some, e), F32), ((some, e), BF),
        ((some, e), F32), ((some, e), F32), ((own, e, e), F32), ((own, 8, e), F32),
        ((some, f), BF), ((some, 3 * e), BF), ((some, d), BF), ((8, d), F32),
        ((some, e), BF), ((5, 8, d), F32), ((8, e), F32), ((e, e), F32), ((8, e), F32))]
    scratch += [pltpu.SemaphoreType.DMA((40,)), pltpu.SemaphoreType.DMA((4, some // BLOCK))]
    cfg = {"m": m, "section": section, "base": base, "share": share, "e": e, "f": f, "hc": hc, "carried": bool(carry), "alias": len(back), "grads": len(g_in), "opened": bool(opened)}
    first = len(operands) - len(back)
    results = pl.pallas_call(
        functools.partial(backward_kernel, cfg),
        out_shape=shapes,
        in_specs=[ANY] * len(operands),
        out_specs=[ANY] * len(shapes),
        scratch_shapes=scratch,
        input_output_aliases={first + i: i for i in range(len(back))},
        compiler_params=pltpu.CompilerParams(vmem_limit_bytes=VMEM_BYTES),
        cost_estimate=pl.CostEstimate(flops=2 * some * d * (4 * e + 2 * f), bytes_accessed=30 * 2 ** 20, transcendentals=0),
        name="backward",
    )(*operands)
    head = 1 if opened else 2
    return list(results[:head]), list(results[head:head + 3]), results[head + 3], list(results[head + 4:])


def down_kernel(cfg, order, *refs):
    count, first, m = cfg["pieces"], cfg["first"], cfg["m"]
    refs = list(refs)

    def take(n):
        out = refs[:n]
        del refs[:n]
        return out

    pieces = take(count)
    (am,) = take(1)
    acc_in = take(0 if first else 1)
    take(cfg["alias"])
    outs = take(2 if count == 4 else 1)
    v_g, v_am, v_acc, v_out, sems, o_sems = refs
    rows, d = v_g.shape
    me = lax.axis_index("tensor")

    def tile(b):
        return rows_at(b, BLOCK)

    def sent(b):
        return pltpu.make_async_copy((v_acc if first else v_out).at[tile(b)], outs[0].at[tile(b)], o_sems.at[b])

    @pl.when(lax.axis_index("section") == cfg["section"])
    def _():
        io = Copies(sems)
        if count == 4:
            loads = io.start(*[(pieces[k], v_g.at[rows_at(me ^ k, rows // 4)]) for k in range(4)])
        else:
            loads = io.start((pieces[0].at[m, 0] if len(pieces[0].shape) == 4 else pieces[0], v_g))
        loads += io.start((am, v_am))
        if not first:
            loads += io.start((acc_in[0], v_acc))
        wait(loads)
        kept = io.start((v_g, outs[1])) if count == 4 else []

        @pl.loop(0, d // BLOCK)
        def _(b):
            product = dot_tn(v_g[:, tile(b)], v_am[...])
            if first:
                v_acc[tile(b)] = product.astype(BF)
            else:
                v_out[tile(b)] = (v_acc[tile(b)].astype(F32) + product).astype(BF)
            sent(b).start()

        wait(kept)

        @pl.loop(0, d // BLOCK)
        def _(b):
            sent(b).wait()


def branch_kernel(order, am, wo, wdown, keep, send, v_am, v_wo, v_wdown, o_part, sems, o_sems):
    rows, d = o_part.shape
    f = v_wdown.shape[0]
    share = rows // 4
    me = lax.axis_index("tensor")

    def outs(b):
        copies = []
        for i in range(WIDE // share):
            at = (b * (WIDE // share) + i) ^ me
            copies.append(Routed(o_part.at[rows_at(b * (WIDE // share) + i, share)], keep, send, at, o_sems.at[i, b]))
        return copies

    @pl.when(lax.axis_index("section") == 1)
    def _():
        wait(Copies(sems).start((am, v_am), (wo.at[0], v_wo), (wdown.at[0], v_wdown)))

        @pl.loop(0, rows // WIDE)
        def _(b):
            rb = rows_at(b, WIDE)
            o_part[rb] = (dot(v_am[rb, f:], v_wo[...]) + dot(v_am[rb, :f], v_wdown[...])).astype(BF)
            for copy in outs(b):
                copy.start()

        @pl.loop(0, rows // WIDE)
        def _(b):
            wait(outs(b))


def branch_call(order, am, w_out, w_down):
    rows, wide = am.shape
    _, f, d = w_down.shape
    return pl.pallas_call(
        branch_kernel,
        out_shape=[like((2, rows // 4, d), BF)] * 2,
        in_specs=[ANY] * 4,
        out_specs=[ANY] * 2,
        scratch_shapes=[pltpu.VMEM((rows, wide), BF), pltpu.VMEM((wide - f, d), BF), pltpu.VMEM((f, d), BF), pltpu.VMEM((rows, d), BF),
                        pltpu.SemaphoreType.DMA((3,)), pltpu.SemaphoreType.DMA((2, rows // WIDE))],
        compiler_params=pltpu.CompilerParams(vmem_limit_bytes=VMEM_BYTES),
        cost_estimate=pl.CostEstimate(flops=0, bytes_accessed=0, transcendentals=0),
        name="branch",
    )(order, am, w_out, w_down)


def arrange_kernel(order, *refs):
    pieces, (out, held, sems) = refs[:4], refs[4:]
    me = lax.axis_index("tensor")

    @pl.when(lax.axis_index("section") == 0)
    def _():
        io = Copies(sems)
        wait(io.start(*[(pieces[k], held.at[rows_at(me ^ k, pieces[k].shape[0])]) for k in range(4)]))
        wait(io.start((held, out)))


def arrange_call(order, pieces):
    share, d = pieces[0].shape
    return pl.pallas_call(
        arrange_kernel,
        out_shape=[like((4 * share, d), BF)],
        in_specs=[ANY] * 5,
        out_specs=[ANY],
        scratch_shapes=[pltpu.VMEM((4 * share, d), BF), pltpu.SemaphoreType.DMA((5,))],
        cost_estimate=pl.CostEstimate(flops=0, bytes_accessed=0, transcendentals=0),
        name="arrange",
    )(order, *pieces)


def unpack_kernel(packed, *outs):
    at = 0
    for out in outs:
        out[0] = packed[:, at:at + out.shape[2]].astype(F32)
        at += out.shape[2]


def unpack_call(packed, widths):
    rows = packed.shape[0]
    whole = pl.BlockSpec(memory_space=pltpu.VMEM)
    return pl.pallas_call(
        unpack_kernel,
        out_shape=[like((1, rows, width), F32) for width in widths],
        in_specs=[whole],
        out_specs=[whole] * len(widths),
        name="unpack",
    )(packed)


def down_call(m, section, order, pieces, am, acc=None, through=None):
    rows, wide = am.shape
    d = pieces[0].shape[-1]
    first = acc is None
    operands = [order, *pieces, am] + ([] if first else [acc]) + ([] if through is None else [through])
    cfg = {"pieces": len(pieces), "first": first, "section": section, "m": m, "alias": int(through is not None)}
    shapes = [like((d, wide), BF)] + [like((rows, d), BF)] * (len(pieces) == 4)
    return pl.pallas_call(
        functools.partial(down_kernel, cfg),
        out_shape=shapes,
        in_specs=[ANY] * len(operands),
        out_specs=[ANY] * len(shapes),
        scratch_shapes=[pltpu.VMEM((rows, d), BF), pltpu.VMEM((rows, wide), BF), pltpu.VMEM((d, wide), BF), pltpu.VMEM((d, wide), BF),
                        pltpu.SemaphoreType.DMA((len(pieces) + 5,)), pltpu.SemaphoreType.DMA((d // BLOCK,))],
        input_output_aliases={} if through is None else {len(operands) - 1: 0},
        compiler_params=pltpu.CompilerParams(vmem_limit_bytes=VMEM_BYTES),
        cost_estimate=pl.CostEstimate(flops=0 if first else 2 * rows * d * wide, bytes_accessed=0 if first else 12 * 2 ** 20, transcendentals=0),
        name="down",
    )(*operands)


def body(tokens, cotangent, lengths, attn_gain, attn_bias, ffn_gain, ffn_bias, w_query, w_key, w_value, w_out, feat_scale, w_up, w_down, down_bias):
    section = lax.axis_index("section")
    tensor = lax.axis_index("tensor")
    teams = lax.axis_size("tensor")
    micro, _, rows, d = tokens.shape
    hc, hd = feat_scale.shape[1:]
    e = hc * hd
    f = w_up.shape[2]
    sizes = (rows, d, e, f, hc)
    whole, early, late = (0, rows), (0, rows // 2), (rows // 2, rows)
    made = host_tables(rows, hc, hd)
    tabs = [attn_gain, attn_bias, ffn_gain, ffn_bias, feat_scale] + [jnp.asarray(made[k]) for k in ("turn", "dct", "heads", "same")] + [lengths]
    weights = [w_query, w_key, w_value, w_out, w_up, w_down]
    both = ("section", "tensor")
    order = attn_gain

    def swap(x, sec, bit):
        sections = range(2) if sec is None else (sec,)
        return lax.ppermute(x, both, [(k * teams + i, k * teams + (i ^ bit)) for k in sections for i in range(teams)])

    def hand(x, source):
        return lax.ppermute(x, "section", [(source, 1 - source)])

    def gather_rows(own, sec):
        far = swap(own, sec, 2)
        return [own, swap(own, sec, 1), far, swap(far, sec, 1)]

    def tie(x, *after):
        return lax.optimization_barrier((x, *after))[0]

    def tie_all(*values):
        return lax.optimization_barrier(values)

    def near_sum(parts, sec):
        keep, send = parts
        got = swap(send, sec, 1)
        return keep[0].astype(F32) + got[0].astype(F32), (keep[1].astype(F32) + got[1].astype(F32)).astype(BF)

    def relay(parts, source):
        near, sent = near_sum(parts, source)
        near = (near + down_bias[0] if source == 0 else near).astype(BF)
        pairs = [[(source * teams + i, (1 - source) * teams + (i ^ bit)) for i in range(teams)] for bit in (0, 2)]
        return [lax.ppermute(near, both, pairs[0]), lax.ppermute(sent, both, pairs[1])], (near, sent)

    def own_rows(x):
        return lax.dynamic_index_in_dim(x.reshape(teams, rows // teams, d), tensor, 0, keepdims=False)

    def whole_rows(own):
        return lax.all_gather(own, "tensor", axis=0, tiled=True)

    def summed(start, took):
        return start.astype(F32) + took[0].astype(F32) + took[1].astype(F32)

    def all_sum(x, axis):
        size, bit = lax.axis_size(axis), 1
        if size & (size - 1):
            return lax.psum(x, axis)
        while bit < size:
            x = x + lax.ppermute(x, axis, [(i, i ^ bit) for i in range(size)])
            bit *= 2
        return x

    def weight_grad(pairs):
        return sum(dot_tn(left, right) for left, right in pairs)

    def scatter(total):
        return lax.psum_scatter(total, "dp", scatter_dimension=0, tiled=True)

    def forward(m, sec, after, pieces, store, **more):
        return forward_call(sizes, m, sec, tie(order, after), pieces, weights, tabs, store, **more)

    def backward(m, sec, after, g_in, h_in, store, back, **more):
        return backward_call(sizes, m, sec, tie(order, after), g_in, h_in, weights, tabs, store, back, **more)

    store_0, _, parts = forward_call(sizes, 0, 0, order, [tokens], weights, tabs, [])
    took, after = relay(parts, 0)
    store_1, _, parts = forward_call(sizes, 1, 0, tie(order, *after), [tokens], weights, tabs, [])
    own_t, *took, parts[0], parts[1] = tie_all(own_rows(tokens[0, 0]), *took, *parts)
    row_0 = summed(own_t, took).astype(BF)
    far_rows = swap(row_0, 1, 2)
    took, after = relay(parts, 0)
    near_rows = swap(tie(row_0, *after), 1, 1)
    far_rows, near_rows = tie_all(far_rows, near_rows)
    store_0, own_0, mix_0 = forward_call(sizes, 0, 1, tie(order, *after), [row_0, near_rows, far_rows, swap(far_rows, 1, 1)], weights, tabs, store_0, cotangent=cotangent)
    own_c = [own_rows(cotangent[m, 0]) for m in range(2)]
    *took, own_0, own_t, own_c[0], own_c[1] = tie_all(*took, own_0, own_rows(tokens[1, 0]), *own_c)
    row_1 = summed(own_t, took).astype(BF)
    rows_1 = whole_rows(row_1)
    back_0, parts, sums_0, _ = backward(0, 1, row_1, [cotangent], store_0[11], store_0, [], opened=[store_0[3], *mix_0])
    took_0, after = relay(parts[:2], 1)
    rows_1 = tie(rows_1, *after)
    store_1, own_1, mix_1 = forward_call(sizes, 1, 1, tie(order, *after), [rows_1], weights, tabs, store_1, cotangent=cotangent)
    *took_0, own_1 = tie_all(*took_0, own_1)
    grad_0 = summed(own_c[0], took_0).astype(BF)
    gb_0 = whole_rows(grad_0)
    back_1, parts, sums_1, _ = backward(1, 1, grad_0, [cotangent], store_1[11], store_1, [], opened=[store_1[3], *mix_1])
    took_1, after = relay(parts[:2], 1)
    gb_0, after = tie_all(gb_0, tie(order, *after))
    ends_0 = [*branch_call(after, store_0[2], w_out, w_down), own_0]
    ends_1 = [*branch_call(after, store_1[2], w_out, w_down), own_1]
    back_0, ends_0, sums_0, _ = backward(0, 0, gb_0, [gb_0], tokens, store_0, [store_0[3], *back_0, *ends_0, sums_0])
    *took_1, ends_0[0] = tie_all(*took_1, ends_0[0])
    grad_1 = summed(own_c[1], took_1).astype(BF)
    far_rows = swap(grad_1, 0, 2)
    (acc,) = down_call(0, 0, tie(order, grad_1), [gb_0], store_0[2])
    near_rows = swap(grad_1, 0, 1)
    (acc_b,) = down_call(0, 1, tie(order, acc), [cotangent], store_0[2])
    (down_sum,) = down_call(1, 1, order, [cotangent], store_1[2], acc_b)
    far_rows, near_rows, down_sum = tie_all(far_rows, near_rows, down_sum)
    down_sum, gb_1 = down_call(1, 0, order, [grad_1, near_rows, far_rows, swap(far_rows, 0, 1)], store_1[2], acc, down_sum)
    down = scatter(down_sum)
    back_1, ends_1, sums_1, _ = backward(1, 0, down_sum, [gb_1], tokens, store_1, [store_1[3], *back_1, *ends_1, sums_1])
    rest_sum = jnp.concatenate([
        weight_grad([(store_0[1], back_0[0]), (store_1[1], back_1[0])]).astype(BF),
        weight_grad([(store_0[0], back_0[1]), (store_1[0], back_1[1])]).astype(BF)], axis=1)
    down, rest_sum = tie_all(down, rest_sum)
    rest = scatter(rest_sum)
    up, query, key, value = unpack_call(rest, (f, e, e, e))
    shift = jnp.where(section == 0, 0.0, down_bias[0])
    ends = []
    for parts in (ends_0, ends_1):
        keep, send, own, _ = tie_all(*parts, rest_sum)
        near, sent = near_sum((keep, send), None)
        ends.append(own.astype(F32) + near + swap(sent, None, 2).astype(F32) + shift)
    ends = jnp.stack(ends)[None, :, None]
    down = down.astype(F32).T
    small = all_sum(sums_0 + sums_1, "dp")
    group = lax.axis_size("dp")
    place = lax.axis_index("dp")
    cut = all_sum(lax.dynamic_slice(small, (0, place * (d // group)), (5, d // group)), "tensor")
    scale_cut = lax.dynamic_slice(small[5, :e].reshape(hc, hd), (0, place * (hd // group)), (hc, hd // group))
    return (
        ends, cut[0:1], cut[1:2], cut[2:3], cut[3:4],
        query, key, value, down[None, f:], scale_cut[None], up, down[None, :f],
        cut[4:5] / teams,
    )


def solution(mesh):
    return jax.shard_map(
        body,
        mesh=mesh,
        in_specs=(
            P(None, "dp", None, None), P(None, "dp", None, None), P(None, "dp"),
            P("section", None), P("section", None), P("section", None), P("section", None),
            P("section", None, "tensor"), P("section", None, "tensor"), P("section", None, "tensor"),
            P("section", "tensor", None), P("section", "tensor", None), P("section", None, "tensor"),
            P("section", "tensor", None), P("section", None),
        ),
        out_specs=(
            P("section", None, "dp", "tensor", None),
            P("section", "dp"), P("section", "dp"), P("section", "dp"), P("section", "dp"),
            P("section", "dp", "tensor"), P("section", "dp", "tensor"), P("section", "dp", "tensor"),
            P("section", "tensor", "dp"), P("section", "tensor", "dp"), P("section", "dp", "tensor"),
            P("section", "tensor", "dp"), P("section", "dp"),
        ),
        check_vma=False,
    )
```

```python
import functools
import math

import jax
import jax.numpy as jnp
import numpy as np
from jax import lax
from jax.experimental import pallas as pl
from jax.experimental.pallas import tpu as pltpu
from jax.sharding import PartitionSpec as P

ROT = 16
EPSILON = 1e-05
BLOCK = 512
CHUNK = 128
WIDE = 512
BF = jnp.bfloat16
F32 = jnp.float32
VMEM_BYTES = 60 * 1024 * 1024
ANY = pl.BlockSpec(memory_space=pl.ANY)


def host_tables(slot_rows, head_count, head_size):
    width = head_count * head_size
    halfway = ROT // 2
    column = np.arange(2 * head_size) % head_size
    pair = np.where(column < halfway, column, column - halfway)
    inverse = np.exp(pair * (-2.0 * math.log(10000.0) / ROT))
    angles = np.arange(slot_rows)[:, None] * inverse[None, :]
    turned = (column < 2 * halfway)[None, :]
    sign = np.where(column < halfway, -1.0, 1.0)[None, :]
    cos_full = np.where(turned, np.cos(angles), 1.0)
    sin_full = np.where(turned, sign * np.sin(angles), 0.0)
    order = np.arange(head_size)
    table = np.cos(np.pi * (order[None, :] + 0.5) * order[:, None] / head_size) * np.sqrt(2.0 / head_size)
    table = np.where(order[:, None] == 0, table * np.sqrt(0.5), table)
    dct = np.kron(np.eye(head_count), table.T)
    high = dct.astype(np.float32).astype(BF)
    low = (dct - high.astype(np.float64)).astype(np.float32).astype(BF)
    lane_head = np.arange(width) // head_size
    heads = (np.arange(head_count)[:, None] == lane_head[None, :]).astype(np.float32)
    same = (lane_head[:, None] == lane_head[None, :]).astype(np.float32)
    return {
        "turn": np.stack([cos_full, sin_full]).astype(np.float32),
        "dct": np.stack([high, low]),
        "heads": np.repeat(heads, CHUNK, axis=0).astype(BF),
        "same": same.astype(np.float32),
    }


def dot(a, b):
    return jnp.dot(a, b, preferred_element_type=F32)


def dot_nt(a, b):
    return lax.dot_general(a, b, (((1,), (1,)), ((), ())), preferred_element_type=F32)


def dot_tn(a, b):
    return lax.dot_general(a, b, (((0,), (0,)), ((), ())), preferred_element_type=F32)


def split(x):
    high = x.astype(BF)
    return high, (x - high.astype(F32)).astype(BF)


def stack_heads(x, heads, head_count):
    return jnp.concatenate([x] * head_count, axis=0) * heads


def lanes_of_heads(x, head_count):
    rows = x.shape[0] // head_count
    return jnp.concatenate([x[h * rows:(h + 1) * rows] for h in range(head_count)], axis=1)


def gelu_parts(u):
    cdf = 0.5 + 0.5 * lax.erf(u * (1.0 / math.sqrt(2.0)))
    return u * cdf, cdf + u * (jnp.exp(-0.5 * u * u) * (1.0 / math.sqrt(2.0 * math.pi)))


def partner(x, head_size):
    half = ROT // 2
    lane = lax.broadcasted_iota(jnp.int32, x.shape, 1) & (head_size - 1)
    return jnp.where(lane < half, pltpu.roll(x, x.shape[1] - half, 1), pltpu.roll(x, half, 1))


def standardize(hidden):
    center = hidden - jnp.mean(hidden, axis=-1, keepdims=True)
    spread = jnp.mean(center * center, axis=-1, keepdims=True)
    rstd = lax.rsqrt(spread + EPSILON)
    return center * rstd, rstd


def rows_at(b, size, base=0):
    return pl.ds(pl.multiple_of(b * size + base, size), size)


def flat_scales(ref, head_count):
    return jnp.concatenate([ref[h:h + 1, :] for h in range(head_count)], axis=1)


class Routed:
    def __init__(self, src, keep, send, at, sem):
        self.near = pltpu.make_async_copy(src, keep.at[at >> 1], sem)
        self.far = pltpu.make_async_copy(src, send.at[at >> 1], sem)
        self.at = at

    def start(self):
        @pl.when((self.at & 1) == 0)
        def _():
            self.near.start()

        @pl.when((self.at & 1) != 0)
        def _():
            self.far.start()

    def wait(self):
        self.near.wait()


class Copies:
    def __init__(self, sems):
        self.sems = sems
        self.used = 0

    def start(self, *pairs):
        made = []
        for src, dst in pairs:
            copy = pltpu.make_async_copy(src, dst, self.sems.at[self.used])
            self.used += 1
            copy.start()
            made.append(copy)
        return made


def wait(copies):
    for copy in copies:
        copy.wait()


def looped_out(pairs, sems, first, b):
    return [pltpu.make_async_copy(src, dst, sems.at[first + i, b]) for i, (src, dst) in enumerate(pairs)]


def forward_kernel(cfg, order, *refs):
    pieces, base, share, origin, e, f, hc = (cfg[k] for k in ("pieces", "base", "share", "origin", "e", "f", "hc"))
    hd = e // hc
    carried = cfg["carried"]
    refs = list(refs)

    def take(n):
        out = refs[:n]
        del refs[:n]
        return out

    h_in = take(pieces)
    wq, wk, wv, wo, wup, wdown, *norms, scales, turn, dct, heads, same, lengths = take(16)
    cotangent = None if cfg["branch"] else take(1)[0]
    c_in = take(2 if carried else 0)
    take(cfg["alias"])
    s_n1, s_n2, s_am, s_gp, s_qf, s_kf, s_v, s_mf, s_inv, s_st, s_kt, s_h, own, c_st, c_kt = take(15)
    keep, send = take(2) if cfg["branch"] else (None, None)
    s_mix = None if cfg["branch"] else take(1)[0]
    (v_h, v_wqkv, v_wo, v_wup, v_wdown, v_norms, v_scales, v_turn, v_dct, v_heads, v_same,
     o_n1, o_n2, o_am, o_gp, o_qf, o_kf, o_v, o_mf, o_inv, o_st, o_kt, o_part, state, total, v_len, v_g, o_mix, sems, o_sems) = refs
    rows = v_h.shape[0]
    blocks = rows // BLOCK
    wides = rows // WIDE
    count = BLOCK // CHUNK
    me = lax.axis_index("tensor")

    def outs_a(b):
        rb, ro = rows_at(b, BLOCK), rows_at(b, BLOCK, base)
        return looped_out([(o_n1.at[rb], s_n1.at[ro]), (o_n2.at[rb], s_n2.at[ro])], o_sems, 0, b)

    def outs_b(b):
        rb, ro = rows_at(b, BLOCK), rows_at(b, BLOCK, base)
        cb, co = pl.ds(b * count, count), pl.ds(b * count + base // CHUNK, count)
        return looped_out([(o.at[rb], s.at[ro]) for o, s in ((o_qf, s_qf), (o_kf, s_kf), (o_v, s_v), (o_mf, s_mf), (o_inv, s_inv))]
                          + [(o_st.at[cb], s_st.at[co]), (o_kt.at[cb], s_kt.at[co])], o_sems, 2, b)

    def outs_c(b):
        rb, ro = rows_at(b, WIDE), rows_at(b, WIDE, base)
        copies = looped_out([(o_am.at[rb], s_am.at[ro]), (o_gp.at[rb], s_gp.at[ro])] + ([] if cfg["branch"] else [(o_mix.at[rb], s_mix.at[ro])]), o_sems, 9, b)
        for i in range(WIDE // share if cfg["branch"] else 0):
            at = (b * (WIDE // share) + i + origin) ^ me
            copies.append(Routed(o_part.at[rows_at(b * (WIDE // share) + i, share)], keep, send, at, o_sems.at[11 + i, b]))
        return copies

    @pl.when(lax.axis_index("section") == cfg["section"])
    def _():
        io = Copies(sems)
        if pieces == 1:
            in_h = io.start((h_in[0].at[cfg["m"], 0, pl.ds(base, rows)] if len(h_in[0].shape) == 4 else h_in[0], v_h))
        else:
            halves = pieces // 4
            in_h = io.start(*[(h_in[h * 4 + k], v_h.at[rows_at((me ^ k) * halves + h, rows // pieces)]) for h in range(halves) for k in range(4)])
        in_h += io.start(*[(norm, v_norms.at[i]) for i, norm in enumerate(norms)], (scales.at[0], v_scales))
        in_b = io.start(*[(w.at[0], v_wqkv.at[:, pl.ds(i * e, e)]) for i, w in enumerate((wq, wk, wv))], (turn.at[:, pl.ds(base, rows)], v_turn),
                        (dct, v_dct), (heads, v_heads), (same, v_same), (lengths, v_len))
        if carried:
            in_b += io.start((c_in[0], state), (c_in[1], total))
        else:
            state[...] = jnp.zeros_like(state)
            total[...] = jnp.zeros_like(total)
        in_c = io.start((wup.at[0], v_wup), (wo.at[0], v_wo), (wdown.at[0], v_wdown),
                        *([] if cfg["branch"] else [(cotangent.at[cfg["m"], 0], v_g)]))
        wait(in_h)
        out_h = io.start(*([(v_h, s_h.at[pl.ds(base, rows)])] if cfg["section"] else []), (v_h.at[rows_at(me, rows // 4)], own))

        @pl.loop(0, blocks)
        def _(b):
            rb = rows_at(b, BLOCK)
            xhat, _ = standardize(v_h[rb].astype(F32))
            o_n1[rb] = (xhat * v_norms[0] + v_norms[1]).astype(BF)
            o_n2[rb] = (xhat * v_norms[2] + v_norms[3]).astype(BF)
            for copy in outs_a(b):
                copy.start()

        wait(in_b)

        @pl.loop(0, blocks)
        def _(b):
            rb = rows_at(b, BLOCK)
            qkv = dot(o_n1[rb], v_wqkv[...])
            cos_b = jnp.concatenate([jnp.concatenate([v_turn[0, rb]] * (hc // 2), axis=1)] * 2, axis=0)
            sin_b = jnp.concatenate([jnp.concatenate([v_turn[1, rb]] * (hc // 2), axis=1)] * 2, axis=0)
            pair = jnp.concatenate([qkv[:, :e], qkv[:, e:2 * e]], axis=0)
            high, low = split(pair * cos_b + partner(pair, hd) * sin_b)
            feats = flat_scales(v_scales, hc) * jnp.exp(dot(high, v_dct[0]) + dot(low, v_dct[0]) + dot(high, v_dct[1]))
            q_feat = feats[:BLOCK]
            slot = lax.broadcasted_iota(jnp.int32, (BLOCK, e), 0) + (b * BLOCK + base)
            k_feat = jnp.where(slot < v_len[cfg["m"]:cfg["m"] + 1, :], feats[BLOCK:], 0.0)
            value = qkv[:, 2 * e:].astype(BF)
            o_qf[rb] = q_feat
            o_kf[rb] = k_feat
            o_v[rb] = value
            q_b = q_feat.astype(BF)
            k_b = k_feat.astype(BF)
            row = lax.broadcasted_iota(jnp.int32, (CHUNK, hc * CHUNK), 0)
            col = lax.broadcasted_iota(jnp.int32, (CHUNK, hc * CHUNK), 1) & (CHUNK - 1)
            causal = row >= col
            for c in range(count):
                rc = slice(c * CHUNK, (c + 1) * CHUNK)
                at = b * count + c
                q_c, k_c, v_c = q_b[rc], k_b[rc], value[rc]
                o_st[at] = state[...]
                o_kt[at] = total[...]
                weighted = (q_c.astype(F32) * total[0:1, :]).astype(BF)
                scores = jnp.where(causal, dot_nt(q_c, stack_heads(k_c, v_heads[...], hc)), 0.0).astype(BF)
                both = dot(scores, jnp.concatenate([stack_heads(v_c, v_heads[...], hc), v_heads[...]], axis=1))
                inverse = 1.0 / (both[:, e:] + dot(weighted, v_same[...].astype(BF)))
                mixed = (both[:, :e] + dot(q_c, state[...].astype(BF))) * inverse
                rg = rows_at(at, CHUNK)
                o_inv[rg] = inverse
                o_mf[rg] = mixed
                o_am[rg, f:] = mixed.astype(BF)
                state[...] += dot_tn(k_c, v_c) * v_same[...]
                total[...] += jnp.sum(k_c.astype(F32), axis=0, keepdims=True)
            for copy in outs_b(b):
                copy.start()

        out_s = io.start((state, c_st), (total, c_kt))
        wait(in_c)

        @pl.loop(0, wides)
        def _(b):
            rb = rows_at(b, WIDE)
            act, slope = gelu_parts(dot(o_n2[rb], v_wup[...]))
            o_am[rb, :f] = act.astype(BF)
            if not cfg["branch"]:
                slope = slope * dot_nt(v_g[rb], v_wdown[...])
                o_mix[rb] = dot_nt(v_g[rb], v_wo[...]).astype(BF)
            o_gp[rb] = slope.astype(BF)
            if cfg["branch"]:
                o_part[rb] = (dot(o_am[rb, f:], v_wo[...]) + dot(o_am[rb, :f], v_wdown[...])).astype(BF)
            for copy in outs_c(b):
                copy.start()

        wait(out_h + out_s)

        @pl.loop(0, blocks)
        def _(b):
            wait(outs_a(b) + outs_b(b))

        @pl.loop(0, wides)
        def _(b):
            wait(outs_c(b))


def backward_kernel(cfg, order, *refs):
    base, share, e, f, hc = (cfg[k] for k in ("base", "share", "e", "f", "hc"))
    hd = e // hc
    carried = cfg["carried"]
    refs = list(refs)

    def take(n):
        out = refs[:n]
        del refs[:n]
        return out

    g_in = take(cfg["grads"])
    h_in, wq, wk, wv, wo, wup, wdown, *norms, scales, turn, dct, heads, same, _ = take(17)
    s_qf, s_kf, s_v, s_mf, s_inv, s_st, s_kt = take(7)
    opened = cfg["opened"]
    (in_gup, in_mix) = take(2) if opened else (None, None)
    c_in = take(2 if carried else 0)
    s_gp = take(cfg["alias"])[0] if not opened else None
    s_gup = take(1)[0] if not opened else None
    s_gqkv, keep, send, own, sums, c_st, c_kt = take(7)
    (v_g, v_h, v_wqkv, v_wo, v_wup, v_wdown, v_norms, v_scales, v_turn, v_dct, v_heads, v_same,
     i_gp, i_qf, i_kf, i_v, i_mf, i_inv, i_st, i_kt,
     o_gup, o_gqkv, o_part, o_sums, mixes, acc, acc_s, state, total, sems, o_sems) = refs
    rows, d = v_h.shape
    blocks = rows // BLOCK
    wides = rows // WIDE
    chunks = rows // CHUNK
    count = BLOCK // CHUNK
    me = lax.axis_index("tensor")

    def place(x):
        return x.at[cfg["m"], 0, pl.ds(base, rows)] if len(x.shape) == 4 else x.at[pl.ds(base, rows)]

    def outs_a(b):
        rb, ro = rows_at(b, WIDE), rows_at(b, WIDE, base)
        return [] if opened else looped_out([(o_gup.at[rb], s_gup.at[ro])], o_sems, 0, b)

    def outs_b(b):
        rb, ro = rows_at(b, BLOCK), rows_at(b, BLOCK, base)
        return looped_out([(o_gqkv.at[rb], s_gqkv.at[ro])], o_sems, 1, b)

    def outs_c(b):
        copies = []
        for i in range(BLOCK // share):
            at = (b * (BLOCK // share) + i) ^ me
            copies.append(Routed(o_part.at[rows_at(b * (BLOCK // share) + i, share)], keep, send, at, o_sems.at[2 + i, b]))
        return copies

    @pl.when(lax.axis_index("section") == cfg["section"])
    def _():
        io = Copies(sems)
        some = pl.ds(base, rows)
        some_chunks = pl.ds(base // CHUNK, chunks)
        in_g = [(place(g_in[0]), v_g)] if len(g_in) == 1 else [(g, v_g.at[pl.ds(i * g.shape[0], g.shape[0])]) for i, g in enumerate(g_in)]
        in_a = io.start(*in_g, *([(in_gup.at[some], o_gup), (in_mix.at[some], mixes)] if opened else
                                [(wdown.at[0], v_wdown), (wo.at[0], v_wo), (s_gp.at[some], i_gp)]))
        in_b = io.start((s_mf.at[some], i_mf), (s_inv.at[some], i_inv), (s_qf.at[some], i_qf), (s_kf.at[some], i_kf), (s_v.at[some], i_v),
                        (s_st.at[some_chunks], i_st), (s_kt.at[some_chunks], i_kt), (heads, v_heads), (same, v_same),
                        (turn.at[:, some], v_turn), (dct, v_dct))
        if carried:
            in_b += io.start((c_in[0], state), (c_in[1], total))
        else:
            state[...] = jnp.zeros_like(state)
            total[...] = jnp.zeros_like(total)
        in_c = io.start(*[(w.at[0], v_wqkv.at[:, pl.ds(i * e, e)]) for i, w in enumerate((wq, wk, wv))], (wup.at[0], v_wup), (place(h_in), v_h),
                        *[(norm, v_norms.at[i]) for i, norm in enumerate(norms)], (scales.at[0], v_scales))
        acc[...] = jnp.zeros_like(acc)
        acc_s[...] = jnp.zeros_like(acc_s)
        wait(in_a)
        out_s = io.start((v_g.at[rows_at(me, rows // 4)], own))

        def fold(x):
            return jnp.sum(x.reshape(x.shape[0] // 8, 8, x.shape[1]), axis=0)

        @pl.loop(0, 0 if opened else wides)
        def _(b):
            rb = rows_at(b, WIDE)
            g_b = v_g[rb]
            o_gup[rb] = (dot_nt(g_b, v_wdown[...]) * i_gp[rb].astype(F32)).astype(BF)
            mixes[rb] = dot_nt(g_b, v_wo[...]).astype(BF)
            for copy in outs_a(b):
                copy.start()

        wait(in_b)

        @pl.loop(0, blocks)
        def _(step):
            b = blocks - 1 - step
            rb = rows_at(b, BLOCK)
            g_num = (mixes[rb].astype(F32) * i_inv[rb]).astype(BF)
            high, low = split(g_num.astype(F32) * i_mf[rb])
            same_b = v_same[...].astype(BF)
            g_den = -(dot(high, same_b) + dot(low, same_b))
            gd_high, gd_low = split(g_den)
            q_feat = i_qf[rb]
            k_feat = i_kf[rb]
            value = i_v[rb]
            q_b = q_feat.astype(BF)
            k_b = k_feat.astype(BF)
            row = lax.broadcasted_iota(jnp.int32, (CHUNK, hc * CHUNK), 0)
            col = lax.broadcasted_iota(jnp.int32, (CHUNK, hc * CHUNK), 1) & (CHUNK - 1)
            causal = row >= col
            row_t = lax.broadcasted_iota(jnp.int32, (hc * CHUNK, CHUNK), 0) & (CHUNK - 1)
            col_t = lax.broadcasted_iota(jnp.int32, (hc * CHUNK, CHUNK), 1)
            causal_t = col_t >= row_t
            hm = v_heads[...]
            sel = hm * jnp.asarray(1.0 / hd, BF)
            gq_parts, gk_parts, gv_parts = [None] * count, [None] * count, [None] * count
            for c in reversed(range(count)):
                rc = slice(c * CHUNK, (c + 1) * CHUNK)
                at = b * count + c
                q_c, k_c, v_c, n_c, dh, dl = q_b[rc], k_b[rc], value[rc], g_num[rc], gd_high[rc], gd_low[rc]
                k_x = stack_heads(k_c, hm, hc)
                spread = jnp.concatenate([jnp.broadcast_to(g_den[rc, h * hd:h * hd + 1], (CHUNK, CHUNK)) for h in range(hc)], axis=1)
                grid = jnp.where(causal, dot_nt(n_c, stack_heads(v_c, hm, hc)) + spread, 0.0).astype(BF)
                grid_s = jnp.concatenate([grid[:, h * CHUNK:(h + 1) * CHUNK] for h in range(hc)], axis=0)
                scores_t = jnp.where(causal_t, dot_nt(k_x, q_c), 0.0).astype(BF)
                before = jnp.concatenate(split(i_st[at]), axis=1)
                gq_parts[c] = dot(grid, k_x) + dot_nt(jnp.concatenate([n_c, n_c], axis=1), before) + g_den[rc] * i_kt[at][0:1, :]
                after = jnp.concatenate(split(state[...]), axis=1)
                gk_parts[c] = dot_tn(grid_s, stack_heads(q_c, hm, hc)) + dot_nt(jnp.concatenate([v_c, v_c], axis=1), after) + total[0:1, :]
                gv_parts[c] = dot(lanes_of_heads(scores_t, hc), stack_heads(n_c, hm, hc)) + dot(k_c, after[:, :e])
                state[...] += dot_tn(q_c, n_c) * v_same[...]
                total[...] += jnp.sum(q_c.astype(F32) * g_den[rc], axis=0, keepdims=True)
            gc_q = jnp.concatenate(gq_parts, axis=0) * q_feat
            gc_k = jnp.concatenate(gk_parts, axis=0) * k_feat
            g_value = jnp.concatenate(gv_parts, axis=0)
            acc_s[...] += fold(gc_q + gc_k)
            cos_b = jnp.concatenate([jnp.concatenate([v_turn[0, rb]] * (hc // 2), axis=1)] * 2, axis=0)
            sin_b = jnp.concatenate([jnp.concatenate([v_turn[1, rb]] * (hc // 2), axis=1)] * 2, axis=0)
            turned = dot_nt(jnp.concatenate([gc_q, gc_k], axis=0).astype(BF), v_dct[0])
            g_qk = turned * cos_b - partner(turned, hd) * sin_b
            o_gqkv[rb] = jnp.concatenate([g_qk[:BLOCK], g_qk[BLOCK:], g_value], axis=1).astype(BF)
            for copy in outs_b(b):
                copy.start()

        out_s += io.start((state, c_st), (total, c_kt))
        wait(in_c)

        @pl.loop(0, blocks)
        def _(b):
            rb = rows_at(b, BLOCK)
            g_one = dot_nt(o_gqkv[rb], v_wqkv[...])
            g_two = dot_nt(o_gup[rb], v_wup[...])
            xhat, rstd = standardize(v_h[rb].astype(F32))
            acc[0] += fold(g_one * xhat)
            acc[1] += fold(g_one)
            acc[2] += fold(g_two * xhat)
            acc[3] += fold(g_two)
            acc[4] += fold(v_g[rb].astype(F32))
            inner = g_one * v_norms[0] + g_two * v_norms[2]
            mean_t = jnp.mean(inner, axis=-1, keepdims=True)
            mean_x = jnp.mean(inner * xhat, axis=-1, keepdims=True)
            o_part[rb] = (rstd * (inner - mean_t - xhat * mean_x)).astype(BF)
            for copy in outs_c(b):
                copy.start()

        for i in range(5):
            o_sums[i:i + 1, :] = jnp.sum(acc[i], axis=0, keepdims=True)
        o_sums[5:8, :] = jnp.zeros((3, d), F32)
        o_sums[5:6, :e] = jnp.sum(acc_s[...], axis=0, keepdims=True) / flat_scales(v_scales, hc)
        out_s += io.start((o_sums, sums))
        wait(out_s)

        @pl.loop(0, 0 if opened else wides)
        def _(b):
            wait(outs_a(b))

        @pl.loop(0, blocks)
        def _(b):
            wait(outs_b(b) + outs_c(b))


def like(shape, dtype):
    return jax.ShapeDtypeStruct(shape, dtype)


def forward_call(sizes, m, section, order, pieces, weights, tabs, store, span=None, carry=(), parts=(), ends=False, cotangent=None):
    rows, d, e, f, hc = sizes
    base, end = span or (0, rows)
    some = end - base
    share = rows // 4 if ends or some == rows else some // 4
    chunks = rows // CHUNK
    own = some // CHUNK
    shapes = [
        like((rows, d), BF), like((rows, d), BF), like((rows, f + e), BF), like((rows, f), BF),
        like((rows, e), F32), like((rows, e), F32), like((rows, e), BF), like((rows, e), F32),
        like((rows, e), F32), like((chunks, e, e), F32), like((chunks, 8, e), F32), like((rows, d), BF),
        like((some // 4, d), BF), like((e, e), F32), like((8, e), F32),
    ] + ([like((2, share, d), BF)] * 2 if section == 0 else [like((rows, e), BF)])
    through = list(store) + list(parts)
    operands = [order, *pieces, *weights, *tabs, *([] if section == 0 else [cotangent]), *carry, *through]
    scratch = [pltpu.VMEM(shape, dtype) for shape, dtype in (
        ((some, d), BF), ((d, 3 * e), BF), ((e, d), BF), ((d, f), BF), ((f, d), BF),
        ((4, 1, d), F32), ((hc, e // hc), F32), ((2, some, 2 * (e // hc)), F32), ((2, e, e), BF), ((hc * CHUNK, e), BF), ((e, e), F32),
        ((some, d), BF), ((some, d), BF), ((some, f + e), BF), ((some, f), BF),
        ((some, e), F32), ((some, e), F32), ((some, e), BF), ((some, e), F32),
        ((some, e), F32), ((own, e, e), F32), ((own, 8, e), F32), ((some, d), BF),
        ((e, e), F32), ((8, e), F32))]
    scratch += [pltpu.VMEM(tabs[-1].shape, jnp.int32), pltpu.VMEM((some, d), BF), pltpu.VMEM((some, e), BF), pltpu.SemaphoreType.DMA((32,)), pltpu.SemaphoreType.DMA((16, some // BLOCK))]
    cfg = {"m": m, "section": section, "pieces": len(pieces), "base": base, "share": share, "origin": base // share if ends else 0,
           "e": e, "f": f, "hc": hc, "carried": bool(carry), "alias": len(through), "branch": section == 0}
    first = len(operands) - len(through)
    results = pl.pallas_call(
        functools.partial(forward_kernel, cfg),
        out_shape=shapes,
        in_specs=[ANY] * len(operands),
        out_specs=[ANY] * len(shapes),
        scratch_shapes=scratch,
        input_output_aliases={first + i: i for i in range(len(through))},
        compiler_params=pltpu.CompilerParams(vmem_limit_bytes=VMEM_BYTES),
        cost_estimate=pl.CostEstimate(flops=2 * some * d * (4 * e + 2 * f), bytes_accessed=25 * 2 ** 20, transcendentals=some * (f + 2 * e)),
        name="forward",
    )(*operands)
    return list(results[:12]), results[12], list(results[15:])


def backward_call(sizes, m, section, order, g_in, h_in, weights, tabs, store, back, span=None, carry=(), opened=()):
    rows, d, e, f, hc = sizes
    base, end = span or (0, rows)
    some = end - base
    share = some // 4
    own = some // CHUNK
    shapes = [like((rows, f), BF)] * (not opened) + [like((rows, 3 * e), BF), like((2, share, d), BF), like((2, share, d), BF), like((some // 4, d), BF), like((8, d), F32), like((e, e), F32), like((8, e), F32)]
    operands = [order, *g_in, h_in, *weights, *tabs, *store[4:11], *opened, *carry, *back]
    scratch = [pltpu.VMEM(shape, dtype) for shape, dtype in (
        ((some, d), BF), ((some, d), BF), ((d, 3 * e), BF), ((e, d), BF), ((d, f), BF), ((f, d), BF),
        ((4, 1, d), F32), ((hc, e // hc), F32), ((2, some, 2 * (e // hc)), F32), ((2, e, e), BF), ((hc * CHUNK, e), BF), ((e, e), F32),
        ((some, f), BF), ((some, e), F32), ((some, e), F32), ((some, e), BF),
        ((some, e), F32), ((some, e), F32), ((own, e, e), F32), ((own, 8, e), F32),
        ((some, f), BF), ((some, 3 * e), BF), ((some, d), BF), ((8, d), F32),
        ((some, e), BF), ((5, 8, d), F32), ((8, e), F32), ((e, e), F32), ((8, e), F32))]
    scratch += [pltpu.SemaphoreType.DMA((40,)), pltpu.SemaphoreType.DMA((4, some // BLOCK))]
    cfg = {"m": m, "section": section, "base": base, "share": share, "e": e, "f": f, "hc": hc, "carried": bool(carry), "alias": len(back), "grads": len(g_in), "opened": bool(opened)}
    first = len(operands) - len(back)
    results = pl.pallas_call(
        functools.partial(backward_kernel, cfg),
        out_shape=shapes,
        in_specs=[ANY] * len(operands),
        out_specs=[ANY] * len(shapes),
        scratch_shapes=scratch,
        input_output_aliases={first + i: i for i in range(len(back))},
        compiler_params=pltpu.CompilerParams(vmem_limit_bytes=VMEM_BYTES),
        cost_estimate=pl.CostEstimate(flops=2 * some * d * (4 * e + 2 * f), bytes_accessed=30 * 2 ** 20, transcendentals=0),
        name="backward",
    )(*operands)
    head = 1 if opened else 2
    return list(results[:head]), list(results[head:head + 3]), results[head + 3], list(results[head + 4:])


def down_kernel(cfg, order, *refs):
    count, first, m = cfg["pieces"], cfg["first"], cfg["m"]
    refs = list(refs)

    def take(n):
        out = refs[:n]
        del refs[:n]
        return out

    pieces = take(count)
    (am,) = take(1)
    acc_in = take(0 if first else 1)
    take(cfg["alias"])
    outs = take(2 if count == 4 else 1)
    v_g, v_am, v_acc, v_out, sems, o_sems = refs
    rows, d = v_g.shape
    me = lax.axis_index("tensor")

    def tile(b):
        return rows_at(b, BLOCK)

    def sent(b):
        return pltpu.make_async_copy((v_acc if first else v_out).at[tile(b)], outs[0].at[tile(b)], o_sems.at[b])

    @pl.when(lax.axis_index("section") == cfg["section"])
    def _():
        io = Copies(sems)
        if count == 4:
            loads = io.start(*[(pieces[k], v_g.at[rows_at(me ^ k, rows // 4)]) for k in range(4)])
        else:
            loads = io.start((pieces[0].at[m, 0] if len(pieces[0].shape) == 4 else pieces[0], v_g))
        loads += io.start((am, v_am))
        if not first:
            loads += io.start((acc_in[0], v_acc))
        wait(loads)
        kept = io.start((v_g, outs[1])) if count == 4 else []

        @pl.loop(0, d // BLOCK)
        def _(b):
            product = dot_tn(v_g[:, tile(b)], v_am[...])
            if first:
                v_acc[tile(b)] = product.astype(BF)
            else:
                v_out[tile(b)] = (v_acc[tile(b)].astype(F32) + product).astype(BF)
            sent(b).start()

        wait(kept)

        @pl.loop(0, d // BLOCK)
        def _(b):
            sent(b).wait()


def branch_kernel(order, am, wo, wdown, keep, send, v_am, v_wo, v_wdown, o_part, sems, o_sems):
    rows, d = o_part.shape
    f = v_wdown.shape[0]
    share = rows // 4
    me = lax.axis_index("tensor")

    def outs(b):
        copies = []
        for i in range(WIDE // share):
            at = (b * (WIDE // share) + i) ^ me
            copies.append(Routed(o_part.at[rows_at(b * (WIDE // share) + i, share)], keep, send, at, o_sems.at[i, b]))
        return copies

    @pl.when(lax.axis_index("section") == 1)
    def _():
        wait(Copies(sems).start((am, v_am), (wo.at[0], v_wo), (wdown.at[0], v_wdown)))

        @pl.loop(0, rows // WIDE)
        def _(b):
            rb = rows_at(b, WIDE)
            o_part[rb] = (dot(v_am[rb, f:], v_wo[...]) + dot(v_am[rb, :f], v_wdown[...])).astype(BF)
            for copy in outs(b):
                copy.start()

        @pl.loop(0, rows // WIDE)
        def _(b):
            wait(outs(b))


def branch_call(order, am, w_out, w_down):
    rows, wide = am.shape
    _, f, d = w_down.shape
    return pl.pallas_call(
        branch_kernel,
        out_shape=[like((2, rows // 4, d), BF)] * 2,
        in_specs=[ANY] * 4,
        out_specs=[ANY] * 2,
        scratch_shapes=[pltpu.VMEM((rows, wide), BF), pltpu.VMEM((wide - f, d), BF), pltpu.VMEM((f, d), BF), pltpu.VMEM((rows, d), BF),
                        pltpu.SemaphoreType.DMA((3,)), pltpu.SemaphoreType.DMA((2, rows // WIDE))],
        compiler_params=pltpu.CompilerParams(vmem_limit_bytes=VMEM_BYTES),
        cost_estimate=pl.CostEstimate(flops=0, bytes_accessed=0, transcendentals=0),
        name="branch",
    )(order, am, w_out, w_down)


def arrange_kernel(order, *refs):
    pieces, (out, held, sems) = refs[:4], refs[4:]
    me = lax.axis_index("tensor")

    @pl.when(lax.axis_index("section") == 0)
    def _():
        io = Copies(sems)
        wait(io.start(*[(pieces[k], held.at[rows_at(me ^ k, pieces[k].shape[0])]) for k in range(4)]))
        wait(io.start((held, out)))


def arrange_call(order, pieces):
    share, d = pieces[0].shape
    return pl.pallas_call(
        arrange_kernel,
        out_shape=[like((4 * share, d), BF)],
        in_specs=[ANY] * 5,
        out_specs=[ANY],
        scratch_shapes=[pltpu.VMEM((4 * share, d), BF), pltpu.SemaphoreType.DMA((5,))],
        cost_estimate=pl.CostEstimate(flops=0, bytes_accessed=0, transcendentals=0),
        name="arrange",
    )(order, *pieces)


def unpack_kernel(packed, *outs):
    at = 0
    for out in outs:
        out[0] = packed[:, at:at + out.shape[2]].astype(F32)
        at += out.shape[2]


def unpack_call(packed, widths):
    rows = packed.shape[0]
    whole = pl.BlockSpec(memory_space=pltpu.VMEM)
    return pl.pallas_call(
        unpack_kernel,
        out_shape=[like((1, rows, width), F32) for width in widths],
        in_specs=[whole],
        out_specs=[whole] * len(widths),
        name="unpack",
    )(packed)


def down_call(m, section, order, pieces, am, acc=None, through=None):
    rows, wide = am.shape
    d = pieces[0].shape[-1]
    first = acc is None
    operands = [order, *pieces, am] + ([] if first else [acc]) + ([] if through is None else [through])
    cfg = {"pieces": len(pieces), "first": first, "section": section, "m": m, "alias": int(through is not None)}
    shapes = [like((d, wide), BF)] + [like((rows, d), BF)] * (len(pieces) == 4)
    return pl.pallas_call(
        functools.partial(down_kernel, cfg),
        out_shape=shapes,
        in_specs=[ANY] * len(operands),
        out_specs=[ANY] * len(shapes),
        scratch_shapes=[pltpu.VMEM((rows, d), BF), pltpu.VMEM((rows, wide), BF), pltpu.VMEM((d, wide), BF), pltpu.VMEM((d, wide), BF),
                        pltpu.SemaphoreType.DMA((len(pieces) + 5,)), pltpu.SemaphoreType.DMA((d // BLOCK,))],
        input_output_aliases={} if through is None else {len(operands) - 1: 0},
        compiler_params=pltpu.CompilerParams(vmem_limit_bytes=VMEM_BYTES),
        cost_estimate=pl.CostEstimate(flops=0 if first else 2 * rows * d * wide, bytes_accessed=0 if first else 12 * 2 ** 20, transcendentals=0),
        name="down",
    )(*operands)


def body(tokens, cotangent, lengths, attn_gain, attn_bias, ffn_gain, ffn_bias, w_query, w_key, w_value, w_out, feat_scale, w_up, w_down, down_bias):
    section = lax.axis_index("section")
    tensor = lax.axis_index("tensor")
    teams = lax.axis_size("tensor")
    micro, _, rows, d = tokens.shape
    hc, hd = feat_scale.shape[1:]
    e = hc * hd
    f = w_up.shape[2]
    sizes = (rows, d, e, f, hc)
    whole, early, late = (0, rows), (0, rows // 2), (rows // 2, rows)
    made = host_tables(rows, hc, hd)
    tabs = [attn_gain, attn_bias, ffn_gain, ffn_bias, feat_scale] + [jnp.asarray(made[k]) for k in ("turn", "dct", "heads", "same")] + [lengths]
    weights = [w_query, w_key, w_value, w_out, w_up, w_down]
    both = ("section", "tensor")
    order = attn_gain

    def swap(x, sec, bit):
        sections = range(2) if sec is None else (sec,)
        return lax.ppermute(x, both, [(k * teams + i, k * teams + (i ^ bit)) for k in sections for i in range(teams)])

    def hand(x, source):
        return lax.ppermute(x, "section", [(source, 1 - source)])

    def gather_rows(own, sec):
        far = swap(own, sec, 2)
        return [own, swap(own, sec, 1), far, swap(far, sec, 1)]

    def tie(x, *after):
        return lax.optimization_barrier((x, *after))[0]

    def tie_all(*values):
        return lax.optimization_barrier(values)

    def near_sum(parts, sec):
        keep, send = parts
        got = swap(send, sec, 1)
        return keep[0].astype(F32) + got[0].astype(F32), (keep[1].astype(F32) + got[1].astype(F32)).astype(BF)

    def relay(parts, source):
        near, sent = near_sum(parts, source)
        near = (near + down_bias[0] if source == 0 else near).astype(BF)
        pairs = [[(source * teams + i, (1 - source) * teams + (i ^ bit)) for i in range(teams)] for bit in (0, 2)]
        return [lax.ppermute(near, both, pairs[0]), lax.ppermute(sent, both, pairs[1])], (near, sent)

    def own_rows(x):
        return lax.dynamic_index_in_dim(x.reshape(teams, rows // teams, d), tensor, 0, keepdims=False)

    def whole_rows(own):
        return lax.all_gather(own, "tensor", axis=0, tiled=True)

    def summed(start, took):
        return start.astype(F32) + took[0].astype(F32) + took[1].astype(F32)

    def all_sum(x, axis):
        size, bit = lax.axis_size(axis), 1
        if size & (size - 1):
            return lax.psum(x, axis)
        while bit < size:
            x = x + lax.ppermute(x, axis, [(i, i ^ bit) for i in range(size)])
            bit *= 2
        return x

    def weight_grad(pairs):
        return sum(dot_tn(left, right) for left, right in pairs)

    def scatter(total):
        return lax.psum_scatter(total, "dp", scatter_dimension=0, tiled=True)

    def forward(m, sec, after, pieces, store, **more):
        return forward_call(sizes, m, sec, tie(order, after), pieces, weights, tabs, store, **more)

    def backward(m, sec, after, g_in, h_in, store, back, **more):
        return backward_call(sizes, m, sec, tie(order, after), g_in, h_in, weights, tabs, store, back, **more)

    store_0, _, parts = forward_call(sizes, 0, 0, order, [tokens], weights, tabs, [])
    took, after = relay(parts, 0)
    store_1, _, parts = forward_call(sizes, 1, 0, tie(order, *after), [tokens], weights, tabs, [])
    own_t, *took, parts[0], parts[1] = tie_all(own_rows(tokens[0, 0]), *took, *parts)
    row_0 = summed(own_t, took).astype(BF)
    far_rows = swap(row_0, 1, 2)
    took, after = relay(parts, 0)
    near_rows = swap(tie(row_0, *after), 1, 1)
    far_rows, near_rows = tie_all(far_rows, near_rows)
    store_0, own_0, mix_0 = forward_call(sizes, 0, 1, tie(order, *after, took[0]), [row_0, near_rows, far_rows, swap(far_rows, 1, 1)], weights, tabs, store_0, cotangent=cotangent)
    own_c = [own_rows(cotangent[m, 0]) for m in range(2)]
    *took, own_0, own_t, own_c[0], own_c[1] = tie_all(*took, own_0, own_rows(tokens[1, 0]), *own_c)
    row_1 = summed(own_t, took).astype(BF)
    rows_1 = whole_rows(row_1)
    back_0, parts, sums_0, _ = backward(0, 1, row_1, [cotangent], store_0[11], store_0, [], opened=[store_0[3], *mix_0])
    took_0, after = relay(parts[:2], 1)
    rows_1 = tie(rows_1, *after)
    store_1, own_1, mix_1 = forward_call(sizes, 1, 1, tie(order, *after), [rows_1], weights, tabs, store_1, cotangent=cotangent)
    *took_0, own_1 = tie_all(*took_0, own_1)
    grad_0 = summed(own_c[0], took_0).astype(BF)
    gb_0 = whole_rows(grad_0)
    back_1, parts, sums_1, _ = backward(1, 1, grad_0, [cotangent], store_1[11], store_1, [], opened=[store_1[3], *mix_1])
    took_1, after = relay(parts[:2], 1)
    gb_0, after = tie_all(gb_0, tie(order, *after))
    ends_0 = [*branch_call(after, store_0[2], w_out, w_down), own_0]
    ends_1 = [*branch_call(after, store_1[2], w_out, w_down), own_1]
    back_0, ends_0, sums_0, _ = backward(0, 0, gb_0, [gb_0], tokens, store_0, [store_0[3], *back_0, *ends_0, sums_0])
    *took_1, ends_0[0] = tie_all(*took_1, ends_0[0])
    grad_1 = summed(own_c[1], took_1).astype(BF)
    far_rows = swap(grad_1, 0, 2)
    (acc,) = down_call(0, 0, tie(order, grad_1), [gb_0], store_0[2])
    near_rows = swap(grad_1, 0, 1)
    (acc_b,) = down_call(0, 1, tie(order, acc), [cotangent], store_0[2])
    (down_sum,) = down_call(1, 1, order, [cotangent], store_1[2], acc_b)
    far_rows, near_rows, down_sum = tie_all(far_rows, near_rows, down_sum)
    down_sum, gb_1 = down_call(1, 0, order, [grad_1, near_rows, far_rows, swap(far_rows, 0, 1)], store_1[2], acc, down_sum)
    down = scatter(down_sum)
    back_1, ends_1, sums_1, _ = backward(1, 0, down_sum, [gb_1], tokens, store_1, [store_1[3], *back_1, *ends_1, sums_1])
    rest_sum = jnp.concatenate([
        weight_grad([(store_0[1], back_0[0]), (store_1[1], back_1[0])]).astype(BF),
        weight_grad([(store_0[0], back_0[1]), (store_1[0], back_1[1])]).astype(BF)], axis=1)
    down, rest_sum = tie_all(down, rest_sum)
    rest = scatter(rest_sum)
    up, query, key, value = unpack_call(rest, (f, e, e, e))
    shift = jnp.where(section == 0, 0.0, down_bias[0])
    ends = []
    for parts in (ends_0, ends_1):
        keep, send, own, _ = tie_all(*parts, rest_sum)
        near, sent = near_sum((keep, send), None)
        ends.append(own.astype(F32) + near + swap(sent, None, 2).astype(F32) + shift)
    ends = jnp.stack(ends)[None, :, None]
    down = down.astype(F32).T
    small = all_sum(sums_0 + sums_1, "dp")
    group = lax.axis_size("dp")
    place = lax.axis_index("dp")
    cut = all_sum(lax.dynamic_slice(small, (0, place * (d // group)), (5, d // group)), "tensor")
    scale_cut = lax.dynamic_slice(small[5, :e].reshape(hc, hd), (0, place * (hd // group)), (hc, hd // group))
    return (
        ends, cut[0:1], cut[1:2], cut[2:3], cut[3:4],
        query, key, value, down[None, f:], scale_cut[None], up, down[None, :f],
        cut[4:5] / teams,
    )


def solution(mesh):
    return jax.shard_map(
        body,
        mesh=mesh,
        in_specs=(
            P(None, "dp", None, None), P(None, "dp", None, None), P(None, "dp"),
            P("section", None), P("section", None), P("section", None), P("section", None),
            P("section", None, "tensor"), P("section", None, "tensor"), P("section", None, "tensor"),
            P("section", "tensor", None), P("section", "tensor", None), P("section", None, "tensor"),
            P("section", "tensor", None), P("section", None),
        ),
        out_specs=(
            P("section", None, "dp", "tensor", None),
            P("section", "dp"), P("section", "dp"), P("section", "dp"), P("section", "dp"),
            P("section", "dp", "tensor"), P("section", "dp", "tensor"), P("section", "dp", "tensor"),
            P("section", "tensor", "dp"), P("section", "tensor", "dp"), P("section", "dp", "tensor"),
            P("section", "tensor", "dp"), P("section", "dp"),
        ),
        check_vma=False,
    )
```

```python
import functools
import math

import jax
import jax.numpy as jnp
import numpy as np
from jax import lax
from jax.experimental import pallas as pl
from jax.experimental.pallas import tpu as pltpu
from jax.sharding import PartitionSpec as P

ROT = 16
EPSILON = 1e-05
BLOCK = 512
CHUNK = 128
WIDE = 512
BF = jnp.bfloat16
F32 = jnp.float32
VMEM_BYTES = 60 * 1024 * 1024
ANY = pl.BlockSpec(memory_space=pl.ANY)


def host_tables(slot_rows, head_count, head_size):
    width = head_count * head_size
    halfway = ROT // 2
    column = np.arange(2 * head_size) % head_size
    pair = np.where(column < halfway, column, column - halfway)
    inverse = np.exp(pair * (-2.0 * math.log(10000.0) / ROT))
    angles = np.arange(slot_rows)[:, None] * inverse[None, :]
    turned = (column < 2 * halfway)[None, :]
    sign = np.where(column < halfway, -1.0, 1.0)[None, :]
    cos_full = np.where(turned, np.cos(angles), 1.0)
    sin_full = np.where(turned, sign * np.sin(angles), 0.0)
    order = np.arange(head_size)
    table = np.cos(np.pi * (order[None, :] + 0.5) * order[:, None] / head_size) * np.sqrt(2.0 / head_size)
    table = np.where(order[:, None] == 0, table * np.sqrt(0.5), table)
    dct = np.kron(np.eye(head_count), table.T)
    high = dct.astype(np.float32).astype(BF)
    low = (dct - high.astype(np.float64)).astype(np.float32).astype(BF)
    lane_head = np.arange(width) // head_size
    heads = (np.arange(head_count)[:, None] == lane_head[None, :]).astype(np.float32)
    same = (lane_head[:, None] == lane_head[None, :]).astype(np.float32)
    return {
        "turn": np.stack([cos_full, sin_full]).astype(np.float32),
        "dct": np.stack([high, low]),
        "heads": np.repeat(heads, CHUNK, axis=0).astype(BF),
        "same": same.astype(np.float32),
    }


def dot(a, b):
    return jnp.dot(a, b, preferred_element_type=F32)


def dot_nt(a, b):
    return lax.dot_general(a, b, (((1,), (1,)), ((), ())), preferred_element_type=F32)


def dot_tn(a, b):
    return lax.dot_general(a, b, (((0,), (0,)), ((), ())), preferred_element_type=F32)


def split(x):
    high = x.astype(BF)
    return high, (x - high.astype(F32)).astype(BF)


def stack_heads(x, heads, head_count):
    return jnp.concatenate([x] * head_count, axis=0) * heads


def lanes_of_heads(x, head_count):
    rows = x.shape[0] // head_count
    return jnp.concatenate([x[h * rows:(h + 1) * rows] for h in range(head_count)], axis=1)


def gelu_parts(u):
    cdf = 0.5 + 0.5 * lax.erf(u * (1.0 / math.sqrt(2.0)))
    return u * cdf, cdf + u * (jnp.exp(-0.5 * u * u) * (1.0 / math.sqrt(2.0 * math.pi)))


def partner(x, head_size):
    half = ROT // 2
    lane = lax.broadcasted_iota(jnp.int32, x.shape, 1) & (head_size - 1)
    return jnp.where(lane < half, pltpu.roll(x, x.shape[1] - half, 1), pltpu.roll(x, half, 1))


def standardize(hidden):
    center = hidden - jnp.mean(hidden, axis=-1, keepdims=True)
    spread = jnp.mean(center * center, axis=-1, keepdims=True)
    rstd = lax.rsqrt(spread + EPSILON)
    return center * rstd, rstd


def rows_at(b, size, base=0):
    return pl.ds(pl.multiple_of(b * size + base, size), size)


def flat_scales(ref, head_count):
    return jnp.concatenate([ref[h:h + 1, :] for h in range(head_count)], axis=1)


class Routed:
    def __init__(self, src, keep, send, at, sem):
        self.near = pltpu.make_async_copy(src, keep.at[at >> 1], sem)
        self.far = pltpu.make_async_copy(src, send.at[at >> 1], sem)
        self.at = at

    def start(self):
        @pl.when((self.at & 1) == 0)
        def _():
            self.near.start()

        @pl.when((self.at & 1) != 0)
        def _():
            self.far.start()

    def wait(self):
        self.near.wait()


class Copies:
    def __init__(self, sems):
        self.sems = sems
        self.used = 0

    def start(self, *pairs):
        made = []
        for src, dst in pairs:
            copy = pltpu.make_async_copy(src, dst, self.sems.at[self.used])
            self.used += 1
            copy.start()
            made.append(copy)
        return made


def wait(copies):
    for copy in copies:
        copy.wait()


def looped_out(pairs, sems, first, b):
    return [pltpu.make_async_copy(src, dst, sems.at[first + i, b]) for i, (src, dst) in enumerate(pairs)]


def forward_kernel(cfg, order, *refs):
    pieces, base, share, origin, e, f, hc = (cfg[k] for k in ("pieces", "base", "share", "origin", "e", "f", "hc"))
    hd = e // hc
    carried = cfg["carried"]
    refs = list(refs)

    def take(n):
        out = refs[:n]
        del refs[:n]
        return out

    h_in = take(pieces)
    wq, wk, wv, wo, wup, wdown, *norms, scales, turn, dct, heads, same, lengths = take(16)
    cotangent = None if cfg["branch"] else take(1)[0]
    c_in = take(2 if carried else 0)
    take(cfg["alias"])
    s_n1, s_n2, s_am, s_gp, s_qf, s_kf, s_v, s_mf, s_inv, s_st, s_kt, s_h, own, c_st, c_kt = take(15)
    keep, send = take(2) if cfg["branch"] else (None, None)
    s_mix = None if cfg["branch"] else take(1)[0]
    (v_h, v_wqkv, v_wo, v_wup, v_wdown, v_norms, v_scales, v_turn, v_dct, v_heads, v_same,
     o_n1, o_n2, o_am, o_gp, o_qf, o_kf, o_v, o_mf, o_inv, o_st, o_kt, o_part, state, total, v_len, v_g, o_mix, sems, o_sems) = refs
    rows = v_h.shape[0]
    blocks = rows // BLOCK
    wides = rows // WIDE
    count = BLOCK // CHUNK
    me = lax.axis_index("tensor")

    def outs_a(b):
        rb, ro = rows_at(b, BLOCK), rows_at(b, BLOCK, base)
        return looped_out([(o_n1.at[rb], s_n1.at[ro]), (o_n2.at[rb], s_n2.at[ro])], o_sems, 0, b)

    def outs_b(b):
        rb, ro = rows_at(b, BLOCK), rows_at(b, BLOCK, base)
        cb, co = pl.ds(b * count, count), pl.ds(b * count + base // CHUNK, count)
        return looped_out([(o.at[rb], s.at[ro]) for o, s in ((o_qf, s_qf), (o_kf, s_kf), (o_v, s_v), (o_mf, s_mf), (o_inv, s_inv))]
                          + [(o_st.at[cb], s_st.at[co]), (o_kt.at[cb], s_kt.at[co])], o_sems, 2, b)

    def outs_c(b):
        rb, ro = rows_at(b, WIDE), rows_at(b, WIDE, base)
        copies = looped_out([(o_am.at[rb], s_am.at[ro]), (o_gp.at[rb], s_gp.at[ro])] + ([] if cfg["branch"] else [(o_mix.at[rb], s_mix.at[ro])]), o_sems, 9, b)
        for i in range(WIDE // share if cfg["branch"] else 0):
            at = (b * (WIDE // share) + i + origin) ^ me
            copies.append(Routed(o_part.at[rows_at(b * (WIDE // share) + i, share)], keep, send, at, o_sems.at[11 + i, b]))
        return copies

    @pl.when(lax.axis_index("section") == cfg["section"])
    def _():
        io = Copies(sems)
        if pieces == 1:
            in_h = io.start((h_in[0].at[cfg["m"], 0, pl.ds(base, rows)] if len(h_in[0].shape) == 4 else h_in[0], v_h))
        else:
            halves = pieces // 4
            in_h = io.start(*[(h_in[h * 4 + k], v_h.at[rows_at((me ^ k) * halves + h, rows // pieces)]) for h in range(halves) for k in range(4)])
        in_h += io.start(*[(norm, v_norms.at[i]) for i, norm in enumerate(norms)], (scales.at[0], v_scales))
        in_b = io.start(*[(w.at[0], v_wqkv.at[:, pl.ds(i * e, e)]) for i, w in enumerate((wq, wk, wv))], (turn.at[:, pl.ds(base, rows)], v_turn),
                        (dct, v_dct), (heads, v_heads), (same, v_same), (lengths, v_len))
        if carried:
            in_b += io.start((c_in[0], state), (c_in[1], total))
        else:
            state[...] = jnp.zeros_like(state)
            total[...] = jnp.zeros_like(total)
        in_c = io.start((wup.at[0], v_wup), (wo.at[0], v_wo), (wdown.at[0], v_wdown),
                        *([] if cfg["branch"] else [(cotangent.at[cfg["m"], 0], v_g)]))
        wait(in_h)
        out_h = io.start(*([(v_h, s_h.at[pl.ds(base, rows)])] if cfg["section"] else []), (v_h.at[rows_at(me, rows // 4)], own))

        @pl.loop(0, blocks)
        def _(b):
            rb = rows_at(b, BLOCK)
            xhat, _ = standardize(v_h[rb].astype(F32))
            o_n1[rb] = (xhat * v_norms[0] + v_norms[1]).astype(BF)
            o_n2[rb] = (xhat * v_norms[2] + v_norms[3]).astype(BF)
            for copy in outs_a(b):
                copy.start()

        wait(in_b)

        @pl.loop(0, blocks)
        def _(b):
            rb = rows_at(b, BLOCK)
            qkv = dot(o_n1[rb], v_wqkv[...])
            cos_b = jnp.concatenate([jnp.concatenate([v_turn[0, rb]] * (hc // 2), axis=1)] * 2, axis=0)
            sin_b = jnp.concatenate([jnp.concatenate([v_turn[1, rb]] * (hc // 2), axis=1)] * 2, axis=0)
            pair = jnp.concatenate([qkv[:, :e], qkv[:, e:2 * e]], axis=0)
            high, low = split(pair * cos_b + partner(pair, hd) * sin_b)
            feats = flat_scales(v_scales, hc) * jnp.exp(dot(high, v_dct[0]) + dot(low, v_dct[0]) + dot(high, v_dct[1]))
            q_feat = feats[:BLOCK]
            slot = lax.broadcasted_iota(jnp.int32, (BLOCK, e), 0) + (b * BLOCK + base)
            k_feat = jnp.where(slot < v_len[cfg["m"]:cfg["m"] + 1, :], feats[BLOCK:], 0.0)
            value = qkv[:, 2 * e:].astype(BF)
            q_b = q_feat.astype(BF)
            k_b = k_feat.astype(BF)
            o_qf[rb] = q_b
            o_kf[rb] = k_b
            o_v[rb] = value
            row = lax.broadcasted_iota(jnp.int32, (CHUNK, hc * CHUNK), 0)
            col = lax.broadcasted_iota(jnp.int32, (CHUNK, hc * CHUNK), 1) & (CHUNK - 1)
            causal = row >= col
            for c in range(count):
                rc = slice(c * CHUNK, (c + 1) * CHUNK)
                at = b * count + c
                q_c, k_c, v_c = q_b[rc], k_b[rc], value[rc]
                o_st[at] = state[...]
                o_kt[at] = total[...]
                weighted = (q_c.astype(F32) * total[0:1, :]).astype(BF)
                scores = jnp.where(causal, dot_nt(q_c, stack_heads(k_c, v_heads[...], hc)), 0.0).astype(BF)
                both = dot(scores, jnp.concatenate([stack_heads(v_c, v_heads[...], hc), v_heads[...]], axis=1))
                inverse = 1.0 / (both[:, e:] + dot(weighted, v_same[...].astype(BF)))
                mixed = (both[:, :e] + dot(q_c, state[...].astype(BF))) * inverse
                rg = rows_at(at, CHUNK)
                o_inv[rg] = inverse.astype(BF)
                o_mf[rg] = mixed
                o_am[rg, f:] = mixed.astype(BF)
                state[...] += dot_tn(k_c, v_c) * v_same[...]
                total[...] += jnp.sum(k_c.astype(F32), axis=0, keepdims=True)
            for copy in outs_b(b):
                copy.start()

        out_s = io.start((state, c_st), (total, c_kt))
        wait(in_c)

        @pl.loop(0, wides)
        def _(b):
            rb = rows_at(b, WIDE)
            act, slope = gelu_parts(dot(o_n2[rb], v_wup[...]))
            o_am[rb, :f] = act.astype(BF)
            if not cfg["branch"]:
                slope = slope * dot_nt(v_g[rb], v_wdown[...])
                o_mix[rb] = dot_nt(v_g[rb], v_wo[...]).astype(BF)
            o_gp[rb] = slope.astype(BF)
            if cfg["branch"]:
                o_part[rb] = (dot(o_am[rb, f:], v_wo[...]) + dot(o_am[rb, :f], v_wdown[...])).astype(BF)
            for copy in outs_c(b):
                copy.start()

        wait(out_h + out_s)

        @pl.loop(0, blocks)
        def _(b):
            wait(outs_a(b) + outs_b(b))

        @pl.loop(0, wides)
        def _(b):
            wait(outs_c(b))


def backward_kernel(cfg, order, *refs):
    base, share, e, f, hc = (cfg[k] for k in ("base", "share", "e", "f", "hc"))
    hd = e // hc
    carried = cfg["carried"]
    refs = list(refs)

    def take(n):
        out = refs[:n]
        del refs[:n]
        return out

    g_in = take(cfg["grads"])
    h_in, wq, wk, wv, wo, wup, wdown, *norms, scales, turn, dct, heads, same, _ = take(17)
    s_qf, s_kf, s_v, s_mf, s_inv, s_st, s_kt = take(7)
    opened = cfg["opened"]
    (in_gup, in_mix) = take(2) if opened else (None, None)
    c_in = take(2 if carried else 0)
    s_gp = take(cfg["alias"])[0] if not opened else None
    s_gup = take(1)[0] if not opened else None
    s_gqkv, keep, send, own, sums, c_st, c_kt = take(7)
    (v_g, v_h, v_wqkv, v_wo, v_wup, v_wdown, v_norms, v_scales, v_turn, v_dct, v_heads, v_same,
     i_gp, i_qf, i_kf, i_v, i_mf, i_inv, i_st, i_kt,
     o_gup, o_gqkv, o_part, o_sums, mixes, acc, acc_s, state, total, sems, o_sems) = refs
    rows, d = v_h.shape
    blocks = rows // BLOCK
    wides = rows // WIDE
    chunks = rows // CHUNK
    count = BLOCK // CHUNK
    me = lax.axis_index("tensor")

    def place(x):
        return x.at[cfg["m"], 0, pl.ds(base, rows)] if len(x.shape) == 4 else x.at[pl.ds(base, rows)]

    def outs_a(b):
        rb, ro = rows_at(b, WIDE), rows_at(b, WIDE, base)
        return [] if opened else looped_out([(o_gup.at[rb], s_gup.at[ro])], o_sems, 0, b)

    def outs_b(b):
        rb, ro = rows_at(b, BLOCK), rows_at(b, BLOCK, base)
        return looped_out([(o_gqkv.at[rb], s_gqkv.at[ro])], o_sems, 1, b)

    def outs_c(b):
        copies = []
        for i in range(BLOCK // share):
            at = (b * (BLOCK // share) + i) ^ me
            copies.append(Routed(o_part.at[rows_at(b * (BLOCK // share) + i, share)], keep, send, at, o_sems.at[2 + i, b]))
        return copies

    @pl.when(lax.axis_index("section") == cfg["section"])
    def _():
        io = Copies(sems)
        some = pl.ds(base, rows)
        some_chunks = pl.ds(base // CHUNK, chunks)
        in_g = [(place(g_in[0]), v_g)] if len(g_in) == 1 else [(g, v_g.at[pl.ds(i * g.shape[0], g.shape[0])]) for i, g in enumerate(g_in)]
        in_a = io.start(*([(in_mix.at[some], mixes)] if opened else
                          in_g + [(wdown.at[0], v_wdown), (wo.at[0], v_wo), (s_gp.at[some], i_gp)]))
        in_b = io.start((s_mf.at[some], i_mf), (s_inv.at[some], i_inv), (s_qf.at[some], i_qf), (s_kf.at[some], i_kf), (s_v.at[some], i_v),
                        (s_st.at[some_chunks], i_st), (s_kt.at[some_chunks], i_kt), (heads, v_heads), (same, v_same),
                        (turn.at[:, some], v_turn), (dct, v_dct))
        if carried:
            in_b += io.start((c_in[0], state), (c_in[1], total))
        else:
            state[...] = jnp.zeros_like(state)
            total[...] = jnp.zeros_like(total)
        in_c = io.start(*(in_g + [(in_gup.at[some], o_gup)] if opened else []))
        in_c += io.start(*[(w.at[0], v_wqkv.at[:, pl.ds(i * e, e)]) for i, w in enumerate((wq, wk, wv))], (wup.at[0], v_wup), (place(h_in), v_h),
                        *[(norm, v_norms.at[i]) for i, norm in enumerate(norms)], (scales.at[0], v_scales))
        acc[...] = jnp.zeros_like(acc)
        acc_s[...] = jnp.zeros_like(acc_s)
        wait(in_a)
        out_s = [] if opened else io.start((v_g.at[rows_at(me, rows // 4)], own))

        def fold(x):
            return jnp.sum(x.reshape(x.shape[0] // 8, 8, x.shape[1]), axis=0)

        @pl.loop(0, 0 if opened else wides)
        def _(b):
            rb = rows_at(b, WIDE)
            g_b = v_g[rb]
            o_gup[rb] = (dot_nt(g_b, v_wdown[...]) * i_gp[rb].astype(F32)).astype(BF)
            mixes[rb] = dot_nt(g_b, v_wo[...]).astype(BF)
            for copy in outs_a(b):
                copy.start()

        wait(in_b)

        @pl.loop(0, blocks)
        def _(step):
            b = blocks - 1 - step
            rb = rows_at(b, BLOCK)
            g_num = (mixes[rb].astype(F32) * i_inv[rb].astype(F32)).astype(BF)
            high, low = split(g_num.astype(F32) * i_mf[rb])
            same_b = v_same[...].astype(BF)
            g_den = -(dot(high, same_b) + dot(low, same_b))
            gd_high, gd_low = split(g_den)
            q_b = i_qf[rb]
            k_b = i_kf[rb]
            value = i_v[rb]
            row = lax.broadcasted_iota(jnp.int32, (CHUNK, hc * CHUNK), 0)
            col = lax.broadcasted_iota(jnp.int32, (CHUNK, hc * CHUNK), 1) & (CHUNK - 1)
            causal = row >= col
            row_t = lax.broadcasted_iota(jnp.int32, (hc * CHUNK, CHUNK), 0) & (CHUNK - 1)
            col_t = lax.broadcasted_iota(jnp.int32, (hc * CHUNK, CHUNK), 1)
            causal_t = col_t >= row_t
            hm = v_heads[...]
            sel = hm * jnp.asarray(1.0 / hd, BF)
            gq_parts, gk_parts, gv_parts = [None] * count, [None] * count, [None] * count
            for c in reversed(range(count)):
                rc = slice(c * CHUNK, (c + 1) * CHUNK)
                at = b * count + c
                q_c, k_c, v_c, n_c, dh, dl = q_b[rc], k_b[rc], value[rc], g_num[rc], gd_high[rc], gd_low[rc]
                k_x = stack_heads(k_c, hm, hc)
                spread = jnp.concatenate([jnp.broadcast_to(g_den[rc, h * hd:h * hd + 1], (CHUNK, CHUNK)) for h in range(hc)], axis=1)
                grid = jnp.where(causal, dot_nt(n_c, stack_heads(v_c, hm, hc)) + spread, 0.0).astype(BF)
                grid_s = jnp.concatenate([grid[:, h * CHUNK:(h + 1) * CHUNK] for h in range(hc)], axis=0)
                scores_t = jnp.where(causal_t, dot_nt(k_x, q_c), 0.0).astype(BF)
                before = jnp.concatenate(split(i_st[at]), axis=1)
                gq_parts[c] = dot(grid, k_x) + dot_nt(jnp.concatenate([n_c, n_c], axis=1), before) + g_den[rc] * i_kt[at][0:1, :]
                after = jnp.concatenate(split(state[...]), axis=1)
                gk_parts[c] = dot_tn(grid_s, stack_heads(q_c, hm, hc)) + dot_nt(jnp.concatenate([v_c, v_c], axis=1), after) + total[0:1, :]
                gv_parts[c] = dot(lanes_of_heads(scores_t, hc), stack_heads(n_c, hm, hc)) + dot(k_c, after[:, :e])
                state[...] += dot_tn(q_c, n_c) * v_same[...]
                total[...] += jnp.sum(q_c.astype(F32) * g_den[rc], axis=0, keepdims=True)
            gc_q = jnp.concatenate(gq_parts, axis=0) * q_b.astype(F32)
            gc_k = jnp.concatenate(gk_parts, axis=0) * k_b.astype(F32)
            g_value = jnp.concatenate(gv_parts, axis=0)
            acc_s[...] += fold(gc_q + gc_k)
            cos_b = jnp.concatenate([jnp.concatenate([v_turn[0, rb]] * (hc // 2), axis=1)] * 2, axis=0)
            sin_b = jnp.concatenate([jnp.concatenate([v_turn[1, rb]] * (hc // 2), axis=1)] * 2, axis=0)
            turned = dot_nt(jnp.concatenate([gc_q, gc_k], axis=0).astype(BF), v_dct[0])
            g_qk = turned * cos_b - partner(turned, hd) * sin_b
            o_gqkv[rb] = jnp.concatenate([g_qk[:BLOCK], g_qk[BLOCK:], g_value], axis=1).astype(BF)
            for copy in outs_b(b):
                copy.start()

        out_s += io.start((state, c_st), (total, c_kt))
        wait(in_c)
        if opened:
            out_s += io.start((v_g.at[rows_at(me, rows // 4)], own))

        @pl.loop(0, blocks)
        def _(b):
            rb = rows_at(b, BLOCK)
            g_one = dot_nt(o_gqkv[rb], v_wqkv[...])
            g_two = dot_nt(o_gup[rb], v_wup[...])
            xhat, rstd = standardize(v_h[rb].astype(F32))
            acc[0] += fold(g_one * xhat)
            acc[1] += fold(g_one)
            acc[2] += fold(g_two * xhat)
            acc[3] += fold(g_two)
            acc[4] += fold(v_g[rb].astype(F32))
            inner = g_one * v_norms[0] + g_two * v_norms[2]
            mean_t = jnp.mean(inner, axis=-1, keepdims=True)
            mean_x = jnp.mean(inner * xhat, axis=-1, keepdims=True)
            o_part[rb] = (rstd * (inner - mean_t - xhat * mean_x)).astype(BF)
            for copy in outs_c(b):
                copy.start()

        for i in range(5):
            o_sums[i:i + 1, :] = jnp.sum(acc[i], axis=0, keepdims=True)
        o_sums[5:8, :] = jnp.zeros((3, d), F32)
        o_sums[5:6, :e] = jnp.sum(acc_s[...], axis=0, keepdims=True) / flat_scales(v_scales, hc)
        out_s += io.start((o_sums, sums))
        wait(out_s)

        @pl.loop(0, 0 if opened else wides)
        def _(b):
            wait(outs_a(b))

        @pl.loop(0, blocks)
        def _(b):
            wait(outs_b(b) + outs_c(b))


def like(shape, dtype):
    return jax.ShapeDtypeStruct(shape, dtype)


def forward_call(sizes, m, section, order, pieces, weights, tabs, store, span=None, carry=(), parts=(), ends=False, cotangent=None):
    rows, d, e, f, hc = sizes
    base, end = span or (0, rows)
    some = end - base
    share = rows // 4 if ends or some == rows else some // 4
    chunks = rows // CHUNK
    own = some // CHUNK
    shapes = [
        like((rows, d), BF), like((rows, d), BF), like((rows, f + e), BF), like((rows, f), BF),
        like((rows, e), BF), like((rows, e), BF), like((rows, e), BF), like((rows, e), F32),
        like((rows, e), BF), like((chunks, e, e), F32), like((chunks, 8, e), F32), like((rows, d), BF),
        like((some // 4, d), BF), like((e, e), F32), like((8, e), F32),
    ] + ([like((2, share, d), BF)] * 2 if section == 0 else [like((rows, e), BF)])
    through = list(store) + list(parts)
    operands = [order, *pieces, *weights, *tabs, *([] if section == 0 else [cotangent]), *carry, *through]
    scratch = [pltpu.VMEM(shape, dtype) for shape, dtype in (
        ((some, d), BF), ((d, 3 * e), BF), ((e, d), BF), ((d, f), BF), ((f, d), BF),
        ((4, 1, d), F32), ((hc, e // hc), F32), ((2, some, 2 * (e // hc)), F32), ((2, e, e), BF), ((hc * CHUNK, e), BF), ((e, e), F32),
        ((some, d), BF), ((some, d), BF), ((some, f + e), BF), ((some, f), BF),
        ((some, e), BF), ((some, e), BF), ((some, e), BF), ((some, e), F32),
        ((some, e), BF), ((own, e, e), F32), ((own, 8, e), F32), ((some, d), BF),
        ((e, e), F32), ((8, e), F32))]
    scratch += [pltpu.VMEM(tabs[-1].shape, jnp.int32), pltpu.VMEM((some, d), BF), pltpu.VMEM((some, e), BF), pltpu.SemaphoreType.DMA((32,)), pltpu.SemaphoreType.DMA((16, some // BLOCK))]
    cfg = {"m": m, "section": section, "pieces": len(pieces), "base": base, "share": share, "origin": base // share if ends else 0,
           "e": e, "f": f, "hc": hc, "carried": bool(carry), "alias": len(through), "branch": section == 0}
    first = len(operands) - len(through)
    results = pl.pallas_call(
        functools.partial(forward_kernel, cfg),
        out_shape=shapes,
        in_specs=[ANY] * len(operands),
        out_specs=[ANY] * len(shapes),
        scratch_shapes=scratch,
        input_output_aliases={first + i: i for i in range(len(through))},
        compiler_params=pltpu.CompilerParams(vmem_limit_bytes=VMEM_BYTES),
        cost_estimate=pl.CostEstimate(flops=2 * some * d * (4 * e + 2 * f), bytes_accessed=25 * 2 ** 20, transcendentals=some * (f + 2 * e)),
        name="forward",
    )(*operands)
    return list(results[:12]), results[12], list(results[15:])


def backward_call(sizes, m, section, order, g_in, h_in, weights, tabs, store, back, span=None, carry=(), opened=()):
    rows, d, e, f, hc = sizes
    base, end = span or (0, rows)
    some = end - base
    share = some // 4
    own = some // CHUNK
    shapes = [like((rows, f), BF)] * (not opened) + [like((rows, 3 * e), BF), like((2, share, d), BF), like((2, share, d), BF), like((some // 4, d), BF), like((8, d), F32), like((e, e), F32), like((8, e), F32)]
    operands = [order, *g_in, h_in, *weights, *tabs, *store[4:11], *opened, *carry, *back]
    scratch = [pltpu.VMEM(shape, dtype) for shape, dtype in (
        ((some, d), BF), ((some, d), BF), ((d, 3 * e), BF), ((e, d), BF), ((d, f), BF), ((f, d), BF),
        ((4, 1, d), F32), ((hc, e // hc), F32), ((2, some, 2 * (e // hc)), F32), ((2, e, e), BF), ((hc * CHUNK, e), BF), ((e, e), F32),
        ((some, f), BF), ((some, e), BF), ((some, e), BF), ((some, e), BF),
        ((some, e), F32), ((some, e), BF), ((own, e, e), F32), ((own, 8, e), F32),
        ((some, f), BF), ((some, 3 * e), BF), ((some, d), BF), ((8, d), F32),
        ((some, e), BF), ((5, 8, d), F32), ((8, e), F32), ((e, e), F32), ((8, e), F32))]
    scratch += [pltpu.SemaphoreType.DMA((40,)), pltpu.SemaphoreType.DMA((4, some // BLOCK))]
    cfg = {"m": m, "section": section, "base": base, "share": share, "e": e, "f": f, "hc": hc, "carried": bool(carry), "alias": len(back), "grads": len(g_in), "opened": bool(opened)}
    first = len(operands) - len(back)
    results = pl.pallas_call(
        functools.partial(backward_kernel, cfg),
        out_shape=shapes,
        in_specs=[ANY] * len(operands),
        out_specs=[ANY] * len(shapes),
        scratch_shapes=scratch,
        input_output_aliases={first + i: i for i in range(len(back))},
        compiler_params=pltpu.CompilerParams(vmem_limit_bytes=VMEM_BYTES),
        cost_estimate=pl.CostEstimate(flops=2 * some * d * (4 * e + 2 * f), bytes_accessed=30 * 2 ** 20, transcendentals=0),
        name="backward",
    )(*operands)
    head = 1 if opened else 2
    return list(results[:head]), list(results[head:head + 3]), results[head + 3], list(results[head + 4:])


def down_kernel(cfg, order, *refs):
    count, first, m = cfg["pieces"], cfg["first"], cfg["m"]
    refs = list(refs)

    def take(n):
        out = refs[:n]
        del refs[:n]
        return out

    pieces = take(count)
    (am,) = take(1)
    acc_in = take(0 if first else 1)
    take(cfg["alias"])
    outs = take(2 if count == 4 else 1)
    v_g, v_am, v_acc, v_out, sems, o_sems = refs
    rows, d = v_g.shape
    me = lax.axis_index("tensor")

    def tile(b):
        return rows_at(b, BLOCK)

    def sent(b):
        return pltpu.make_async_copy((v_acc if first else v_out).at[tile(b)], outs[0].at[tile(b)], o_sems.at[b])

    @pl.when(lax.axis_index("section") == cfg["section"])
    def _():
        io = Copies(sems)
        if count == 4:
            loads = io.start(*[(pieces[k], v_g.at[rows_at(me ^ k, rows // 4)]) for k in range(4)])
        else:
            loads = io.start((pieces[0].at[m, 0] if len(pieces[0].shape) == 4 else pieces[0], v_g))
        loads += io.start((am, v_am))
        if not first:
            loads += io.start((acc_in[0], v_acc))
        wait(loads)
        kept = io.start((v_g, outs[1])) if count == 4 else []

        @pl.loop(0, d // BLOCK)
        def _(b):
            product = dot_tn(v_g[:, tile(b)], v_am[...])
            if first:
                v_acc[tile(b)] = product.astype(BF)
            else:
                v_out[tile(b)] = (v_acc[tile(b)].astype(F32) + product).astype(BF)
            sent(b).start()

        wait(kept)

        @pl.loop(0, d // BLOCK)
        def _(b):
            sent(b).wait()


def branch_kernel(order, am, wo, wdown, keep, send, v_am, v_wo, v_wdown, o_part, sems, o_sems):
    rows, d = o_part.shape
    f = v_wdown.shape[0]
    share = rows // 4
    me = lax.axis_index("tensor")

    def outs(b):
        copies = []
        for i in range(WIDE // share):
            at = (b * (WIDE // share) + i) ^ me
            copies.append(Routed(o_part.at[rows_at(b * (WIDE // share) + i, share)], keep, send, at, o_sems.at[i, b]))
        return copies

    @pl.when(lax.axis_index("section") == 1)
    def _():
        wait(Copies(sems).start((am, v_am), (wo.at[0], v_wo), (wdown.at[0], v_wdown)))

        @pl.loop(0, rows // WIDE)
        def _(b):
            rb = rows_at(b, WIDE)
            o_part[rb] = (dot(v_am[rb, f:], v_wo[...]) + dot(v_am[rb, :f], v_wdown[...])).astype(BF)
            for copy in outs(b):
                copy.start()

        @pl.loop(0, rows // WIDE)
        def _(b):
            wait(outs(b))


def branch_call(order, am, w_out, w_down):
    rows, wide = am.shape
    _, f, d = w_down.shape
    return pl.pallas_call(
        branch_kernel,
        out_shape=[like((2, rows // 4, d), BF)] * 2,
        in_specs=[ANY] * 4,
        out_specs=[ANY] * 2,
        scratch_shapes=[pltpu.VMEM((rows, wide), BF), pltpu.VMEM((wide - f, d), BF), pltpu.VMEM((f, d), BF), pltpu.VMEM((rows, d), BF),
                        pltpu.SemaphoreType.DMA((3,)), pltpu.SemaphoreType.DMA((2, rows // WIDE))],
        compiler_params=pltpu.CompilerParams(vmem_limit_bytes=VMEM_BYTES),
        cost_estimate=pl.CostEstimate(flops=0, bytes_accessed=0, transcendentals=0),
        name="branch",
    )(order, am, w_out, w_down)


def arrange_kernel(order, *refs):
    pieces, (out, held, sems) = refs[:4], refs[4:]
    me = lax.axis_index("tensor")

    @pl.when(lax.axis_index("section") == 0)
    def _():
        io = Copies(sems)
        wait(io.start(*[(pieces[k], held.at[rows_at(me ^ k, pieces[k].shape[0])]) for k in range(4)]))
        wait(io.start((held, out)))


def arrange_call(order, pieces):
    share, d = pieces[0].shape
    return pl.pallas_call(
        arrange_kernel,
        out_shape=[like((4 * share, d), BF)],
        in_specs=[ANY] * 5,
        out_specs=[ANY],
        scratch_shapes=[pltpu.VMEM((4 * share, d), BF), pltpu.SemaphoreType.DMA((5,))],
        cost_estimate=pl.CostEstimate(flops=0, bytes_accessed=0, transcendentals=0),
        name="arrange",
    )(order, *pieces)


def unpack_kernel(packed, *outs):
    at = 0
    for out in outs:
        out[0] = packed[:, at:at + out.shape[2]].astype(F32)
        at += out.shape[2]


def unpack_call(packed, widths):
    rows = packed.shape[0]
    whole = pl.BlockSpec(memory_space=pltpu.VMEM)
    return pl.pallas_call(
        unpack_kernel,
        out_shape=[like((1, rows, width), F32) for width in widths],
        in_specs=[whole],
        out_specs=[whole] * len(widths),
        name="unpack",
    )(packed)


def down_call(m, section, order, pieces, am, acc=None, through=None):
    rows, wide = am.shape
    d = pieces[0].shape[-1]
    first = acc is None
    operands = [order, *pieces, am] + ([] if first else [acc]) + ([] if through is None else [through])
    cfg = {"pieces": len(pieces), "first": first, "section": section, "m": m, "alias": int(through is not None)}
    shapes = [like((d, wide), BF)] + [like((rows, d), BF)] * (len(pieces) == 4)
    return pl.pallas_call(
        functools.partial(down_kernel, cfg),
        out_shape=shapes,
        in_specs=[ANY] * len(operands),
        out_specs=[ANY] * len(shapes),
        scratch_shapes=[pltpu.VMEM((rows, d), BF), pltpu.VMEM((rows, wide), BF), pltpu.VMEM((d, wide), BF), pltpu.VMEM((d, wide), BF),
                        pltpu.SemaphoreType.DMA((len(pieces) + 5,)), pltpu.SemaphoreType.DMA((d // BLOCK,))],
        input_output_aliases={} if through is None else {len(operands) - 1: 0},
        compiler_params=pltpu.CompilerParams(vmem_limit_bytes=VMEM_BYTES),
        cost_estimate=pl.CostEstimate(flops=0 if first else 2 * rows * d * wide, bytes_accessed=0 if first else 12 * 2 ** 20, transcendentals=0),
        name="down",
    )(*operands)


def body(tokens, cotangent, lengths, attn_gain, attn_bias, ffn_gain, ffn_bias, w_query, w_key, w_value, w_out, feat_scale, w_up, w_down, down_bias):
    section = lax.axis_index("section")
    tensor = lax.axis_index("tensor")
    teams = lax.axis_size("tensor")
    micro, _, rows, d = tokens.shape
    hc, hd = feat_scale.shape[1:]
    e = hc * hd
    f = w_up.shape[2]
    sizes = (rows, d, e, f, hc)
    whole, early, late = (0, rows), (0, rows // 2), (rows // 2, rows)
    made = host_tables(rows, hc, hd)
    tabs = [attn_gain, attn_bias, ffn_gain, ffn_bias, feat_scale] + [jnp.asarray(made[k]) for k in ("turn", "dct", "heads", "same")] + [lengths]
    weights = [w_query, w_key, w_value, w_out, w_up, w_down]
    both = ("section", "tensor")
    order = attn_gain

    def swap(x, sec, bit):
        sections = range(2) if sec is None else (sec,)
        return lax.ppermute(x, both, [(k * teams + i, k * teams + (i ^ bit)) for k in sections for i in range(teams)])

    def hand(x, source):
        return lax.ppermute(x, "section", [(source, 1 - source)])

    def gather_rows(own, sec):
        far = swap(own, sec, 2)
        return [own, swap(own, sec, 1), far, swap(far, sec, 1)]

    def tie(x, *after):
        return lax.optimization_barrier((x, *after))[0]

    def tie_all(*values):
        return lax.optimization_barrier(values)

    def near_sum(parts, sec):
        keep, send = parts
        got = swap(send, sec, 1)
        return keep[0].astype(F32) + got[0].astype(F32), (keep[1].astype(F32) + got[1].astype(F32)).astype(BF)

    def relay(parts, source):
        near, sent = near_sum(parts, source)
        near = (near + down_bias[0] if source == 0 else near).astype(BF)
        pairs = [[(source * teams + i, (1 - source) * teams + (i ^ bit)) for i in range(teams)] for bit in (0, 2)]
        return [lax.ppermute(near, both, pairs[0]), lax.ppermute(sent, both, pairs[1])], (near, sent)

    def own_rows(x):
        return lax.dynamic_index_in_dim(x.reshape(teams, rows // teams, d), tensor, 0, keepdims=False)

    def whole_rows(own):
        return lax.all_gather(own, "tensor", axis=0, tiled=True)

    def summed(start, took):
        return start.astype(F32) + took[0].astype(F32) + took[1].astype(F32)

    def all_sum(x, axis):
        size, bit = lax.axis_size(axis), 1
        if size & (size - 1):
            return lax.psum(x, axis)
        while bit < size:
            x = x + lax.ppermute(x, axis, [(i, i ^ bit) for i in range(size)])
            bit *= 2
        return x

    def weight_grad(pairs):
        return sum(dot_tn(left, right) for left, right in pairs)

    def scatter(total):
        return lax.psum_scatter(total, "dp", scatter_dimension=0, tiled=True)

    def forward(m, sec, after, pieces, store, **more):
        return forward_call(sizes, m, sec, tie(order, after), pieces, weights, tabs, store, **more)

    def backward(m, sec, after, g_in, h_in, store, back, **more):
        return backward_call(sizes, m, sec, tie(order, after), g_in, h_in, weights, tabs, store, back, **more)

    store_0, _, parts = forward_call(sizes, 0, 0, order, [tokens], weights, tabs, [])
    took, after = relay(parts, 0)
    store_1, _, parts = forward_call(sizes, 1, 0, tie(order, *after), [tokens], weights, tabs, [])
    own_t, *took, parts[0], parts[1] = tie_all(own_rows(tokens[0, 0]), *took, *parts)
    row_0 = summed(own_t, took).astype(BF)
    far_rows = swap(row_0, 1, 2)
    took, after = relay(parts, 0)
    near_rows = swap(tie(row_0, *after), 1, 1)
    far_rows, near_rows = tie_all(far_rows, near_rows)
    store_0, own_0, mix_0 = forward_call(sizes, 0, 1, tie(order, *after, took[0]), [row_0, near_rows, far_rows, swap(far_rows, 1, 1)], weights, tabs, store_0, cotangent=cotangent)
    own_c = [own_rows(cotangent[m, 0]) for m in range(2)]
    *took, own_0, own_t, own_c[0], own_c[1] = tie_all(*took, own_0, own_rows(tokens[1, 0]), *own_c)
    row_1 = summed(own_t, took).astype(BF)
    rows_1 = whole_rows(row_1)
    back_0, parts, sums_0, _ = backward(0, 1, row_1, [cotangent], store_0[11], store_0, [], opened=[store_0[3], *mix_0])
    took_0, after = relay(parts[:2], 1)
    rows_1 = tie(rows_1, *after)
    store_1, own_1, mix_1 = forward_call(sizes, 1, 1, tie(order, *after), [rows_1], weights, tabs, store_1, cotangent=cotangent)
    *took_0, own_1 = tie_all(*took_0, own_1)
    grad_0 = summed(own_c[0], took_0).astype(BF)
    gb_0 = whole_rows(grad_0)
    back_1, parts, sums_1, _ = backward(1, 1, grad_0, [cotangent], store_1[11], store_1, [], opened=[store_1[3], *mix_1])
    took_1, after = relay(parts[:2], 1)
    gb_0, after = tie_all(gb_0, tie(order, *after))
    ends_0 = [*branch_call(after, store_0[2], w_out, w_down), own_0]
    ends_1 = [*branch_call(after, store_1[2], w_out, w_down), own_1]
    back_0, ends_0, sums_0, _ = backward(0, 0, gb_0, [gb_0], tokens, store_0, [store_0[3], *back_0, *ends_0, sums_0])
    *took_1, ends_0[0] = tie_all(*took_1, ends_0[0])
    grad_1 = summed(own_c[1], took_1).astype(BF)
    far_rows = swap(grad_1, 0, 2)
    (acc,) = down_call(0, 0, tie(order, grad_1), [gb_0], store_0[2])
    near_rows = swap(grad_1, 0, 1)
    (acc_b,) = down_call(0, 1, tie(order, acc), [cotangent], store_0[2])
    (down_sum,) = down_call(1, 1, order, [cotangent], store_1[2], acc_b)
    far_rows, near_rows, down_sum = tie_all(far_rows, near_rows, down_sum)
    down_sum, gb_1 = down_call(1, 0, order, [grad_1, near_rows, far_rows, swap(far_rows, 0, 1)], store_1[2], acc, down_sum)
    down = scatter(down_sum)
    back_1, ends_1, sums_1, _ = backward(1, 0, down_sum, [gb_1], tokens, store_1, [store_1[3], *back_1, *ends_1, sums_1])
    rest_sum = jnp.concatenate([
        weight_grad([(store_0[1], back_0[0]), (store_1[1], back_1[0])]).astype(BF),
        weight_grad([(store_0[0], back_0[1]), (store_1[0], back_1[1])]).astype(BF)], axis=1)
    down, rest_sum = tie_all(down, rest_sum)
    rest = scatter(rest_sum)
    up, query, key, value = unpack_call(rest, (f, e, e, e))
    shift = jnp.where(section == 0, 0.0, down_bias[0])
    ends = []
    for parts in (ends_0, ends_1):
        keep, send, own, _ = tie_all(*parts, rest_sum)
        near, sent = near_sum((keep, send), None)
        ends.append(own.astype(F32) + near + swap(sent, None, 2).astype(F32) + shift)
    ends = jnp.stack(ends)[None, :, None]
    down = down.astype(F32).T
    small = all_sum(sums_0 + sums_1, "dp")
    group = lax.axis_size("dp")
    place = lax.axis_index("dp")
    cut = all_sum(lax.dynamic_slice(small, (0, place * (d // group)), (5, d // group)), "tensor")
    scale_cut = lax.dynamic_slice(small[5, :e].reshape(hc, hd), (0, place * (hd // group)), (hc, hd // group))
    return (
        ends, cut[0:1], cut[1:2], cut[2:3], cut[3:4],
        query, key, value, down[None, f:], scale_cut[None], up, down[None, :f],
        cut[4:5] / teams,
    )


def solution(mesh):
    return jax.shard_map(
        body,
        mesh=mesh,
        in_specs=(
            P(None, "dp", None, None), P(None, "dp", None, None), P(None, "dp"),
            P("section", None), P("section", None), P("section", None), P("section", None),
            P("section", None, "tensor"), P("section", None, "tensor"), P("section", None, "tensor"),
            P("section", "tensor", None), P("section", "tensor", None), P("section", None, "tensor"),
            P("section", "tensor", None), P("section", None),
        ),
        out_specs=(
            P("section", None, "dp", "tensor", None),
            P("section", "dp"), P("section", "dp"), P("section", "dp"), P("section", "dp"),
            P("section", "dp", "tensor"), P("section", "dp", "tensor"), P("section", "dp", "tensor"),
            P("section", "tensor", "dp"), P("section", "tensor", "dp"), P("section", "dp", "tensor"),
            P("section", "tensor", "dp"), P("section", "dp"),
        ),
        check_vma=False,
    )
```

```python
import functools
import math

import jax
import jax.numpy as jnp
import numpy as np
from jax import lax
from jax.experimental import pallas as pl
from jax.experimental.pallas import tpu as pltpu
from jax.sharding import PartitionSpec as P

ROT = 16
EPSILON = 1e-05
BLOCK = 512
CHUNK = 128
WIDE = 512
BF = jnp.bfloat16
F32 = jnp.float32
VMEM_BYTES = 60 * 1024 * 1024
ANY = pl.BlockSpec(memory_space=pl.ANY)


def host_tables(slot_rows, head_count, head_size):
    width = head_count * head_size
    halfway = ROT // 2
    column = np.arange(2 * head_size) % head_size
    pair = np.where(column < halfway, column, column - halfway)
    inverse = np.exp(pair * (-2.0 * math.log(10000.0) / ROT))
    angles = np.arange(slot_rows)[:, None] * inverse[None, :]
    turned = (column < 2 * halfway)[None, :]
    sign = np.where(column < halfway, -1.0, 1.0)[None, :]
    cos_full = np.where(turned, np.cos(angles), 1.0)
    sin_full = np.where(turned, sign * np.sin(angles), 0.0)
    order = np.arange(head_size)
    table = np.cos(np.pi * (order[None, :] + 0.5) * order[:, None] / head_size) * np.sqrt(2.0 / head_size)
    table = np.where(order[:, None] == 0, table * np.sqrt(0.5), table)
    dct = np.kron(np.eye(head_count), table.T)
    high = dct.astype(np.float32).astype(BF)
    low = (dct - high.astype(np.float64)).astype(np.float32).astype(BF)
    lane_head = np.arange(width) // head_size
    heads = (np.arange(head_count)[:, None] == lane_head[None, :]).astype(np.float32)
    same = (lane_head[:, None] == lane_head[None, :]).astype(np.float32)
    return {
        "turn": np.stack([cos_full, sin_full]).astype(np.float32),
        "dct": np.stack([high, low]),
        "heads": np.repeat(heads, CHUNK, axis=0).astype(BF),
        "same": same.astype(np.float32),
    }


def dot(a, b):
    return jnp.dot(a, b, preferred_element_type=F32)


def dot_nt(a, b):
    return lax.dot_general(a, b, (((1,), (1,)), ((), ())), preferred_element_type=F32)


def dot_tn(a, b):
    return lax.dot_general(a, b, (((0,), (0,)), ((), ())), preferred_element_type=F32)


def split(x):
    high = x.astype(BF)
    return high, (x - high.astype(F32)).astype(BF)


def stack_heads(x, heads, head_count):
    return jnp.concatenate([x] * head_count, axis=0) * heads


def lanes_of_heads(x, head_count):
    rows = x.shape[0] // head_count
    return jnp.concatenate([x[h * rows:(h + 1) * rows] for h in range(head_count)], axis=1)


def gelu_parts(u):
    cdf = 0.5 + 0.5 * lax.erf(u * (1.0 / math.sqrt(2.0)))
    return u * cdf, cdf + u * (jnp.exp(-0.5 * u * u) * (1.0 / math.sqrt(2.0 * math.pi)))


def partner(x, head_size):
    half = ROT // 2
    lane = lax.broadcasted_iota(jnp.int32, x.shape, 1) & (head_size - 1)
    return jnp.where(lane < half, pltpu.roll(x, x.shape[1] - half, 1), pltpu.roll(x, half, 1))


def standardize(hidden):
    center = hidden - jnp.mean(hidden, axis=-1, keepdims=True)
    spread = jnp.mean(center * center, axis=-1, keepdims=True)
    rstd = lax.rsqrt(spread + EPSILON)
    return center * rstd, rstd


def rows_at(b, size, base=0):
    return pl.ds(pl.multiple_of(b * size + base, size), size)


def flat_scales(ref, head_count):
    return jnp.concatenate([ref[h:h + 1, :] for h in range(head_count)], axis=1)


class Routed:
    def __init__(self, src, keep, send, at, sem):
        self.near = pltpu.make_async_copy(src, keep.at[at >> 1], sem)
        self.far = pltpu.make_async_copy(src, send.at[at >> 1], sem)
        self.at = at

    def start(self):
        @pl.when((self.at & 1) == 0)
        def _():
            self.near.start()

        @pl.when((self.at & 1) != 0)
        def _():
            self.far.start()

    def wait(self):
        self.near.wait()


class Copies:
    def __init__(self, sems):
        self.sems = sems
        self.used = 0

    def start(self, *pairs):
        made = []
        for src, dst in pairs:
            copy = pltpu.make_async_copy(src, dst, self.sems.at[self.used])
            self.used += 1
            copy.start()
            made.append(copy)
        return made


def wait(copies):
    for copy in copies:
        copy.wait()


def looped_out(pairs, sems, first, b):
    return [pltpu.make_async_copy(src, dst, sems.at[first + i, b]) for i, (src, dst) in enumerate(pairs)]


def forward_kernel(cfg, order, *refs):
    pieces, base, share, origin, e, f, hc = (cfg[k] for k in ("pieces", "base", "share", "origin", "e", "f", "hc"))
    hd = e // hc
    carried = cfg["carried"]
    refs = list(refs)

    def take(n):
        out = refs[:n]
        del refs[:n]
        return out

    h_in = take(pieces)
    wq, wk, wv, wo, wup, wdown, *norms, scales, turn, dct, heads, same, lengths = take(16)
    cotangent = None if cfg["branch"] else take(1)[0]
    c_in = take(2 if carried else 0)
    take(cfg["alias"])
    s_n1, s_n2, s_am, s_gp, s_qf, s_kf, s_v, s_mf, s_inv, s_st, s_kt, s_h, own, c_st, c_kt = take(15)
    keep, send = take(2) if cfg["branch"] else (None, None)
    s_mix = None if cfg["branch"] else take(1)[0]
    (v_h, v_wqkv, v_wo, v_wup, v_wdown, v_norms, v_scales, v_turn, v_dct, v_heads, v_same,
     o_n1, o_n2, o_am, o_gp, o_qf, o_kf, o_v, o_mf, o_inv, o_st, o_kt, o_part, state, total, v_len, v_g, o_mix, sems, o_sems) = refs
    rows = v_h.shape[0]
    blocks = rows // BLOCK
    wides = rows // WIDE
    count = BLOCK // CHUNK
    me = lax.axis_index("tensor")

    def outs_a(b):
        rb, ro = rows_at(b, BLOCK), rows_at(b, BLOCK, base)
        return looped_out([(o_n1.at[rb], s_n1.at[ro]), (o_n2.at[rb], s_n2.at[ro])], o_sems, 0, b)

    def outs_b(b):
        rb, ro = rows_at(b, BLOCK), rows_at(b, BLOCK, base)
        cb, co = pl.ds(b * count, count), pl.ds(b * count + base // CHUNK, count)
        return looped_out([(o.at[rb], s.at[ro]) for o, s in ((o_qf, s_qf), (o_kf, s_kf), (o_v, s_v), (o_mf, s_mf), (o_inv, s_inv))]
                          + [(o_st.at[cb], s_st.at[co]), (o_kt.at[cb], s_kt.at[co])], o_sems, 2, b)

    def outs_c(b):
        rb, ro = rows_at(b, WIDE), rows_at(b, WIDE, base)
        copies = looped_out([(o_am.at[rb], s_am.at[ro]), (o_gp.at[rb], s_gp.at[ro])] + ([] if cfg["branch"] else [(o_mix.at[rb], s_mix.at[ro])]), o_sems, 9, b)
        for i in range(WIDE // share if cfg["branch"] else 0):
            at = (b * (WIDE // share) + i + origin) ^ me
            copies.append(Routed(o_part.at[rows_at(b * (WIDE // share) + i, share)], keep, send, at, o_sems.at[11 + i, b]))
        return copies

    @pl.when(lax.axis_index("section") == cfg["section"])
    def _():
        io = Copies(sems)
        if pieces == 1:
            in_h = io.start((h_in[0].at[cfg["m"], 0, pl.ds(base, rows)] if len(h_in[0].shape) == 4 else h_in[0], v_h))
        else:
            halves = pieces // 4
            in_h = io.start(*[(h_in[h * 4 + k], v_h.at[rows_at((me ^ k) * halves + h, rows // pieces)]) for h in range(halves) for k in range(4)])
        in_h += io.start(*[(norm, v_norms.at[i]) for i, norm in enumerate(norms)], (scales.at[0], v_scales))
        in_b = io.start(*[(w.at[0], v_wqkv.at[:, pl.ds(i * e, e)]) for i, w in enumerate((wq, wk, wv))], (turn.at[:, pl.ds(base, rows)], v_turn),
                        (dct, v_dct), (heads, v_heads), (same, v_same), (lengths, v_len))
        if carried:
            in_b += io.start((c_in[0], state), (c_in[1], total))
        else:
            state[...] = jnp.zeros_like(state)
            total[...] = jnp.zeros_like(total)
        wait(in_h)
        in_c = io.start((wup.at[0], v_wup), (wo.at[0], v_wo), (wdown.at[0], v_wdown),
                        *([] if cfg["branch"] else [(cotangent.at[cfg["m"], 0], v_g)]))
        out_h = io.start(*([(v_h, s_h.at[pl.ds(base, rows)])] if cfg["section"] else []), (v_h.at[rows_at(me, rows // 4)], own))

        @pl.loop(0, blocks)
        def _(b):
            rb = rows_at(b, BLOCK)
            xhat, _ = standardize(v_h[rb].astype(F32))
            o_n1[rb] = (xhat * v_norms[0] + v_norms[1]).astype(BF)
            o_n2[rb] = (xhat * v_norms[2] + v_norms[3]).astype(BF)
            for copy in outs_a(b):
                copy.start()

        wait(in_b)

        @pl.loop(0, blocks)
        def _(b):
            rb = rows_at(b, BLOCK)
            qkv = dot(o_n1[rb], v_wqkv[...])
            cos_b = jnp.concatenate([jnp.concatenate([v_turn[0, rb]] * (hc // 2), axis=1)] * 2, axis=0)
            sin_b = jnp.concatenate([jnp.concatenate([v_turn[1, rb]] * (hc // 2), axis=1)] * 2, axis=0)
            pair = jnp.concatenate([qkv[:, :e], qkv[:, e:2 * e]], axis=0)
            high, low = split(pair * cos_b + partner(pair, hd) * sin_b)
            feats = flat_scales(v_scales, hc) * jnp.exp(dot(high, v_dct[0]) + dot(low, v_dct[0]) + dot(high, v_dct[1]))
            q_feat = feats[:BLOCK]
            slot = lax.broadcasted_iota(jnp.int32, (BLOCK, e), 0) + (b * BLOCK + base)
            k_feat = jnp.where(slot < v_len[cfg["m"]:cfg["m"] + 1, :], feats[BLOCK:], 0.0)
            value = qkv[:, 2 * e:].astype(BF)
            q_b = q_feat.astype(BF)
            k_b = k_feat.astype(BF)
            o_qf[rb] = q_b
            o_kf[rb] = k_b
            o_v[rb] = value
            row = lax.broadcasted_iota(jnp.int32, (CHUNK, hc * CHUNK), 0)
            col = lax.broadcasted_iota(jnp.int32, (CHUNK, hc * CHUNK), 1) & (CHUNK - 1)
            causal = row >= col
            for c in range(count):
                rc = slice(c * CHUNK, (c + 1) * CHUNK)
                at = b * count + c
                q_c, k_c, v_c = q_b[rc], k_b[rc], value[rc]
                o_st[at] = state[...]
                o_kt[at] = total[...]
                weighted = (q_c.astype(F32) * total[0:1, :]).astype(BF)
                scores = jnp.where(causal, dot_nt(q_c, stack_heads(k_c, v_heads[...], hc)), 0.0).astype(BF)
                both = dot(scores, jnp.concatenate([stack_heads(v_c, v_heads[...], hc), v_heads[...]], axis=1))
                inverse = 1.0 / (both[:, e:] + dot(weighted, v_same[...].astype(BF)))
                mixed = (both[:, :e] + dot(q_c, state[...].astype(BF))) * inverse
                rg = rows_at(at, CHUNK)
                o_inv[rg] = inverse.astype(BF)
                o_mf[rg] = mixed
                o_am[rg, f:] = mixed.astype(BF)
                state[...] += dot_tn(k_c, v_c) * v_same[...]
                total[...] += jnp.sum(k_c.astype(F32), axis=0, keepdims=True)
            for copy in outs_b(b):
                copy.start()

        out_s = io.start((state, c_st), (total, c_kt))
        wait(in_c)

        @pl.loop(0, wides)
        def _(b):
            rb = rows_at(b, WIDE)
            act, slope = gelu_parts(dot(o_n2[rb], v_wup[...]))
            o_am[rb, :f] = act.astype(BF)
            if not cfg["branch"]:
                slope = slope * dot_nt(v_g[rb], v_wdown[...])
                o_mix[rb] = dot_nt(v_g[rb], v_wo[...]).astype(BF)
            o_gp[rb] = slope.astype(BF)
            if cfg["branch"]:
                o_part[rb] = (dot(o_am[rb, f:], v_wo[...]) + dot(o_am[rb, :f], v_wdown[...])).astype(BF)
            for copy in outs_c(b):
                copy.start()

        wait(out_h + out_s)

        @pl.loop(0, blocks)
        def _(b):
            wait(outs_a(b) + outs_b(b))

        @pl.loop(0, wides)
        def _(b):
            wait(outs_c(b))


def backward_kernel(cfg, order, *refs):
    base, share, e, f, hc = (cfg[k] for k in ("base", "share", "e", "f", "hc"))
    hd = e // hc
    carried = cfg["carried"]
    refs = list(refs)

    def take(n):
        out = refs[:n]
        del refs[:n]
        return out

    g_in = take(cfg["grads"])
    h_in, wq, wk, wv, wo, wup, wdown, *norms, scales, turn, dct, heads, same, _ = take(17)
    s_qf, s_kf, s_v, s_mf, s_inv, s_st, s_kt = take(7)
    opened = cfg["opened"]
    (in_gup, in_mix) = take(2) if opened else (None, None)
    c_in = take(2 if carried else 0)
    s_gp = take(cfg["alias"])[0] if not opened else None
    s_gup = take(1)[0] if not opened else None
    s_gqkv, keep, send, own, sums, c_st, c_kt = take(7)
    (v_g, v_h, v_wqkv, v_wo, v_wup, v_wdown, v_norms, v_scales, v_turn, v_dct, v_heads, v_same,
     i_gp, i_qf, i_kf, i_v, i_mf, i_inv, i_st, i_kt,
     o_gup, o_gqkv, o_part, o_sums, mixes, acc, acc_s, state, total, sems, o_sems) = refs
    rows, d = v_h.shape
    blocks = rows // BLOCK
    wides = rows // WIDE
    chunks = rows // CHUNK
    count = BLOCK // CHUNK
    me = lax.axis_index("tensor")

    def place(x):
        return x.at[cfg["m"], 0, pl.ds(base, rows)] if len(x.shape) == 4 else x.at[pl.ds(base, rows)]

    def outs_a(b):
        rb, ro = rows_at(b, WIDE), rows_at(b, WIDE, base)
        return [] if opened else looped_out([(o_gup.at[rb], s_gup.at[ro])], o_sems, 0, b)

    def outs_b(b):
        rb, ro = rows_at(b, BLOCK), rows_at(b, BLOCK, base)
        return looped_out([(o_gqkv.at[rb], s_gqkv.at[ro])], o_sems, 1, b)

    def outs_c(b):
        copies = []
        for i in range(BLOCK // share):
            at = (b * (BLOCK // share) + i) ^ me
            copies.append(Routed(o_part.at[rows_at(b * (BLOCK // share) + i, share)], keep, send, at, o_sems.at[2 + i, b]))
        return copies

    @pl.when(lax.axis_index("section") == cfg["section"])
    def _():
        io = Copies(sems)
        some = pl.ds(base, rows)
        some_chunks = pl.ds(base // CHUNK, chunks)
        in_g = [(place(g_in[0]), v_g)] if len(g_in) == 1 else [(g, v_g.at[pl.ds(i * g.shape[0], g.shape[0])]) for i, g in enumerate(g_in)]
        in_a = io.start(*([(in_mix.at[some], mixes)] if opened else
                          in_g + [(wdown.at[0], v_wdown), (wo.at[0], v_wo), (s_gp.at[some], i_gp)]))
        in_b = io.start((s_mf.at[some], i_mf), (s_inv.at[some], i_inv), (s_qf.at[some], i_qf), (s_kf.at[some], i_kf), (s_v.at[some], i_v),
                        (s_st.at[some_chunks], i_st), (s_kt.at[some_chunks], i_kt), (heads, v_heads), (same, v_same),
                        (turn.at[:, some], v_turn), (dct, v_dct))
        if carried:
            in_b += io.start((c_in[0], state), (c_in[1], total))
        else:
            state[...] = jnp.zeros_like(state)
            total[...] = jnp.zeros_like(total)
        in_c = io.start(*(in_g + [(in_gup.at[some], o_gup)] if opened else []))
        in_c += io.start(*[(w.at[0], v_wqkv.at[:, pl.ds(i * e, e)]) for i, w in enumerate((wq, wk, wv))], (wup.at[0], v_wup), (place(h_in), v_h),
                        *[(norm, v_norms.at[i]) for i, norm in enumerate(norms)], (scales.at[0], v_scales))
        acc[...] = jnp.zeros_like(acc)
        acc_s[...] = jnp.zeros_like(acc_s)
        wait(in_a)
        out_s = [] if opened else io.start((v_g.at[rows_at(me, rows // 4)], own))

        def fold(x):
            return jnp.sum(x.reshape(x.shape[0] // 8, 8, x.shape[1]), axis=0)

        @pl.loop(0, 0 if opened else wides)
        def _(b):
            rb = rows_at(b, WIDE)
            g_b = v_g[rb]
            o_gup[rb] = (dot_nt(g_b, v_wdown[...]) * i_gp[rb].astype(F32)).astype(BF)
            mixes[rb] = dot_nt(g_b, v_wo[...]).astype(BF)
            for copy in outs_a(b):
                copy.start()

        wait(in_b)

        @pl.loop(0, blocks)
        def _(step):
            b = blocks - 1 - step
            rb = rows_at(b, BLOCK)
            g_num = (mixes[rb].astype(F32) * i_inv[rb].astype(F32)).astype(BF)
            high, low = split(g_num.astype(F32) * i_mf[rb])
            same_b = v_same[...].astype(BF)
            g_den = -(dot(high, same_b) + dot(low, same_b))
            gd_high, gd_low = split(g_den)
            q_b = i_qf[rb]
            k_b = i_kf[rb]
            value = i_v[rb]
            row = lax.broadcasted_iota(jnp.int32, (CHUNK, hc * CHUNK), 0)
            col = lax.broadcasted_iota(jnp.int32, (CHUNK, hc * CHUNK), 1) & (CHUNK - 1)
            causal = row >= col
            row_t = lax.broadcasted_iota(jnp.int32, (hc * CHUNK, CHUNK), 0) & (CHUNK - 1)
            col_t = lax.broadcasted_iota(jnp.int32, (hc * CHUNK, CHUNK), 1)
            causal_t = col_t >= row_t
            hm = v_heads[...]
            sel = hm * jnp.asarray(1.0 / hd, BF)
            gq_parts, gk_parts, gv_parts = [None] * count, [None] * count, [None] * count
            for c in reversed(range(count)):
                rc = slice(c * CHUNK, (c + 1) * CHUNK)
                at = b * count + c
                q_c, k_c, v_c, n_c, dh, dl = q_b[rc], k_b[rc], value[rc], g_num[rc], gd_high[rc], gd_low[rc]
                k_x = stack_heads(k_c, hm, hc)
                spread = jnp.concatenate([jnp.broadcast_to(g_den[rc, h * hd:h * hd + 1], (CHUNK, CHUNK)) for h in range(hc)], axis=1)
                grid = jnp.where(causal, dot_nt(n_c, stack_heads(v_c, hm, hc)) + spread, 0.0).astype(BF)
                grid_s = jnp.concatenate([grid[:, h * CHUNK:(h + 1) * CHUNK] for h in range(hc)], axis=0)
                scores_t = jnp.where(causal_t, dot_nt(k_x, q_c), 0.0).astype(BF)
                before = jnp.concatenate(split(i_st[at]), axis=1)
                gq_parts[c] = dot(grid, k_x) + dot_nt(jnp.concatenate([n_c, n_c], axis=1), before) + g_den[rc] * i_kt[at][0:1, :]
                after = jnp.concatenate(split(state[...]), axis=1)
                gk_parts[c] = dot_tn(grid_s, stack_heads(q_c, hm, hc)) + dot_nt(jnp.concatenate([v_c, v_c], axis=1), after) + total[0:1, :]
                gv_parts[c] = dot(lanes_of_heads(scores_t, hc), stack_heads(n_c, hm, hc)) + dot(k_c, after[:, :e])
                state[...] += dot_tn(q_c, n_c) * v_same[...]
                total[...] += jnp.sum(q_c.astype(F32) * g_den[rc], axis=0, keepdims=True)
            gc_q = jnp.concatenate(gq_parts, axis=0) * q_b.astype(F32)
            gc_k = jnp.concatenate(gk_parts, axis=0) * k_b.astype(F32)
            g_value = jnp.concatenate(gv_parts, axis=0)
            acc_s[...] += fold(gc_q + gc_k)
            cos_b = jnp.concatenate([jnp.concatenate([v_turn[0, rb]] * (hc // 2), axis=1)] * 2, axis=0)
            sin_b = jnp.concatenate([jnp.concatenate([v_turn[1, rb]] * (hc // 2), axis=1)] * 2, axis=0)
            turned = dot_nt(jnp.concatenate([gc_q, gc_k], axis=0).astype(BF), v_dct[0])
            g_qk = turned * cos_b - partner(turned, hd) * sin_b
            o_gqkv[rb] = jnp.concatenate([g_qk[:BLOCK], g_qk[BLOCK:], g_value], axis=1).astype(BF)
            for copy in outs_b(b):
                copy.start()

        out_s += io.start((state, c_st), (total, c_kt))
        wait(in_c)
        if opened:
            out_s += io.start((v_g.at[rows_at(me, rows // 4)], own))

        @pl.loop(0, blocks)
        def _(b):
            rb = rows_at(b, BLOCK)
            g_one = dot_nt(o_gqkv[rb], v_wqkv[...])
            g_two = dot_nt(o_gup[rb], v_wup[...])
            xhat, rstd = standardize(v_h[rb].astype(F32))
            acc[0] += fold(g_one * xhat)
            acc[1] += fold(g_one)
            acc[2] += fold(g_two * xhat)
            acc[3] += fold(g_two)
            acc[4] += fold(v_g[rb].astype(F32))
            inner = g_one * v_norms[0] + g_two * v_norms[2]
            mean_t = jnp.mean(inner, axis=-1, keepdims=True)
            mean_x = jnp.mean(inner * xhat, axis=-1, keepdims=True)
            o_part[rb] = (rstd * (inner - mean_t - xhat * mean_x)).astype(BF)
            for copy in outs_c(b):
                copy.start()

        for i in range(5):
            o_sums[i:i + 1, :] = jnp.sum(acc[i], axis=0, keepdims=True)
        o_sums[5:8, :] = jnp.zeros((3, d), F32)
        o_sums[5:6, :e] = jnp.sum(acc_s[...], axis=0, keepdims=True) / flat_scales(v_scales, hc)
        out_s += io.start((o_sums, sums))
        wait(out_s)

        @pl.loop(0, 0 if opened else wides)
        def _(b):
            wait(outs_a(b))

        @pl.loop(0, blocks)
        def _(b):
            wait(outs_b(b) + outs_c(b))


def like(shape, dtype):
    return jax.ShapeDtypeStruct(shape, dtype)


def forward_call(sizes, m, section, order, pieces, weights, tabs, store, span=None, carry=(), parts=(), ends=False, cotangent=None):
    rows, d, e, f, hc = sizes
    base, end = span or (0, rows)
    some = end - base
    share = rows // 4 if ends or some == rows else some // 4
    chunks = rows // CHUNK
    own = some // CHUNK
    shapes = [
        like((rows, d), BF), like((rows, d), BF), like((rows, f + e), BF), like((rows, f), BF),
        like((rows, e), BF), like((rows, e), BF), like((rows, e), BF), like((rows, e), F32),
        like((rows, e), BF), like((chunks, e, e), F32), like((chunks, 8, e), F32), like((rows, d), BF),
        like((some // 4, d), BF), like((e, e), F32), like((8, e), F32),
    ] + ([like((2, share, d), BF)] * 2 if section == 0 else [like((rows, e), BF)])
    through = list(store) + list(parts)
    operands = [order, *pieces, *weights, *tabs, *([] if section == 0 else [cotangent]), *carry, *through]
    scratch = [pltpu.VMEM(shape, dtype) for shape, dtype in (
        ((some, d), BF), ((d, 3 * e), BF), ((e, d), BF), ((d, f), BF), ((f, d), BF),
        ((4, 1, d), F32), ((hc, e // hc), F32), ((2, some, 2 * (e // hc)), F32), ((2, e, e), BF), ((hc * CHUNK, e), BF), ((e, e), F32),
        ((some, d), BF), ((some, d), BF), ((some, f + e), BF), ((some, f), BF),
        ((some, e), BF), ((some, e), BF), ((some, e), BF), ((some, e), F32),
        ((some, e), BF), ((own, e, e), F32), ((own, 8, e), F32), ((some, d), BF),
        ((e, e), F32), ((8, e), F32))]
    scratch += [pltpu.VMEM(tabs[-1].shape, jnp.int32), pltpu.VMEM((some, d), BF), pltpu.VMEM((some, e), BF), pltpu.SemaphoreType.DMA((32,)), pltpu.SemaphoreType.DMA((16, some // BLOCK))]
    cfg = {"m": m, "section": section, "pieces": len(pieces), "base": base, "share": share, "origin": base // share if ends else 0,
           "e": e, "f": f, "hc": hc, "carried": bool(carry), "alias": len(through), "branch": section == 0}
    first = len(operands) - len(through)
    results = pl.pallas_call(
        functools.partial(forward_kernel, cfg),
        out_shape=shapes,
        in_specs=[ANY] * len(operands),
        out_specs=[ANY] * len(shapes),
        scratch_shapes=scratch,
        input_output_aliases={first + i: i for i in range(len(through))},
        compiler_params=pltpu.CompilerParams(vmem_limit_bytes=VMEM_BYTES),
        cost_estimate=pl.CostEstimate(flops=2 * some * d * (4 * e + 2 * f), bytes_accessed=25 * 2 ** 20, transcendentals=some * (f + 2 * e)),
        name="forward",
    )(*operands)
    return list(results[:12]), results[12], list(results[15:])


def backward_call(sizes, m, section, order, g_in, h_in, weights, tabs, store, back, span=None, carry=(), opened=()):
    rows, d, e, f, hc = sizes
    base, end = span or (0, rows)
    some = end - base
    share = some // 4
    own = some // CHUNK
    shapes = [like((rows, f), BF)] * (not opened) + [like((rows, 3 * e), BF), like((2, share, d), BF), like((2, share, d), BF), like((some // 4, d), BF), like((8, d), F32), like((e, e), F32), like((8, e), F32)]
    operands = [order, *g_in, h_in, *weights, *tabs, *store[4:11], *opened, *carry, *back]
    scratch = [pltpu.VMEM(shape, dtype) for shape, dtype in (
        ((some, d), BF), ((some, d), BF), ((d, 3 * e), BF), ((e, d), BF), ((d, f), BF), ((f, d), BF),
        ((4, 1, d), F32), ((hc, e // hc), F32), ((2, some, 2 * (e // hc)), F32), ((2, e, e), BF), ((hc * CHUNK, e), BF), ((e, e), F32),
        ((some, f), BF), ((some, e), BF), ((some, e), BF), ((some, e), BF),
        ((some, e), F32), ((some, e), BF), ((own, e, e), F32), ((own, 8, e), F32),
        ((some, f), BF), ((some, 3 * e), BF), ((some, d), BF), ((8, d), F32),
        ((some, e), BF), ((5, 8, d), F32), ((8, e), F32), ((e, e), F32), ((8, e), F32))]
    scratch += [pltpu.SemaphoreType.DMA((40,)), pltpu.SemaphoreType.DMA((4, some // BLOCK))]
    cfg = {"m": m, "section": section, "base": base, "share": share, "e": e, "f": f, "hc": hc, "carried": bool(carry), "alias": len(back), "grads": len(g_in), "opened": bool(opened)}
    first = len(operands) - len(back)
    results = pl.pallas_call(
        functools.partial(backward_kernel, cfg),
        out_shape=shapes,
        in_specs=[ANY] * len(operands),
        out_specs=[ANY] * len(shapes),
        scratch_shapes=scratch,
        input_output_aliases={first + i: i for i in range(len(back))},
        compiler_params=pltpu.CompilerParams(vmem_limit_bytes=VMEM_BYTES),
        cost_estimate=pl.CostEstimate(flops=2 * some * d * (4 * e + 2 * f), bytes_accessed=30 * 2 ** 20, transcendentals=0),
        name="backward",
    )(*operands)
    head = 1 if opened else 2
    return list(results[:head]), list(results[head:head + 3]), results[head + 3], list(results[head + 4:])


def down_kernel(cfg, order, *refs):
    count, first, m = cfg["pieces"], cfg["first"], cfg["m"]
    refs = list(refs)

    def take(n):
        out = refs[:n]
        del refs[:n]
        return out

    pieces = take(count)
    (am,) = take(1)
    acc_in = take(0 if first else 1)
    take(cfg["alias"])
    outs = take(2 if count == 4 else 1)
    v_g, v_am, v_acc, v_out, sems, o_sems = refs
    rows, d = v_g.shape
    me = lax.axis_index("tensor")

    def tile(b):
        return rows_at(b, BLOCK)

    def sent(b):
        return pltpu.make_async_copy((v_acc if first else v_out).at[tile(b)], outs[0].at[tile(b)], o_sems.at[b])

    @pl.when(lax.axis_index("section") == cfg["section"])
    def _():
        io = Copies(sems)
        if count == 4:
            loads = io.start(*[(pieces[k], v_g.at[rows_at(me ^ k, rows // 4)]) for k in range(4)])
        else:
            loads = io.start((pieces[0].at[m, 0] if len(pieces[0].shape) == 4 else pieces[0], v_g))
        loads += io.start((am, v_am))
        if not first:
            loads += io.start((acc_in[0], v_acc))
        wait(loads)
        kept = io.start((v_g, outs[1])) if count == 4 else []

        @pl.loop(0, d // BLOCK)
        def _(b):
            product = dot_tn(v_g[:, tile(b)], v_am[...])
            if first:
                v_acc[tile(b)] = product.astype(BF)
            else:
                v_out[tile(b)] = (v_acc[tile(b)].astype(F32) + product).astype(BF)
            sent(b).start()

        wait(kept)

        @pl.loop(0, d // BLOCK)
        def _(b):
            sent(b).wait()


def branch_kernel(order, am, wo, wdown, keep, send, v_am, v_wo, v_wdown, o_part, sems, o_sems):
    rows, d = o_part.shape
    f = v_wdown.shape[0]
    share = rows // 4
    me = lax.axis_index("tensor")

    def outs(b):
        copies = []
        for i in range(WIDE // share):
            at = (b * (WIDE // share) + i) ^ me
            copies.append(Routed(o_part.at[rows_at(b * (WIDE // share) + i, share)], keep, send, at, o_sems.at[i, b]))
        return copies

    @pl.when(lax.axis_index("section") == 1)
    def _():
        wait(Copies(sems).start((am, v_am), (wo.at[0], v_wo), (wdown.at[0], v_wdown)))

        @pl.loop(0, rows // WIDE)
        def _(b):
            rb = rows_at(b, WIDE)
            o_part[rb] = (dot(v_am[rb, f:], v_wo[...]) + dot(v_am[rb, :f], v_wdown[...])).astype(BF)
            for copy in outs(b):
                copy.start()

        @pl.loop(0, rows // WIDE)
        def _(b):
            wait(outs(b))


def branch_call(order, am, w_out, w_down):
    rows, wide = am.shape
    _, f, d = w_down.shape
    return pl.pallas_call(
        branch_kernel,
        out_shape=[like((2, rows // 4, d), BF)] * 2,
        in_specs=[ANY] * 4,
        out_specs=[ANY] * 2,
        scratch_shapes=[pltpu.VMEM((rows, wide), BF), pltpu.VMEM((wide - f, d), BF), pltpu.VMEM((f, d), BF), pltpu.VMEM((rows, d), BF),
                        pltpu.SemaphoreType.DMA((3,)), pltpu.SemaphoreType.DMA((2, rows // WIDE))],
        compiler_params=pltpu.CompilerParams(vmem_limit_bytes=VMEM_BYTES),
        cost_estimate=pl.CostEstimate(flops=0, bytes_accessed=0, transcendentals=0),
        name="branch",
    )(order, am, w_out, w_down)


def arrange_kernel(order, *refs):
    pieces, (out, held, sems) = refs[:4], refs[4:]
    me = lax.axis_index("tensor")

    @pl.when(lax.axis_index("section") == 0)
    def _():
        io = Copies(sems)
        wait(io.start(*[(pieces[k], held.at[rows_at(me ^ k, pieces[k].shape[0])]) for k in range(4)]))
        wait(io.start((held, out)))


def arrange_call(order, pieces):
    share, d = pieces[0].shape
    return pl.pallas_call(
        arrange_kernel,
        out_shape=[like((4 * share, d), BF)],
        in_specs=[ANY] * 5,
        out_specs=[ANY],
        scratch_shapes=[pltpu.VMEM((4 * share, d), BF), pltpu.SemaphoreType.DMA((5,))],
        cost_estimate=pl.CostEstimate(flops=0, bytes_accessed=0, transcendentals=0),
        name="arrange",
    )(order, *pieces)


def unpack_kernel(packed, *outs):
    at = 0
    for out in outs:
        out[0] = packed[:, at:at + out.shape[2]].astype(F32)
        at += out.shape[2]


def unpack_call(packed, widths):
    rows = packed.shape[0]
    whole = pl.BlockSpec(memory_space=pltpu.VMEM)
    return pl.pallas_call(
        unpack_kernel,
        out_shape=[like((1, rows, width), F32) for width in widths],
        in_specs=[whole],
        out_specs=[whole] * len(widths),
        name="unpack",
    )(packed)


def down_call(m, section, order, pieces, am, acc=None, through=None):
    rows, wide = am.shape
    d = pieces[0].shape[-1]
    first = acc is None
    operands = [order, *pieces, am] + ([] if first else [acc]) + ([] if through is None else [through])
    cfg = {"pieces": len(pieces), "first": first, "section": section, "m": m, "alias": int(through is not None)}
    shapes = [like((d, wide), BF)] + [like((rows, d), BF)] * (len(pieces) == 4)
    return pl.pallas_call(
        functools.partial(down_kernel, cfg),
        out_shape=shapes,
        in_specs=[ANY] * len(operands),
        out_specs=[ANY] * len(shapes),
        scratch_shapes=[pltpu.VMEM((rows, d), BF), pltpu.VMEM((rows, wide), BF), pltpu.VMEM((d, wide), BF), pltpu.VMEM((d, wide), BF),
                        pltpu.SemaphoreType.DMA((len(pieces) + 5,)), pltpu.SemaphoreType.DMA((d // BLOCK,))],
        input_output_aliases={} if through is None else {len(operands) - 1: 0},
        compiler_params=pltpu.CompilerParams(vmem_limit_bytes=VMEM_BYTES),
        cost_estimate=pl.CostEstimate(flops=0 if first else 2 * rows * d * wide, bytes_accessed=0 if first else 12 * 2 ** 20, transcendentals=0),
        name="down",
    )(*operands)


def body(tokens, cotangent, lengths, attn_gain, attn_bias, ffn_gain, ffn_bias, w_query, w_key, w_value, w_out, feat_scale, w_up, w_down, down_bias):
    section = lax.axis_index("section")
    tensor = lax.axis_index("tensor")
    teams = lax.axis_size("tensor")
    micro, _, rows, d = tokens.shape
    hc, hd = feat_scale.shape[1:]
    e = hc * hd
    f = w_up.shape[2]
    sizes = (rows, d, e, f, hc)
    whole, early, late = (0, rows), (0, rows // 2), (rows // 2, rows)
    made = host_tables(rows, hc, hd)
    tabs = [attn_gain, attn_bias, ffn_gain, ffn_bias, feat_scale] + [jnp.asarray(made[k]) for k in ("turn", "dct", "heads", "same")] + [lengths]
    weights = [w_query, w_key, w_value, w_out, w_up, w_down]
    both = ("section", "tensor")
    order = attn_gain

    def swap(x, sec, bit):
        sections = range(2) if sec is None else (sec,)
        return lax.ppermute(x, both, [(k * teams + i, k * teams + (i ^ bit)) for k in sections for i in range(teams)])

    def hand(x, source):
        return lax.ppermute(x, "section", [(source, 1 - source)])

    def gather_rows(own, sec):
        far = swap(own, sec, 2)
        return [own, swap(own, sec, 1), far, swap(far, sec, 1)]

    def tie(x, *after):
        return lax.optimization_barrier((x, *after))[0]

    def tie_all(*values):
        return lax.optimization_barrier(values)

    def near_sum(parts, sec):
        keep, send = parts
        got = swap(send, sec, 1)
        return keep[0].astype(F32) + got[0].astype(F32), (keep[1].astype(F32) + got[1].astype(F32)).astype(BF)

    def relay(parts, source):
        near, sent = near_sum(parts, source)
        near = (near + down_bias[0] if source == 0 else near).astype(BF)
        pairs = [[(source * teams + i, (1 - source) * teams + (i ^ bit)) for i in range(teams)] for bit in (0, 2)]
        return [lax.ppermute(near, both, pairs[0]), lax.ppermute(sent, both, pairs[1])], (near, sent)

    def own_rows(x):
        return lax.dynamic_index_in_dim(x.reshape(teams, rows // teams, d), tensor, 0, keepdims=False)

    def whole_rows(own):
        return lax.all_gather(own, "tensor", axis=0, tiled=True)

    def summed(start, took):
        return start.astype(F32) + took[0].astype(F32) + took[1].astype(F32)

    def all_sum(x, axis):
        size, bit = lax.axis_size(axis), 1
        if size & (size - 1):
            return lax.psum(x, axis)
        while bit < size:
            x = x + lax.ppermute(x, axis, [(i, i ^ bit) for i in range(size)])
            bit *= 2
        return x

    def weight_grad(pairs):
        return sum(dot_tn(left, right) for left, right in pairs)

    def scatter(total):
        return lax.psum_scatter(total, "dp", scatter_dimension=0, tiled=True)

    def forward(m, sec, after, pieces, store, **more):
        return forward_call(sizes, m, sec, tie(order, after), pieces, weights, tabs, store, **more)

    def backward(m, sec, after, g_in, h_in, store, back, **more):
        return backward_call(sizes, m, sec, tie(order, after), g_in, h_in, weights, tabs, store, back, **more)

    store_0, _, parts = forward_call(sizes, 0, 0, order, [tokens], weights, tabs, [])
    took, after = relay(parts, 0)
    store_1, _, parts = forward_call(sizes, 1, 0, tie(order, *after), [tokens], weights, tabs, [])
    own_t, *took, parts[0], parts[1] = tie_all(own_rows(tokens[0, 0]), *took, *parts)
    row_0 = summed(own_t, took).astype(BF)
    far_rows = swap(row_0, 1, 2)
    took, after = relay(parts, 0)
    near_rows = swap(tie(row_0, *after), 1, 1)
    far_rows, near_rows = tie_all(far_rows, near_rows)
    store_0, own_0, mix_0 = forward_call(sizes, 0, 1, tie(order, *after, took[0]), [row_0, near_rows, far_rows, swap(far_rows, 1, 1)], weights, tabs, store_0, cotangent=cotangent)
    own_c = [own_rows(cotangent[m, 0]) for m in range(2)]
    *took, own_0, own_t, own_c[0], own_c[1] = tie_all(*took, own_0, own_rows(tokens[1, 0]), *own_c)
    row_1 = summed(own_t, took).astype(BF)
    rows_1 = whole_rows(row_1)
    back_0, parts, sums_0, _ = backward(0, 1, row_1, [cotangent], store_0[11], store_0, [], opened=[store_0[3], *mix_0])
    took_0, after = relay(parts[:2], 1)
    rows_1 = tie(rows_1, *after)
    store_1, own_1, mix_1 = forward_call(sizes, 1, 1, tie(order, *after), [rows_1], weights, tabs, store_1, cotangent=cotangent)
    *took_0, own_1 = tie_all(*took_0, own_1)
    grad_0 = summed(own_c[0], took_0).astype(BF)
    gb_0 = whole_rows(grad_0)
    back_1, parts, sums_1, _ = backward(1, 1, grad_0, [cotangent], store_1[11], store_1, [], opened=[store_1[3], *mix_1])
    took_1, after = relay(parts[:2], 1)
    gb_0, after = tie_all(gb_0, tie(order, *after))
    ends_0 = [*branch_call(after, store_0[2], w_out, w_down), own_0]
    ends_1 = [*branch_call(after, store_1[2], w_out, w_down), own_1]
    back_0, ends_0, sums_0, _ = backward(0, 0, gb_0, [gb_0], tokens, store_0, [store_0[3], *back_0, *ends_0, sums_0])
    *took_1, ends_0[0] = tie_all(*took_1, ends_0[0])
    grad_1 = summed(own_c[1], took_1).astype(BF)
    far_rows = swap(grad_1, 0, 2)
    near_rows = swap(grad_1, 0, 1)
    (acc,) = down_call(0, 0, tie(order, near_rows), [gb_0], store_0[2])
    (acc_b,) = down_call(0, 1, tie(order, acc), [cotangent], store_0[2])
    (down_sum,) = down_call(1, 1, order, [cotangent], store_1[2], acc_b)
    far_rows, near_rows, down_sum = tie_all(far_rows, near_rows, down_sum)
    down_sum, gb_1 = down_call(1, 0, order, [grad_1, near_rows, far_rows, swap(far_rows, 0, 1)], store_1[2], acc, down_sum)
    down = scatter(down_sum)
    back_1, ends_1, sums_1, _ = backward(1, 0, down_sum, [gb_1], tokens, store_1, [store_1[3], *back_1, *ends_1, sums_1])
    rest_sum = jnp.concatenate([
        weight_grad([(store_0[1], back_0[0]), (store_1[1], back_1[0])]).astype(BF),
        weight_grad([(store_0[0], back_0[1]), (store_1[0], back_1[1])]).astype(BF)], axis=1)
    down, rest_sum = tie_all(down, rest_sum)
    rest = scatter(rest_sum)
    up, query, key, value = unpack_call(rest, (f, e, e, e))
    shift = jnp.where(section == 0, 0.0, down_bias[0])
    ends = []
    for parts in (ends_0, ends_1):
        keep, send, own, _ = tie_all(*parts, rest_sum)
        near, sent = near_sum((keep, send), None)
        ends.append(own.astype(F32) + near + swap(sent, None, 2).astype(F32) + shift)
    ends = jnp.stack(ends)[None, :, None]
    down = down.astype(F32).T
    small = all_sum(sums_0 + sums_1, "dp")
    group = lax.axis_size("dp")
    place = lax.axis_index("dp")
    cut = all_sum(lax.dynamic_slice(small, (0, place * (d // group)), (5, d // group)), "tensor")
    scale_cut = lax.dynamic_slice(small[5, :e].reshape(hc, hd), (0, place * (hd // group)), (hc, hd // group))
    return (
        ends, cut[0:1], cut[1:2], cut[2:3], cut[3:4],
        query, key, value, down[None, f:], scale_cut[None], up, down[None, :f],
        cut[4:5] / teams,
    )


def solution(mesh):
    return jax.shard_map(
        body,
        mesh=mesh,
        in_specs=(
            P(None, "dp", None, None), P(None, "dp", None, None), P(None, "dp"),
            P("section", None), P("section", None), P("section", None), P("section", None),
            P("section", None, "tensor"), P("section", None, "tensor"), P("section", None, "tensor"),
            P("section", "tensor", None), P("section", "tensor", None), P("section", None, "tensor"),
            P("section", "tensor", None), P("section", None),
        ),
        out_specs=(
            P("section", None, "dp", "tensor", None),
            P("section", "dp"), P("section", "dp"), P("section", "dp"), P("section", "dp"),
            P("section", "dp", "tensor"), P("section", "dp", "tensor"), P("section", "dp", "tensor"),
            P("section", "tensor", "dp"), P("section", "tensor", "dp"), P("section", "dp", "tensor"),
            P("section", "tensor", "dp"), P("section", "dp"),
        ),
        check_vma=False,
    )
```
